128 devices in a mesh: ctx: 16 (over z, y_lo, core), fsdp: 8 (over x, y_hi).
Axes of the slice: x: 4, y: 4 (y_hi: 2, y_lo: 2; y = y_hi * 2 + y_lo), z: 4, core: 2. Of those that a mesh axis runs over, the one named last changes fastest.
Arguments:
- tokens: bfloat16 [8, 2, 16, 64, 2048], P('fsdp', None, 'ctx'), may hold values from -6 to 6
- gain_in: float32 [2048], replicated, may hold values from 0.5 to 1.5
- query_weight: bfloat16 [2048, 2048], P('fsdp'), may hold values from -0.125 to 0.125
- key_weight: bfloat16 [2048, 1024], P('fsdp'), may hold values from -0.125 to 0.125
- value_weight: bfloat16 [2048, 1024], P('fsdp'), may hold values from -0.125 to 0.125
- gain_query: float32 [128], replicated, may hold values from 0.5 to 1.5
- gain_key: float32 [128], replicated, may hold values from 0.5 to 1.5
- out_weight: bfloat16 [2048, 2048], P('fsdp'), may hold values from -4 to 4
- gain_mid: float32 [2048], replicated, may hold values from 0.5 to 1.5
- gate_weight: bfloat16 [2048, 6144], P('fsdp'), may hold values from -0.125 to 0.125
- up_weight: bfloat16 [2048, 6144], P('fsdp'), may hold values from -0.125 to 0.125
- down_weight: bfloat16 [6144, 2048], P('fsdp'), may hold values from -0.078125 to 0.078125
- cotangent: bfloat16 [8, 2, 16, 64, 2048], P('fsdp', None, 'ctx'), may hold values from -6 to 6
Outputs:
- mixed: bfloat16 [8, 2, 16, 64, 2048], P('fsdp', None, 'ctx')
- tokens_grad: bfloat16 [8, 2, 16, 64, 2048], P('fsdp', None, 'ctx')
- grad_gain_in: float32 [2048], replicated
- grad_query: float32 [2048, 2048], P(('ctx', 'fsdp'))
- grad_key: float32 [2048, 1024], P(('ctx', 'fsdp'))
- grad_value: float32 [2048, 1024], P(('ctx', 'fsdp'))
- grad_gain_query: float32 [128], replicated
- grad_gain_key: float32 [128], replicated
- grad_out: float32 [2048, 2048], P(('ctx', 'fsdp'))
- grad_gain_mid: float32 [2048], replicated
- grad_gate: float32 [2048, 6144], P(('ctx', 'fsdp'))
- grad_up: float32 [2048, 6144], P(('ctx', 'fsdp'))
- grad_down: float32 [6144, 2048], P(('ctx', 'fsdp'))
The draws below stay inside these ranges and needn't reach their ends.
All inputs are finite; a program needn't handle non-finite values.
Results may differ from the reference program's by a relative error of at most 0.02.
Values may be sent and summed in bfloat16 or wider, within the bound.
A program may use at most 576 MiB of HBM per device.

```python
import jax
import jax.numpy as jnp
from jax import lax

D = 2048
NH = 16
KVH = 8
HD = 128
FF = 6144
HALF = 64
LEN = 2048
SEQS = 8
QW = 2048
KVW = 1024
N_CTX = 16


def steps_of(rng, dims, split, low, top_value):
    factor_of, own = 1.0, jax.random.fold_in(rng, 6)
    for axis_at, blocks in split:
        heights = jnp.exp(jax.random.uniform(jax.random.fold_in(own, axis_at), (blocks,), jnp.float32, low / len(split), top_value / len(split)))
        factor_of = factor_of * jnp.repeat(heights, dims[axis_at] // blocks).reshape([-1 if axis == axis_at else 1 for axis in range(len(dims))])
    return factor_of


def bell_draw(stream_key, extent, scale, most, pieces=(), kind=jnp.bfloat16):
    entries = scale * jax.random.normal(stream_key, extent, jnp.float32)
    if pieces:
        entries = entries * steps_of(stream_key, extent, pieces, -0.22, 0.18)
    return jnp.clip(entries, -most, most).astype(kind)


def setup_inputs(seed: int = 0) -> dict:
    arg_keys = jax.random.split(jax.random.key(seed), 14)
    tokens = bell_draw(arg_keys[0], (SEQS, 2, N_CTX, HALF, D), 1.0, 6.0, ((0, 8), (2, 16)))
    gain_in = jnp.clip(1.0 + 0.1 * jax.random.normal(arg_keys[1], (D,), jnp.float32), 0.5, 1.5)
    query_weight = bell_draw(arg_keys[2], (D, QW), D ** -0.5, 0.125, ((0, 8),))
    key_weight = bell_draw(arg_keys[3], (D, KVW), D ** -0.5, 0.125, ((0, 8),))
    value_weight = bell_draw(arg_keys[4], (D, KVW), D ** -0.5, 0.125, ((0, 8),))
    gain_query = jnp.clip(1.0 + 0.1 * jax.random.normal(arg_keys[5], (HD,), jnp.float32), 0.5, 1.5)
    gain_key = jnp.clip(1.0 + 0.1 * jax.random.normal(arg_keys[6], (HD,), jnp.float32), 0.5, 1.5)
    out_weight = bell_draw(arg_keys[7], (QW, D), (max(1, 2 * QW // LEN)) ** -0.5, 4.0, ((0, 8),))
    gain_mid = jnp.clip(1.0 + 0.1 * jax.random.normal(arg_keys[8], (D,), jnp.float32), 0.5, 1.5)
    gate_weight = bell_draw(arg_keys[9], (D, FF), D ** -0.5, 0.125, ((0, 8),))
    up_weight = bell_draw(arg_keys[10], (D, FF), D ** -0.5, 0.125, ((0, 8),))
    down_weight = bell_draw(arg_keys[11], (FF, D), FF ** -0.5, 0.078125, ((0, 8),))
    cotangent = bell_draw(arg_keys[12], (SEQS, 2, N_CTX, HALF, D), 1.0, 6.0, ((0, 8), (2, 16)))
    return {"tokens": tokens, "gain_in": gain_in, "query_weight": query_weight, "key_weight": key_weight, "value_weight": value_weight, "gain_query": gain_query, "gain_key": gain_key, "out_weight": out_weight, "gain_mid": gain_mid, "gate_weight": gate_weight, "up_weight": up_weight, "down_weight": down_weight, "cotangent": cotangent}


EPS = 1e-06
THETA = 1000000.0

@jax.custom_vjp
def low(v):
    return lax.optimization_barrier(v.astype(jnp.bfloat16)).astype(jnp.float32)

@jax.custom_vjp
def low_back(v):
    return v

def low_keep(v):
    return (low(v), None)

def low_pass(kept, grad):
    return (grad,)

def back_keep(v):
    return (v, None)

def back_low(kept, grad):
    return (low(grad),)
low.defvjp(low_keep, low_pass)
low_back.defvjp(back_keep, back_low)

def mat(left, right):
    return jnp.dot(left, right, precision=lax.Precision.HIGHEST, preferred_element_type=jnp.float32)

def scale_of(vals):
    return lax.rsqrt(lax.optimization_barrier(jnp.mean(vals * vals, -1, keepdims=True)) + EPS)

def rotary(positions, width):
    half = width // 2
    freq = THETA ** (-2.0 * jnp.arange(half, dtype=jnp.float32) / width)
    angle = positions.astype(jnp.float32)[:, None] * freq[None, :]
    cosine = jnp.concatenate([jnp.cos(angle), jnp.cos(angle)], 1)[:, None, :]
    sine = jnp.concatenate([jnp.sin(angle), jnp.sin(angle)], 1)[:, None, :]
    return (cosine, sine)

def turn(vals, cosine, sine):
    half = vals.shape[-1] // 2
    return vals * cosine + jnp.concatenate([-vals[..., half:], vals[..., :half]], -1) * sine

def forward(x, gain_in, query_weight, key_weight, value_weight, gain_query, gain_key, out_weight, gain_mid, gate_weight, up_weight, down_weight):
    length = x.shape[0]
    group = NH // KVH
    positions = jnp.arange(length, dtype=jnp.int32)
    cosine, sine = rotary(positions, HD)
    h = low(x * scale_of(x) * gain_in)
    qraw = low_back(mat(h, query_weight)).reshape(length, NH, HD)
    kraw = low_back(mat(h, key_weight)).reshape(length, KVH, HD)
    values = low_back(low(mat(h, value_weight))).reshape(length, KVH, HD)
    query = low_back(low(turn(qraw * scale_of(qraw) * gain_query, cosine, sine)))
    keys = low_back(low(turn(kraw * scale_of(kraw) * gain_key, cosine, sine)))
    qg = query.reshape(length, KVH, group, HD)
    scores = jnp.einsum('tgjd,sgd->gjts', qg, keys, precision=lax.Precision.HIGHEST) * HD ** (-0.5)
    scores = low_back(scores)
    allowed = positions[None, :] <= positions[:, None]
    scores = jnp.where(allowed, scores, -1e+30)
    top = lax.optimization_barrier(jnp.max(scores, -1, keepdims=True))
    expo = jnp.exp(scores - top)
    probs = expo / lax.optimization_barrier(jnp.sum(expo, -1, keepdims=True))
    attended = jnp.einsum('gjts,sgd->tgjd', low(probs), values, precision=lax.Precision.HIGHEST)
    attended = low_back(low(attended.reshape(length, NH * HD)))
    y_mid = x + low_back(mat(attended, out_weight))
    h_mid = low(y_mid * scale_of(y_mid) * gain_mid)
    gate = low_back(mat(h_mid, gate_weight))
    upper = low_back(mat(h_mid, up_weight))
    act = low(jax.nn.silu(gate) * upper)
    return y_mid + mat(act, down_weight)

def natural(arr):
    early = arr[:, 0]
    late = jnp.flip(arr[:, 1], axis=1)
    return jnp.concatenate([early, late], 1).reshape(arr.shape[0], LEN, D)

def layout(arr):
    blocks = arr.reshape(arr.shape[0], 2 * N_CTX, HALF, D)
    return jnp.stack([blocks[:, :N_CTX], jnp.flip(blocks[:, N_CTX:], axis=1)], 1)

def reference(tokens, gain_in, query_weight, key_weight, value_weight, gain_query, gain_key, out_weight, gain_mid, gate_weight, up_weight, down_weight, cotangent):
    params = tuple((p.astype(jnp.float32) for p in (gain_in, query_weight, key_weight, value_weight, gain_query, gain_key, out_weight, gain_mid, gate_weight, up_weight, down_weight)))
    inputs = natural(tokens.astype(jnp.float32))
    grads_in = natural(cotangent.astype(jnp.float32))

    def step(totals, pair):
        x_seq, g_seq = pair
        result, pull = jax.vjp(forward, x_seq, *params)
        grads = pull(g_seq)
        return (tuple((a + b for a, b in zip(totals, grads[1:]))), (result, grads[0]))
    start = tuple((jnp.zeros_like(p) for p in params))
    totals, (results, dxs) = lax.scan(step, start, (inputs, grads_in))
    mixed = layout(results).astype(jnp.bfloat16)
    tokens_grad = layout(dxs).astype(jnp.bfloat16)
    return (mixed, tokens_grad, totals[0], totals[1], totals[2], totals[3], totals[4], totals[5], totals[6], totals[7], totals[8], totals[9], totals[10])
```

```python
import jax
import jax.numpy as jnp
from jax import lax
from jax.sharding import Mesh, PartitionSpec as P

EPS = 1e-06
THETA = 1000000.0
BF = jnp.bfloat16
F32 = jnp.float32
TP = ("z", "core")
FS = ("x", "yh")
DP = ("yl", "x", "yh")
ALL = ("z", "yl", "core", "x", "yh")


def rotary(positions, width):
    half = width // 2
    freq = THETA ** (-2.0 * jnp.arange(half, dtype=F32) / width)
    angle = positions.astype(F32)[:, None] * freq[None, :]
    cosine = jnp.concatenate([jnp.cos(angle), jnp.cos(angle)], 1)[:, None, :]
    sine = jnp.concatenate([jnp.sin(angle), jnp.sin(angle)], 1)[:, None, :]
    return (cosine, sine)


def turn(vals, cosine, sine):
    half = vals.shape[-1] // 2
    return vals * cosine + jnp.concatenate([-vals[..., half:], vals[..., :half]], -1) * sine


def turn_back(grads, cosine, sine):
    half = grads.shape[-1] // 2
    moved = grads * sine
    return grads * cosine + jnp.concatenate([moved[..., half:], -moved[..., :half]], -1)


def row_norm(vals):
    scale = lax.rsqrt(jnp.mean(vals * vals, -1, keepdims=True) + EPS)
    return (vals * scale, scale)


def norm_back(grad_unit, unit, scale):
    return scale * (grad_unit - unit * jnp.mean(grad_unit * unit, -1, keepdims=True))


def mm(left, right):
    return jnp.dot(left, right, preferred_element_type=F32)


def mm_t(left, right):
    return lax.dot_general(left, right, (((1,), (1,)), ((), ())), preferred_element_type=F32)


def t_mm(left, right):
    return lax.dot_general(left, right, (((0,), (0,)), ((), ())), preferred_element_type=F32)


def gather(val, axes):
    return lax.all_gather(val, axes, axis=0, tiled=True)


def scatter(val, axes):
    return lax.psum_scatter(val, axes, scatter_dimension=0, tiled=True)


def shards(
    tokens,
    gain_in,
    query_weight,
    key_weight,
    value_weight,
    gain_query,
    gain_key,
    out_weight,
    gain_mid,
    gate_weight,
    up_weight,
    down_weight,
    cotangent,
):
    half = tokens.shape[3]
    width = tokens.shape[4]
    n_z, n_yl, n_core = (lax.axis_size(a) for a in ("z", "yl", "core"))
    n_tp = n_z * n_core
    n_fs = lax.axis_size("x") * lax.axis_size("yh")
    n_ctx = n_tp * n_yl
    rows = 2 * half
    head = gain_query.shape[0]
    kv_width = key_weight.shape[1]
    q_width = query_weight.shape[1]
    hidden = gate_weight.shape[1]
    factor = head ** (-0.5)
    qc, kc, fc = q_width // n_tp, kv_width // n_tp, hidden // n_tp
    group = qc // head
    t = lax.axis_index(TP)
    yl = lax.axis_index("yl")

    def positions(lane):
        idx = jnp.arange(n_tp * rows, dtype=jnp.int32)
        who, spot = idx // rows, idx % rows
        c = (who // n_core) * (n_yl * n_core) + lane * n_core + who % n_core
        block = jnp.where(spot // half == 0, c, 2 * n_ctx - 1 - c)
        return block * half + spot % half

    query_pos = positions(yl)
    key_pos = jnp.concatenate([positions(i) for i in range(n_yl)])
    allowed = key_pos[None, :] <= query_pos[:, None]
    cosine, sine = rotary(query_pos, head)

    cut = lambda w, n: lax.dynamic_slice_in_dim(w, t * n, n, 1)
    w_qkv = gather(
        jnp.concatenate([cut(query_weight, qc), cut(key_weight, kc), cut(value_weight, kc)], 1), FS
    )
    w_gu = gather(jnp.concatenate([cut(gate_weight, fc), cut(up_weight, fc)], 1), FS)
    o_s, d_s = out_weight.shape[0] // n_tp, down_weight.shape[0] // n_tp
    rows_od = jnp.concatenate(
        [
            lax.dynamic_slice_in_dim(out_weight, t * o_s, o_s, 0),
            lax.dynamic_slice_in_dim(down_weight, t * d_s, d_s, 0),
        ],
        0,
    )
    rows_od = lax.ppermute(
        rows_od,
        TP + FS,
        [(a * n_fs + b, b * n_fs + a) for a in range(n_tp) for b in range(n_fs)],
    )
    w_od = gather(rows_od[None], FS)
    w_out = w_od[:, :o_s].reshape(n_fs * o_s, width)
    w_down = w_od[:, o_s:].reshape(n_fs * d_s, width)

    x = tokens.reshape(rows, width).astype(F32)
    unit_in, scale_in = row_norm(x)
    h = gather((unit_in * gain_in).astype(BF), TP)
    grad_l = cotangent.reshape(rows, width)
    g = gather(grad_l, TP)
    qkv = mm(h, w_qkv)
    value_b = qkv[:, qc + kc :].astype(BF)
    unit_q, scale_q = row_norm(qkv[:, :qc].reshape(-1, group, head))
    unit_k, scale_k = row_norm(qkv[:, qc : qc + kc].reshape(-1, 1, head))
    query_b = turn(unit_q * gain_query, cosine, sine).astype(BF)
    keys_b = turn(unit_k * gain_key, cosine, sine).astype(BF).reshape(-1, head)
    kv = gather(jnp.concatenate([keys_b, value_b], 1), ("yl",))
    keys, values = kv[:, :head], kv[:, head:]

    raw = jnp.einsum("tjd,sd->jts", query_b, keys, preferred_element_type=F32) * factor
    scores = jnp.where(allowed, raw, -1e30)
    top = jnp.max(scores, -1, keepdims=True)
    expo = jnp.exp(scores - top)
    probs = expo / jnp.sum(expo, -1, keepdims=True)
    probs_b = probs.astype(BF)
    attended = jnp.einsum("jts,sd->tjd", probs_b, values, preferred_element_type=F32)
    attended = attended.reshape(-1, qc).astype(BF)
    y_mid = x + scatter(mm(attended, w_out).astype(BF), TP).astype(F32)
    unit_mid, scale_mid = row_norm(y_mid)
    h2 = gather((unit_mid * gain_mid).astype(BF), TP)
    gu = mm(h2, w_gu)
    gate, upper = gu[:, :fc], gu[:, fc:]
    sig = jax.nn.sigmoid(gate)
    silu_gate = gate * sig
    act_b = (silu_gate * upper).astype(BF)
    mixed = (y_mid + scatter(mm(act_b, w_down).astype(BF), TP).astype(F32)).astype(BF)
    grad_act = mm_t(g, w_down)
    dgate_b = (grad_act * upper * sig * (1.0 + gate * (1.0 - sig))).astype(BF)
    dup_b = (grad_act * silu_gate).astype(BF)
    dgu = jnp.concatenate([dgate_b, dup_b], 1)
    grad_h2 = scatter(mm_t(dgu, w_gu).astype(BF), TP).astype(F32)
    term_mid = jnp.sum(grad_h2 * unit_mid, 0)
    grad_mid = grad_l.astype(F32) + norm_back(grad_h2 * gain_mid, unit_mid, scale_mid)
    dz = gather(grad_mid.astype(BF), TP)
    do_b = mm_t(dz, w_out).astype(BF).reshape(-1, group, head)
    grad_probs = jnp.einsum("tjd,sd->jts", do_b, values, preferred_element_type=F32)
    delta = jnp.sum(probs * grad_probs, -1, keepdims=True)
    ds_b = (probs * (grad_probs - delta)).astype(BF)
    grad_query = jnp.einsum("jts,sd->tjd", ds_b, keys, preferred_element_type=F32) * factor
    grad_keys = jnp.einsum("jts,tjd->sd", ds_b, query_b, preferred_element_type=F32) * factor
    grad_values = jnp.einsum("jts,tjd->sd", probs_b, do_b, preferred_element_type=F32)
    own = scatter(jnp.concatenate([grad_keys, grad_values], 1).astype(BF), ("yl",))
    dv_b = own[:, head:]
    grad_q_norm = turn_back(grad_query.astype(BF).astype(F32), cosine, sine)
    grad_k_norm = turn_back(own[:, :head].astype(F32).reshape(-1, 1, head), cosine, sine)
    term_query = jnp.sum(grad_q_norm * unit_q, (0, 1))
    term_key = jnp.sum(grad_k_norm * unit_k, (0, 1))
    dq_b = norm_back(grad_q_norm * gain_query, unit_q, scale_q).reshape(-1, qc).astype(BF)
    dk_b = norm_back(grad_k_norm * gain_key, unit_k, scale_k).reshape(-1, kc).astype(BF)
    dqkv = jnp.concatenate([dq_b, dk_b, dv_b], 1)
    grad_h = scatter(mm_t(dqkv, w_qkv).astype(BF), TP).astype(F32)
    term_in = jnp.sum(grad_h * unit_in, 0)
    tokens_grad = (grad_mid + norm_back(grad_h * gain_in, unit_in, scale_in)).astype(BF)

    def by_cols(part):
        cols = part.shape[1]
        part = part.astype(BF).reshape(n_z, n_yl, n_core, n_fs, -1, cols)
        part = part.transpose(1, 3, 0, 2, 4, 5).reshape(-1, cols)
        return scatter(part, DP)

    mine = jnp.concatenate([by_cols(t_mm(h2, dgu)), by_cols(t_mm(h, dqkv))], 1)
    mine = mine.reshape(n_tp, -1, mine.shape[1])
    mine = lax.all_to_all(mine, TP, 0, 0, tiled=True).transpose(1, 0, 2).astype(F32)

    def take(at, n):
        return mine[:, :, at : at + n].reshape(-1, n_tp * n)

    grad_gate_w, grad_up_w = take(0, fc), take(fc, fc)
    grad_q_w, grad_k_w, grad_v_w = (
        take(2 * fc, qc),
        take(2 * fc + qc, kc),
        take(2 * fc + qc + kc, kc),
    )
    blocks = n_yl * n_fs
    late = jnp.concatenate(
        [
            t_mm(act_b, g).astype(BF).reshape(blocks, -1, width),
            t_mm(attended, dz).astype(BF).reshape(blocks, -1, width),
        ],
        1,
    )
    ff_dev = fc // blocks
    late = scatter(late, DP)[0]
    late = lax.ppermute(
        late, ("yl", "core"), [(a * n_core + b, b * n_yl + a) for a in range(n_yl) for b in range(n_core)]
    ).astype(F32)
    grad_down, grad_out = late[:ff_dev], late[ff_dev:]
    sum_in, sum_mid, sum_query, sum_key = lax.psum((term_in, term_mid, term_query, term_key), ALL)
    return (
        mixed.reshape(tokens.shape),
        tokens_grad.reshape(tokens.shape),
        sum_in,
        grad_q_w,
        grad_k_w,
        grad_v_w,
        sum_query,
        sum_key,
        grad_out,
        sum_mid,
        grad_gate_w,
        grad_up_w,
        grad_down,
    )


def solution(mesh):
    fine = Mesh(mesh.devices.reshape(4, 2, 2, 4, 2), ALL)
    ctx, fsdp = ("z", "yl", "core"), FS
    act = P(fsdp, None, ctx, None, None)
    weight = P(fsdp, None)
    grad = P(ctx + fsdp, None)
    placed = (
        act, P(), weight, weight, weight, P(), P(), weight, P(), weight, weight, weight, act,
    )
    return jax.shard_map(
        shards,
        mesh=fine,
        in_specs=placed,
        out_specs=(act, act, P(), grad, grad, grad, P(), P(), grad, P(), grad, grad, grad),
        check_vma=False,
    )
```

```python
import functools

import jax
import jax.numpy as jnp
from jax import lax
from jax.experimental import pallas as pl
from jax.experimental.pallas import tpu as pltpu
from jax.sharding import Mesh, PartitionSpec as P

EPS = 1e-06
THETA = 1000000.0
BF = jnp.bfloat16
F32 = jnp.float32
TP = ("z", "core")
FS = ("x", "yh")
DP = ("yl", "x", "yh")
ALL = ("z", "yl", "core", "x", "yh")
MESH = pl.DeviceIdType.MESH
VMEM = pl.BlockSpec(memory_space=pltpu.VMEM)
HBM = pl.BlockSpec(memory_space=pl.ANY)
MB = 2**20
LOG2E = 1.4426950408889634


class Place:
    def __init__(self):
        self.z, self.yl, self.core, self.x, self.yh = (lax.axis_index(a) for a in ALL)
        self.t = 2 * self.z + self.core
        self.shard = 2 * self.x + self.yh

    def at(self, z=None, yl=None, core=None, x=None, yh=None):
        here = (self.z, self.yl, self.core, self.x, self.yh)
        return tuple(h if n is None else n for h, n in zip(here, (z, yl, core, x, yh)))

    def up(self, n):
        return lax.rem(self.z + n, 4)

    def east(self, n):
        return lax.rem(self.x + n, 4)

    def peers(self, which):
        table = {
            "z": [self.at(z=self.up(1)), self.at(z=self.up(3))],
            "sib": [self.at(core=1 - self.core)],
            "x": [self.at(x=self.east(1)), self.at(x=self.east(3))],
            "cross": [self.at(yl=1 - self.yl, yh=1 - self.yh)],
            "pair": [self.at(yl=1 - self.yl)],
            "tp": [
                self.at(z=self.up(dz), core=lax.rem(self.core + dc, 2))
                for dz in range(4)
                for dc in range(2)
                if dz or dc
            ],
        }
        return [p for name in which for p in table[name]]


class Wire:
    def __init__(self, send_sem, recv_sem, here_sem):
        self.send_sem, self.recv_sem, self.here_sem = send_sem, recv_sem, here_sem
        self.n = self.m = 0
        self.sent = []

    def send(self, src, dst, peer):
        copy = pltpu.make_async_remote_copy(
            src_ref=src,
            dst_ref=dst,
            send_sem=self.send_sem.at[self.n],
            recv_sem=self.recv_sem.at[self.n],
            device_id=peer,
            device_id_type=MESH,
        )
        self.n += 1
        copy.start()
        self.sent.append(copy)
        return copy

    def here(self, src, dst):
        copy = pltpu.make_async_copy(src, dst, self.here_sem.at[self.m])
        self.m += 1
        copy.start()
        return copy

    def finish(self):
        for copy in self.sent:
            copy.wait_send()


def sems(n, m):
    return [
        pltpu.SemaphoreType.DMA((n,)),
        pltpu.SemaphoreType.DMA((n,)),
        pltpu.SemaphoreType.DMA((m,)),
    ]


def meet(peers):
    barrier = pltpu.get_barrier_semaphore()
    for peer in peers:
        pl.semaphore_signal(barrier, inc=1, device_id=peer, device_id_type=MESH)
    pl.semaphore_wait(barrier, len(peers))


def run(*tasks):
    tasks = list(tasks)
    while tasks:
        advance(tasks)


def advance(tasks):
    for task in list(tasks):
        try:
            next(task)
        except StopIteration:
            tasks.remove(task)


def swap_kernel(kv, far, send_sem, recv_sem, here_sem):
    p = Place()
    w = Wire(send_sem, recv_sem, here_sem)
    meet(p.peers(("pair",)))
    w.send(kv, far, p.at(yl=1 - p.yl)).wait()


def swap(kv):
    return pl.pallas_call(
        swap_kernel,
        out_shape=jax.ShapeDtypeStruct(kv.shape, kv.dtype),
        in_specs=[VMEM],
        out_specs=VMEM,
        scratch_shapes=sems(1, 1),
        compiler_params=pltpu.CompilerParams(
            collective_id=0, has_side_effects=True, vmem_limit_bytes=16 * MB
        ),
        name="swap",
    )(kv)

def rotary(positions, width):
    half = width // 2
    freq = THETA ** (-2.0 * jnp.arange(half, dtype=F32) / width)
    angle = positions.astype(F32)[:, None] * freq[None, :]
    cosine = jnp.concatenate([jnp.cos(angle), jnp.cos(angle)], 1)[:, None, :]
    sine = jnp.concatenate([jnp.sin(angle), jnp.sin(angle)], 1)[:, None, :]
    return (cosine, sine)


def turn(vals, cosine, sine):
    half = vals.shape[-1] // 2
    return vals * cosine + jnp.concatenate([-vals[..., half:], vals[..., :half]], -1) * sine


def turn_back(grads, cosine, sine):
    half = grads.shape[-1] // 2
    moved = grads * sine
    return grads * cosine + jnp.concatenate([moved[..., half:], -moved[..., :half]], -1)


def row_norm(vals):
    scale = lax.rsqrt(jnp.mean(vals * vals, -1, keepdims=True) + EPS)
    return (vals * scale, scale)


def norm_back(grad_unit, unit, scale):
    return scale * (grad_unit - unit * jnp.mean(grad_unit * unit, -1, keepdims=True))


def mm(left, right):
    return jnp.dot(left, right, preferred_element_type=F32)


def mm_t(left, right):
    return lax.dot_general(left, right, (((1,), (1,)), ((), ())), preferred_element_type=F32)


def t_mm(left, right):
    return lax.dot_general(left, right, (((0,), (0,)), ((), ())), preferred_element_type=F32)


def gather(val, axes):
    return lax.all_gather(val, axes, axis=0, tiled=True)


def scatter(val, axes):
    return lax.psum_scatter(val, axes, scatter_dimension=0, tiled=True)


def shards(
    tokens,
    gain_in,
    query_weight,
    key_weight,
    value_weight,
    gain_query,
    gain_key,
    out_weight,
    gain_mid,
    gate_weight,
    up_weight,
    down_weight,
    cotangent,
):
    half = tokens.shape[3]
    width = tokens.shape[4]
    n_z, n_yl, n_core = (lax.axis_size(a) for a in ("z", "yl", "core"))
    n_tp = n_z * n_core
    n_fs = lax.axis_size("x") * lax.axis_size("yh")
    n_ctx = n_tp * n_yl
    rows = 2 * half
    head = gain_query.shape[0]
    kv_width = key_weight.shape[1]
    q_width = query_weight.shape[1]
    hidden = gate_weight.shape[1]
    factor = head ** (-0.5)
    qc, kc, fc = q_width // n_tp, kv_width // n_tp, hidden // n_tp
    group = qc // head
    t = lax.axis_index(TP)
    yl = lax.axis_index("yl")

    def positions(lane):
        idx = jnp.arange(n_tp * rows, dtype=jnp.int32)
        who, spot = idx // rows, idx % rows
        c = (who // n_core) * (n_yl * n_core) + lane * n_core + who % n_core
        block = jnp.where(spot // half == 0, c, 2 * n_ctx - 1 - c)
        return block * half + spot % half

    query_pos = positions(yl)
    key_pos = jnp.concatenate([positions(i) for i in range(n_yl)])
    allowed = key_pos[None, :] <= query_pos[:, None]
    cosine, sine = rotary(query_pos, head)

    cut = lambda w, n: lax.dynamic_slice_in_dim(w, t * n, n, 1)
    w_qkv = gather(
        jnp.concatenate([cut(query_weight, qc), cut(key_weight, kc), cut(value_weight, kc)], 1), FS
    )
    w_gu = gather(jnp.concatenate([cut(gate_weight, fc), cut(up_weight, fc)], 1), FS)
    o_s, d_s = out_weight.shape[0] // n_tp, down_weight.shape[0] // n_tp
    rows_od = jnp.concatenate(
        [
            lax.dynamic_slice_in_dim(out_weight, t * o_s, o_s, 0),
            lax.dynamic_slice_in_dim(down_weight, t * d_s, d_s, 0),
        ],
        0,
    )
    rows_od = lax.ppermute(
        rows_od,
        TP + FS,
        [(a * n_fs + b, b * n_fs + a) for a in range(n_tp) for b in range(n_fs)],
    )
    w_od = gather(rows_od[None], FS)
    w_out = w_od[:, :o_s].reshape(n_fs * o_s, width)
    w_down = w_od[:, o_s:].reshape(n_fs * d_s, width)

    x = tokens.reshape(rows, width).astype(F32)
    unit_in, scale_in = row_norm(x)
    h = gather((unit_in * gain_in).astype(BF), TP)
    grad_l = cotangent.reshape(rows, width)
    g = gather(grad_l, TP)
    qkv = mm(h, w_qkv)
    value_b = qkv[:, qc + kc :].astype(BF)
    unit_q, scale_q = row_norm(qkv[:, :qc].reshape(-1, group, head))
    unit_k, scale_k = row_norm(qkv[:, qc : qc + kc].reshape(-1, 1, head))
    query_b = turn(unit_q * gain_query, cosine, sine).astype(BF)
    keys_b = turn(unit_k * gain_key, cosine, sine).astype(BF).reshape(-1, head)
    kv = jnp.concatenate([keys_b, value_b], 1)
    kv_far = swap(kv)
    kv = jnp.concatenate([jnp.where(yl == 0, kv, kv_far), jnp.where(yl == 0, kv_far, kv)])
    keys, values = kv[:, :head], kv[:, head:]

    raw = jnp.einsum("tjd,sd->jts", query_b, keys, preferred_element_type=F32) * factor
    scores = jnp.where(allowed, raw, -1e30)
    top = jnp.max(scores, -1, keepdims=True)
    expo = jnp.exp(scores - top)
    probs = expo / jnp.sum(expo, -1, keepdims=True)
    probs_b = probs.astype(BF)
    attended = jnp.einsum("jts,sd->tjd", probs_b, values, preferred_element_type=F32)
    attended = attended.reshape(-1, qc).astype(BF)
    y_mid = x + scatter(mm(attended, w_out).astype(BF), TP).astype(F32)
    unit_mid, scale_mid = row_norm(y_mid)
    h2 = gather((unit_mid * gain_mid).astype(BF), TP)
    gu = mm(h2, w_gu)
    gate, upper = gu[:, :fc], gu[:, fc:]
    sig = jax.nn.sigmoid(gate)
    silu_gate = gate * sig
    act_b = (silu_gate * upper).astype(BF)
    mixed = (y_mid + scatter(mm(act_b, w_down).astype(BF), TP).astype(F32)).astype(BF)
    grad_act = mm_t(g, w_down)
    dgate_b = (grad_act * upper * sig * (1.0 + gate * (1.0 - sig))).astype(BF)
    dup_b = (grad_act * silu_gate).astype(BF)
    dgu = jnp.concatenate([dgate_b, dup_b], 1)
    grad_h2 = scatter(mm_t(dgu, w_gu).astype(BF), TP).astype(F32)
    term_mid = jnp.sum(grad_h2 * unit_mid, 0)
    grad_mid = grad_l.astype(F32) + norm_back(grad_h2 * gain_mid, unit_mid, scale_mid)
    dz = gather(grad_mid.astype(BF), TP)
    do_b = mm_t(dz, w_out).astype(BF).reshape(-1, group, head)
    grad_probs = jnp.einsum("tjd,sd->jts", do_b, values, preferred_element_type=F32)
    delta = jnp.sum(probs * grad_probs, -1, keepdims=True)
    ds_b = (probs * (grad_probs - delta)).astype(BF)
    grad_query = jnp.einsum("jts,sd->tjd", ds_b, keys, preferred_element_type=F32) * factor
    grad_keys = jnp.einsum("jts,tjd->sd", ds_b, query_b, preferred_element_type=F32) * factor
    grad_values = jnp.einsum("jts,tjd->sd", probs_b, do_b, preferred_element_type=F32)
    own = scatter(jnp.concatenate([grad_keys, grad_values], 1).astype(BF), ("yl",))
    dv_b = own[:, head:]
    grad_q_norm = turn_back(grad_query.astype(BF).astype(F32), cosine, sine)
    grad_k_norm = turn_back(own[:, :head].astype(F32).reshape(-1, 1, head), cosine, sine)
    term_query = jnp.sum(grad_q_norm * unit_q, (0, 1))
    term_key = jnp.sum(grad_k_norm * unit_k, (0, 1))
    dq_b = norm_back(grad_q_norm * gain_query, unit_q, scale_q).reshape(-1, qc).astype(BF)
    dk_b = norm_back(grad_k_norm * gain_key, unit_k, scale_k).reshape(-1, kc).astype(BF)
    dqkv = jnp.concatenate([dq_b, dk_b, dv_b], 1)
    grad_h = scatter(mm_t(dqkv, w_qkv).astype(BF), TP).astype(F32)
    term_in = jnp.sum(grad_h * unit_in, 0)
    tokens_grad = (grad_mid + norm_back(grad_h * gain_in, unit_in, scale_in)).astype(BF)

    def by_cols(part):
        cols = part.shape[1]
        part = part.astype(BF).reshape(n_z, n_yl, n_core, n_fs, -1, cols)
        part = part.transpose(1, 3, 0, 2, 4, 5).reshape(-1, cols)
        return scatter(part, DP)

    mine = jnp.concatenate([by_cols(t_mm(h2, dgu)), by_cols(t_mm(h, dqkv))], 1)
    mine = mine.reshape(n_tp, -1, mine.shape[1])
    mine = lax.all_to_all(mine, TP, 0, 0, tiled=True).transpose(1, 0, 2).astype(F32)

    def take(at, n):
        return mine[:, :, at : at + n].reshape(-1, n_tp * n)

    grad_gate_w, grad_up_w = take(0, fc), take(fc, fc)
    grad_q_w, grad_k_w, grad_v_w = (
        take(2 * fc, qc),
        take(2 * fc + qc, kc),
        take(2 * fc + qc + kc, kc),
    )
    blocks = n_yl * n_fs
    late = jnp.concatenate(
        [
            t_mm(act_b, g).astype(BF).reshape(blocks, -1, width),
            t_mm(attended, dz).astype(BF).reshape(blocks, -1, width),
        ],
        1,
    )
    ff_dev = fc // blocks
    late = scatter(late, DP)[0]
    late = lax.ppermute(
        late, ("yl", "core"), [(a * n_core + b, b * n_yl + a) for a in range(n_yl) for b in range(n_core)]
    ).astype(F32)
    grad_down, grad_out = late[:ff_dev], late[ff_dev:]
    sum_in, sum_mid, sum_query, sum_key = lax.psum((term_in, term_mid, term_query, term_key), ALL)
    return (
        mixed.reshape(tokens.shape),
        tokens_grad.reshape(tokens.shape),
        sum_in,
        grad_q_w,
        grad_k_w,
        grad_v_w,
        sum_query,
        sum_key,
        grad_out,
        sum_mid,
        grad_gate_w,
        grad_up_w,
        grad_down,
    )


def solution(mesh):
    fine = Mesh(mesh.devices.reshape(4, 2, 2, 4, 2), ALL)
    ctx, fsdp = ("z", "yl", "core"), FS
    act = P(fsdp, None, ctx, None, None)
    weight = P(fsdp, None)
    grad = P(ctx + fsdp, None)
    placed = (
        act, P(), weight, weight, weight, P(), P(), weight, P(), weight, weight, weight, act,
    )
    return jax.shard_map(
        shards,
        mesh=fine,
        in_specs=placed,
        out_specs=(act, act, P(), grad, grad, grad, P(), P(), grad, P(), grad, grad, grad),
        check_vma=False,
    )
```

```python
import functools

import jax
import jax.numpy as jnp
from jax import lax
from jax.experimental import pallas as pl
from jax.experimental.pallas import tpu as pltpu
from jax.sharding import Mesh, PartitionSpec as P

EPS = 1e-06
THETA = 1000000.0
BF = jnp.bfloat16
F32 = jnp.float32
TP = ("z", "core")
FS = ("x", "yh")
DP = ("yl", "x", "yh")
ALL = ("z", "yl", "core", "x", "yh")
MESH = pl.DeviceIdType.MESH
VMEM = pl.BlockSpec(memory_space=pltpu.VMEM)
HBM = pl.BlockSpec(memory_space=pl.ANY)
MB = 2**20
LOG2E = 1.4426950408889634


class Place:
    def __init__(self):
        self.z, self.yl, self.core, self.x, self.yh = (lax.axis_index(a) for a in ALL)
        self.t = 2 * self.z + self.core
        self.shard = 2 * self.x + self.yh
        self.y = 2 * self.yh + self.yl

    def at(self, z=None, yl=None, core=None, x=None, yh=None):
        here = (self.z, self.yl, self.core, self.x, self.yh)
        return tuple(h if n is None else n for h, n in zip(here, (z, yl, core, x, yh)))

    def up(self, n):
        return lax.rem(self.z + n, 4)

    def east(self, n):
        return lax.rem(self.x + n, 4)

    def north(self, n):
        y = lax.rem(self.y + n, 4)
        return self.at(yh=y // 2, yl=lax.rem(y, 2))

    def peers(self, which):
        table = {
            "z": [self.at(z=self.up(1)), self.at(z=self.up(3))],
            "sib": [self.at(core=1 - self.core)],
            "x": [self.at(x=self.east(1)), self.at(x=self.east(3))],
            "cross": [self.at(yl=1 - self.yl, yh=1 - self.yh)],
            "pair": [self.at(yl=1 - self.yl)],
            "plane": [self.at(x=self.east(d)) for d in (1, 2, 3)]
            + [self.north(d) for d in (1, 2, 3)],
            "swap": [self.at(yl=1 - self.yl, core=1 - self.core)],
            "tp": [
                self.at(z=self.up(dz), core=lax.rem(self.core + dc, 2))
                for dz in range(4)
                for dc in range(2)
                if dz or dc
            ],
        }
        return [p for name in which for p in table[name]]


class Wire:
    def __init__(self, send_sem, recv_sem, here_sem):
        self.send_sem, self.recv_sem, self.here_sem = send_sem, recv_sem, here_sem
        self.n = self.m = 0
        self.sent = []

    def send(self, src, dst, peer):
        copy = pltpu.make_async_remote_copy(
            src_ref=src,
            dst_ref=dst,
            send_sem=self.send_sem.at[self.n],
            recv_sem=self.recv_sem.at[self.n],
            device_id=peer,
            device_id_type=MESH,
        )
        self.n += 1
        copy.start()
        self.sent.append(copy)
        return copy

    def here(self, src, dst):
        copy = pltpu.make_async_copy(src, dst, self.here_sem.at[self.m])
        self.m += 1
        copy.start()
        return copy

    def finish(self):
        for copy in self.sent:
            copy.wait_send()


def sems(n, m):
    return [
        pltpu.SemaphoreType.DMA((n,)),
        pltpu.SemaphoreType.DMA((n,)),
        pltpu.SemaphoreType.DMA((m,)),
    ]


def meet(peers):
    barrier = pltpu.get_barrier_semaphore()
    for peer in peers:
        pl.semaphore_signal(barrier, inc=1, device_id=peer, device_id_type=MESH)
    pl.semaphore_wait(barrier, len(peers))


def run(*tasks):
    tasks = list(tasks)
    while tasks:
        advance(tasks)


def advance(tasks):
    for task in list(tasks):
        try:
            next(task)
        except StopIteration:
            tasks.remove(task)


def gather_z(w, p, own, dst):
    up, down, sib = p.at(z=p.up(1)), p.at(z=p.up(3)), p.at(core=1 - p.core)
    before, after, far = (2 * p.up(n) + p.core for n in (3, 1, 2))
    u0 = w.send(own(0), dst(p.t, 0), up)
    d1 = w.send(own(1), dst(p.t, 1), down)
    u1 = w.send(own(1), dst(p.t, 1), up)
    d0 = w.send(own(0), dst(p.t, 0), down)
    s = [w.send(own(k), dst(p.t, k), sib) for k in (0, 1)]

    def on(t, k):
        s.append(w.send(dst(t, k), dst(t, k), sib))

    yield
    u0.wait_recv()
    f0 = w.send(dst(before, 0), dst(before, 0), up)
    on(before, 0)
    d1.wait_recv()
    f1 = w.send(dst(after, 1), dst(after, 1), down)
    on(after, 1)
    yield
    u1.wait_recv()
    on(before, 1)
    d0.wait_recv()
    on(after, 0)
    yield
    f0.wait_recv()
    on(far, 0)
    f1.wait_recv()
    on(far, 1)
    yield
    for copy in s:
        copy.wait_recv()


def gather_xy(w, p, own, dst, n, ready=None):
    east, west = p.at(x=p.east(1)), p.at(x=p.east(3))
    cross, pair = p.at(yl=1 - p.yl, yh=1 - p.yh), p.at(yl=1 - p.yl)
    half = n // 2
    west_s, east_s, far_s = (2 * p.east(k) + p.yh for k in (3, 1, 2))
    mine = p.yl * half
    other = half - mine
    flip = 1 - 2 * p.yh

    def over(s):
        return w.send(dst(s, mine, half), dst(s, mine, half), cross)

    def along(s):
        return w.send(dst(s + flip, other, half), dst(s + flip, other, half), pair)

    e0 = w.send(own(0, half), dst(p.shard, 0, half), east)
    w1 = w.send(own(half, half), dst(p.shard, half, half), west)
    c0 = w.send(own(mine, half), dst(p.shard, mine, half), cross)
    e1 = w.send(own(half, half), dst(p.shard, half, half), east)
    w0 = w.send(own(0, half), dst(p.shard, 0, half), west)
    yield
    e0.wait_recv()
    f0 = w.send(dst(west_s, 0, half), dst(west_s, 0, half), east)
    w1.wait_recv()
    f1 = w.send(dst(east_s, half, half), dst(east_s, half, half), west)
    yield
    c0.wait_recv()
    a0 = along(p.shard)
    e1.wait_recv()
    c1 = over(west_s)
    w0.wait_recv()
    c2 = over(east_s)
    if ready:
        ready(west_s)
        ready(east_s)
    yield
    f0.wait_recv()
    f1.wait_recv()
    c3 = over(far_s)
    if ready:
        ready(far_s)
    yield
    c1.wait_recv()
    a1 = along(west_s)
    c2.wait_recv()
    a2 = along(east_s)
    yield
    c3.wait_recv()
    a3 = along(far_s)
    yield
    for s, a in ((p.shard, a0), (west_s, a1), (east_s, a2), (far_s, a3)):
        a.wait_recv()
        if ready:
            ready(s + flip)


def norm_rope(raw, gain, cosine, sine):
    unit = raw * lax.rsqrt(jnp.mean(raw * raw, -1, keepdims=True) + EPS)
    vals = unit * gain
    return vals * cosine + pltpu.roll(vals, 64, 1) * sine


def front_kernel(
    tok, gain, w_own, cosine, sine, gq, gk, h, w_qkv, q, kv, raw, send_sem, recv_sem, here_sem
):
    p = Place()
    w = Wire(send_sem, recv_sem, here_sem)
    w_qkv[pl.ds(pl.multiple_of(p.shard * 256, 256), 256)] = w_own[...]
    for k in (0, 1):
        x = tok[k].astype(F32)
        unit = x * lax.rsqrt(jnp.mean(x * x, -1, keepdims=True) + EPS)
        h[p.t if k == 0 else 15 - p.t] = (unit * gain[...]).astype(BF)
    meet(p.peers(("z", "sib", "x", "cross", "pair")))

    def block(t, k):
        return h.at[t if k == 0 else 15 - t]

    def part(s, at, n):
        return w_qkv.at[pl.ds(pl.multiple_of(s * 256 + at, 128), n)]

    run(
        gather_z(w, p, lambda k: block(p.t, k), block),
        gather_xy(w, p, lambda at, n: part(p.shard, at, n), part, 256),
    )

    @pl.loop(0, 4)
    def _(j):
        at = pl.ds(pl.multiple_of(j * 256, 256), 256)
        rows_h = h[pl.ds(4 * j, 4)].reshape(256, 2048)
        out = jnp.dot(rows_h, w_qkv[...], preferred_element_type=F32)
        cos, sin = cosine[at], sine[at]
        raw[at] = out[:, :384]
        for n in (0, 1):
            cols = slice(n * 128, n * 128 + 128)
            q[at, cols] = norm_rope(out[:, cols], gq[...], cos, sin).astype(BF)
        kv[at, 0:128] = norm_rope(out[:, 256:384], gk[...], cos, sin).astype(BF)
        kv[at, 128:256] = out[:, 384:].astype(BF)

    w.finish()


def front(tok, gain, w_own, cosine, sine, gq, gk):
    sds = jax.ShapeDtypeStruct
    return pl.pallas_call(
        front_kernel,
        out_shape=(
            sds((16, 64, 2048), BF),
            sds((2048, 512), BF),
            sds((1024, 256), BF),
            sds((1024, 256), BF),
            sds((1024, 384), F32),
        ),
        in_specs=[VMEM] * 7,
        out_specs=[VMEM] * 5,
        scratch_shapes=sems(48, 4),
        compiler_params=pltpu.CompilerParams(
            collective_id=0, has_side_effects=True, vmem_limit_bytes=48 * MB
        ),
        name="front",
    )(tok, gain, w_own, cosine, sine, gq, gk)


SCALE = 128**-0.5 * LOG2E


def dot_t(a, b):
    return lax.dot_general(a, b, (((1,), (1,)), ((), ())), preferred_element_type=F32)


def t_dot(a, b):
    return lax.dot_general(a, b, (((0,), (0,)), ((), ())), preferred_element_type=F32)


def both(ref, at):
    return jnp.concatenate([ref[at, 0:128], ref[at, 128:256]], 0)


def weights_of(q, k, j, edge):
    s = jnp.exp2(dot_t(q, k) * SCALE)
    last = jnp.where(edge, s[:, j * 128 :], 0.0)
    return last if j == 0 else jnp.concatenate([s[:, : j * 128], last], 1)


def edges(p, j):
    row = lax.broadcasted_iota(jnp.int32, (256, 128), 0) % 128
    col = lax.broadcasted_iota(jnp.int32, (256, 128), 1)
    seen = (p.yl if j < 4 else 1 - p.yl) * 128
    return col <= row, col < seen


def attend_kernel(
    q, kv, cot, wo, gu_own, o, o_tok, kv_far, g, w_out, w_gu, send_sem, recv_sem, here_sem
):
    p = Place()
    w = Wire(send_sem, recv_sem, here_sem)
    g[p.t] = cot[0]
    g[15 - p.t] = cot[1]
    w_out[p.shard, p.core] = wo[...]
    w_gu[p.shard] = gu_own[...]
    meet(p.peers(("tp", "x", "cross", "pair")))
    swap = w.send(kv, kv_far, p.at(yl=1 - p.yl))

    def block(t, k):
        return g.at[t if k == 0 else 15 - t]

    def part(s, at, n):
        return w_out.at[s, p.core, pl.ds(pl.multiple_of(at, 64), n)]

    twin = []

    def ready(s):
        twin.append(
            w.send(w_out.at[s, p.core], w_out.at[s, p.core], p.at(core=1 - p.core))
        )

    ready(p.shard)

    def part_gu(s, at, n):
        return w_gu.at[s, pl.ds(pl.multiple_of(at, 128), n)]

    tasks = [
        gather_z(w, p, lambda k: block(p.t, k), block),
        gather_xy(w, p, lambda at, n: part(p.shard, at, n), part, 128, ready),
        gather_xy(w, p, lambda at, n: part_gu(p.shard, at, n), part_gu, 256),
    ]
    advance(tasks)
    swap.wait_recv()
    spread = []
    mine = pl.ds(pl.multiple_of(p.t * 256, 256), 256)
    for j in range(8):
        at = pl.ds(j * 128, 128)
        keys = pl.ds(0, j * 128 + 128)
        tri, seen = edges(p, j)
        qj = both(q, at)
        near = weights_of(qj, kv[keys, 0:128], j, tri)
        far = weights_of(qj, kv_far[keys, 0:128], j, seen)
        total = jnp.sum(near, -1, keepdims=True) + jnp.sum(far, -1, keepdims=True)
        out = jnp.dot(near.astype(BF), kv[keys, 128:256], preferred_element_type=F32)
        out += jnp.dot(far.astype(BF), kv_far[keys, 128:256], preferred_element_type=F32)
        out = (out / total).astype(BF)
        for n in (0, 1):
            o[2 * j : 2 * j + 2, :, n * 128 : n * 128 + 128] = out[
                n * 128 : n * 128 + 128
            ].reshape(2, 64, 128)
        advance(tasks)
    run(*tasks)
    for dz in range(4):
        for dc in range(2):
            z, core = p.up(dz), lax.rem(p.core + dc, 2)
            t = 2 * z + core
            for k in (0, 1):
                src = o.at[t if k == 0 else 15 - t]
                dst = o_tok.at[k, :, mine]
                if dz or dc:
                    spread.append(w.send(src, dst, p.at(z=z, core=core)))
                else:
                    spread.append(w.here(src, dst))
    for copy in twin:
        copy.wait_recv()
    for copy in spread[:2]:
        copy.wait()
    for copy in spread[2:]:
        copy.wait_recv()
    w.finish()


def attend(q, kv, cot, wo, gu_own):
    sds = jax.ShapeDtypeStruct
    return pl.pallas_call(
        attend_kernel,
        out_shape=(
            sds((16, 64, 256), BF),
            sds((2, 64, 2048), BF),
            sds((1024, 256), BF),
            sds((16, 64, 2048), BF),
            sds((8, 2, 128, 2048), BF),
            sds((8, 256, 1536), BF),
        ),
        in_specs=[VMEM] * 5,
        out_specs=[VMEM] * 6,
        scratch_shapes=sems(80, 8),
        compiler_params=pltpu.CompilerParams(
            collective_id=1, has_side_effects=True, vmem_limit_bytes=56 * MB
        ),
        name="attend",
    )(q, kv, cot, wo, gu_own)


def mid_kernel(h2_own, down_own, h2, w_down, send_sem, recv_sem, here_sem):
    p = Place()
    w = Wire(send_sem, recv_sem, here_sem)
    h2[p.t] = h2_own[0]
    h2[15 - p.t] = h2_own[1]
    w_down[p.shard] = down_own[...]
    meet(p.peers(("z", "sib", "x", "cross", "pair")))

    def block(t, k):
        return h2.at[t if k == 0 else 15 - t]

    def part(s, at, n):
        return w_down.at[s, pl.ds(pl.multiple_of(at, 48), n)]

    run(
        gather_z(w, p, lambda k: block(p.t, k), block),
        gather_xy(w, p, lambda at, n: part(p.shard, at, n), part, 96),
    )
    w.finish()


def mid(h2_own, down_own):
    sds = jax.ShapeDtypeStruct
    return pl.pallas_call(
        mid_kernel,
        out_shape=(sds((16, 64, 2048), BF), sds((8, 96, 2048), BF)),
        in_specs=[VMEM] * 2,
        out_specs=[VMEM] * 2,
        scratch_shapes=sems(48, 1),
        compiler_params=pltpu.CompilerParams(
            collective_id=2, has_side_effects=True, vmem_limit_bytes=32 * MB
        ),
        name="mid",
    )(h2_own, down_own)


def add(*vals):
    total = vals[0].astype(F32)
    for val in vals[1:]:
        total = total + val.astype(F32)
    return total


def z_room():
    return [
        pltpu.VMEM((4, 2, 64, 2048), BF),
        pltpu.VMEM((4, 2, 64, 2048), BF),
        pltpu.VMEM((2, 64, 2048), BF),
        pltpu.VMEM((2, 2, 64, 2048), BF),
    ]


def reduce_z(w, p, part, room, out):
    near, mine, relay, last = room
    up, down, sib = p.at(z=p.up(1)), p.at(z=p.up(3)), p.at(core=1 - p.core)

    def block(n, core, k):
        t = 2 * p.up(n) + core
        return t if k == 0 else 15 - t

    first = {}
    for n in (2, 1, 3, 0):
        for k in (0, 1):
            first[n, k] = w.send(part.at[block(n, 1 - p.core, k)], near.at[n, k], sib)

    def fold(n, k):
        first[n, k].wait_recv()
        mine[n, k] = add(part[block(n, p.core, k)], near[n, k]).astype(BF)

    yield
    fold(2, 0)
    e0 = w.send(mine.at[2, 0], relay.at[0], up)
    fold(2, 1)
    e1 = w.send(mine.at[2, 1], relay.at[1], down)
    fold(1, 1)
    a1 = w.send(mine.at[1, 1], last.at[0, 1], up)
    fold(3, 0)
    b0 = w.send(mine.at[3, 0], last.at[1, 0], down)
    fold(1, 0)
    fold(3, 1)
    yield
    fold(0, 0)
    fold(0, 1)
    e0.wait_recv()
    mine[1, 0] = add(mine[1, 0], relay[0]).astype(BF)
    a0 = w.send(mine.at[1, 0], last.at[0, 0], up)
    e1.wait_recv()
    mine[3, 1] = add(mine[3, 1], relay[1]).astype(BF)
    b1 = w.send(mine.at[3, 1], last.at[1, 1], down)
    yield
    for k, (a, b) in enumerate(((a0, b0), (a1, b1))):
        a.wait_recv()
        b.wait_recv()
        out[k] = add(mine[0, k], last[0, k], last[1, k])


def xy_room(rows, cols):
    half = cols // 2
    return [
        pltpu.VMEM((3, 4, rows, half), BF),
        pltpu.VMEM((4, rows, half), BF),
        pltpu.VMEM((3, rows, half), BF),
    ] * 2


def reduce_xy(w, p, part, room, out):
    ra, sa, fa, rb, sb, fb = room
    half = part.shape[3] // 2
    left, right = pl.ds(0, half), pl.ds(half, half)
    spans = (1, 2, 3)
    easts = [p.at(x=p.east(d)) for d in spans]
    norths = [p.north(d) for d in spans]
    ca = [w.send(part.at[p.east(d), :, :, left], ra.at[d - 1], easts[d - 1]) for d in spans]
    cb = [
        w.send(part.at[:, lax.rem(p.y + d, 4), :, right], rb.at[d - 1], norths[d - 1])
        for d in spans
    ]
    yield
    yield
    for copy in ca:
        copy.wait_recv()

    @pl.loop(0, 4)
    def _(y):
        sa[y] = add(part[p.x, y, :, left], ra[0, y], ra[1, y], ra[2, y]).astype(BF)

    da = [w.send(sa.at[lax.rem(p.y + d, 4)], fa.at[d - 1], norths[d - 1]) for d in spans]
    yield
    for copy in cb:
        copy.wait_recv()

    @pl.loop(0, 4)
    def _(x):
        sb[x] = add(part[x, p.y, :, right], rb[0, x], rb[1, x], rb[2, x]).astype(BF)

    db = [w.send(sb.at[p.east(d)], fb.at[d - 1], easts[d - 1]) for d in spans]
    yield
    for copy in da:
        copy.wait_recv()
    out[:, left] = add(sa[p.y], fa[0], fa[1], fa[2]).astype(BF)
    yield
    for copy in db:
        copy.wait_recv()
    out[:, right] = add(sb[p.x], fb[0], fb[1], fb[2]).astype(BF)


def sums_kernel(part, grads, out, mine, *rest):
    zr, xr, (send_sem, recv_sem, here_sem) = rest[:4], rest[4:10], rest[10:]
    p = Place()
    w = Wire(send_sem, recv_sem, here_sem)
    meet(p.peers(("z", "sib", "plane")))
    run(reduce_z(w, p, part, zr, out), reduce_xy(w, p, grads, xr, mine))
    w.finish()


def sums(part, grads, cid):
    sds = jax.ShapeDtypeStruct
    _, _, rows, cols = grads.shape
    return pl.pallas_call(
        sums_kernel,
        out_shape=(sds((2, 64, 2048), F32), sds((rows, cols), BF)),
        in_specs=[VMEM] * 2,
        out_specs=[VMEM] * 2,
        scratch_shapes=z_room() + xy_room(rows, cols) + sems(32, 1),
        compiler_params=pltpu.CompilerParams(
            collective_id=cid, has_side_effects=True, vmem_limit_bytes=40 * MB
        ),
        name="sums",
    )(part, grads)


def sums2_kernel(part, grads, more, out, mine, mine2, *rest):
    zr, xr, yr, (send_sem, recv_sem, here_sem) = rest[:4], rest[4:10], rest[10:16], rest[16:]
    p = Place()
    w = Wire(send_sem, recv_sem, here_sem)
    meet(p.peers(("z", "sib", "plane")))
    run(
        reduce_z(w, p, part, zr, out),
        reduce_xy(w, p, grads, xr, mine),
        reduce_xy(w, p, more, yr, mine2),
    )
    w.finish()


def sums2(part, grads, more, cid):
    sds = jax.ShapeDtypeStruct
    (_, _, r1, c1), (_, _, r2, c2) = grads.shape, more.shape
    return pl.pallas_call(
        sums2_kernel,
        out_shape=(sds((2, 64, 2048), F32), sds((r1, c1), BF), sds((r2, c2), BF)),
        in_specs=[VMEM] * 3,
        out_specs=[VMEM] * 3,
        scratch_shapes=z_room() + xy_room(r1, c1) + xy_room(r2, c2) + sems(48, 1),
        compiler_params=pltpu.CompilerParams(
            collective_id=cid, has_side_effects=True, vmem_limit_bytes=40 * MB
        ),
        name="sums2",
    )(part, grads, more)


def attend_back_kernel(
    q, kv, kv_far, d_tok, dz_own, mixed_part, gu_part, dq, dkv, dz, mixed, gu_mine,
    do, acc, acc_far, out_far, in_far, *rest
):
    zr, xr, (send_sem, recv_sem, here_sem) = rest[:4], rest[4:10], rest[10:]
    p = Place()
    w = Wire(send_sem, recv_sem, here_sem)
    dz[p.t] = dz_own[0]
    dz[15 - p.t] = dz_own[1]
    meet(p.peers(("tp", "plane")))
    pair = p.at(yl=1 - p.yl)
    spread = []
    for dz_ in (2, 1, 3, 0):
        for dc in (0, 1):
            z, core = p.up(dz_), lax.rem(p.core + dc, 2)
            cols = pl.ds(pl.multiple_of((2 * z + core) * 256, 256), 256)
            for k in (0, 1):
                if dz_ or dc:
                    dst = do.at[p.t if k == 0 else 15 - p.t]
                    spread.append(w.send(d_tok.at[k, :, cols], dst, p.at(z=z, core=core)))
                else:
                    do[p.t if k == 0 else 15 - p.t] = d_tok[k, :, cols]

    def block(t, k):
        return dz.at[t if k == 0 else 15 - t]

    tasks = [
        reduce_xy(w, p, gu_part, xr, gu_mine),
        gather_z(w, p, lambda k: block(p.t, k), block),
        reduce_z(w, p, mixed_part, zr, mixed),
    ]
    advance(tasks)
    acc[...] = jnp.zeros_like(acc)
    acc_far[...] = jnp.zeros_like(acc_far)
    for copy in spread:
        copy.wait_recv()
    back = []
    for j in range(7, -1, -1):
        at = pl.ds(j * 128, 128)
        keys = pl.ds(0, j * 128 + 128)
        tri, seen = edges(p, j)
        qj = both(q, at)
        dj = jnp.concatenate(
            [do[2 * j : 2 * j + 2, :, n * 128 : n * 128 + 128].reshape(128, 128) for n in (0, 1)], 0
        )
        near = weights_of(qj, kv[keys, 0:128], j, tri)
        far = weights_of(qj, kv_far[keys, 0:128], j, seen)
        scale = 1.0 / (jnp.sum(near, -1, keepdims=True) + jnp.sum(far, -1, keepdims=True))
        near = near * scale
        far = far * scale
        d_near = dot_t(dj, kv[keys, 128:256])
        d_far = dot_t(dj, kv_far[keys, 128:256])
        delta = jnp.sum(near * d_near, -1, keepdims=True) + jnp.sum(
            far * d_far, -1, keepdims=True
        )
        s_near = (near * (d_near - delta)).astype(BF)
        s_far = (far * (d_far - delta)).astype(BF)
        grad = jnp.dot(s_near, kv[keys, 0:128], preferred_element_type=F32)
        grad += jnp.dot(s_far, kv_far[keys, 0:128], preferred_element_type=F32)
        grad = (grad * 128**-0.5).astype(BF)
        dq[at, 0:128] = grad[:128]
        dq[at, 128:256] = grad[128:]
        acc[keys, 0:128] += t_dot(s_near, qj)
        acc_far[keys, 0:128] += t_dot(s_far, qj)
        acc[keys, 128:256] += t_dot(near.astype(BF), dj)
        acc_far[keys, 128:256] += t_dot(far.astype(BF), dj)
        out_far[at, 0:128] = (acc_far[at, 0:128] * 128**-0.5).astype(BF)
        out_far[at, 128:256] = acc_far[at, 128:256].astype(BF)
        back.append((at, w.send(out_far.at[at], in_far.at[at], pair)))
        advance(tasks)
    run(*tasks)
    for at, copy in back:
        copy.wait_recv()
        dkv[at, 0:128] = add(acc[at, 0:128] * 128**-0.5, in_far[at, 0:128]).astype(BF)
        dkv[at, 128:256] = add(acc[at, 128:256], in_far[at, 128:256]).astype(BF)
    w.finish()


def attend_back(q, kv, kv_far, d_tok, dz_own, mixed_part, gu_part):
    sds = jax.ShapeDtypeStruct
    return pl.pallas_call(
        attend_back_kernel,
        out_shape=(
            sds((1024, 256), BF),
            sds((1024, 256), BF),
            sds((16, 64, 2048), BF),
            sds((2, 64, 2048), F32),
            sds((128, 1536), BF),
        ),
        in_specs=[VMEM] * 7,
        out_specs=[VMEM] * 5,
        scratch_shapes=[
            pltpu.VMEM((16, 64, 256), BF),
            pltpu.VMEM((1024, 256), F32),
            pltpu.VMEM((1024, 256), F32),
            pltpu.VMEM((1024, 256), BF),
            pltpu.VMEM((1024, 256), BF),
        ]
        + z_room()
        + xy_room(128, 1536)
        + sems(80, 1),
        compiler_params=pltpu.CompilerParams(
            collective_id=4, has_side_effects=True, vmem_limit_bytes=58 * MB
        ),
        name="attend_back",
    )(q, kv, kv_far, d_tok, dz_own, mixed_part, gu_part)


def last_kernel(cols, rows, vec, cols_out, rows_out, vec_out, ra, rb, rc, send_sem, recv_sem, here_sem):
    p = Place()
    w = Wire(send_sem, recv_sem, here_sem)
    meet(p.peers(("tp", "plane", "swap")))
    stay = p.yl == p.core
    cols_out[p.t] = cols[p.t]
    ra[p.t] = vec[...]
    moves = []
    for dz in range(4):
        for dc in range(2):
            if dz or dc:
                z, core = p.up(dz), lax.rem(p.core + dc, 2)
                peer = p.at(z=z, core=core)
                moves.append(w.send(vec, ra.at[p.t], peer))
                moves.append(w.send(cols.at[2 * z + core], cols_out.at[p.t], peer))
    n = w.n
    swap = pltpu.make_async_remote_copy(
        src_ref=rows,
        dst_ref=rows_out,
        send_sem=send_sem.at[n],
        recv_sem=recv_sem.at[n],
        device_id=p.at(yl=1 - p.yl, core=1 - p.core),
        device_id_type=MESH,
    )
    w.n += 1

    @pl.when(jnp.logical_not(stay))
    def _():
        swap.start()

    @pl.when(stay)
    def _():
        rows_out[...] = rows[...]

    for copy in moves[0::2]:
        copy.wait_recv()
    rb[p.x] = sum((ra[i] for i in range(1, 8)), ra[0])
    xs = [w.send(rb.at[p.x], rb.at[p.x], p.at(x=p.east(d))) for d in (1, 2, 3)]
    for copy in xs:
        copy.wait_recv()
    rc[p.y] = sum((rb[i] for i in range(1, 4)), rb[0])
    ys = [w.send(rc.at[p.y], rc.at[p.y], p.north(d)) for d in (1, 2, 3)]
    for copy in ys:
        copy.wait_recv()
    vec_out[...] = sum((rc[i] for i in range(1, 4)), rc[0])
    for copy in moves[1::2]:
        copy.wait_recv()

    @pl.when(jnp.logical_not(stay))
    def _():
        swap.wait()

    w.finish()


def last(cols, rows, vec):
    sds = jax.ShapeDtypeStruct
    n = vec.shape
    return pl.pallas_call(
        last_kernel,
        out_shape=(sds(cols.shape, BF), sds(rows.shape, BF), sds(n, F32)),
        in_specs=[VMEM] * 3,
        out_specs=[VMEM] * 3,
        scratch_shapes=[
            pltpu.VMEM((8,) + n, F32),
            pltpu.VMEM((4,) + n, F32),
            pltpu.VMEM((4,) + n, F32),
        ]
        + sems(32, 1),
        compiler_params=pltpu.CompilerParams(
            collective_id=6, has_side_effects=True, vmem_limit_bytes=32 * MB
        ),
        name="last",
    )(cols, rows, vec)


def rotary(positions, width):
    half = width // 2
    freq = THETA ** (-2.0 * jnp.arange(half, dtype=F32) / width)
    angle = positions.astype(F32)[:, None] * freq[None, :]
    cosine = jnp.concatenate([jnp.cos(angle), jnp.cos(angle)], 1)
    sine = jnp.concatenate([-jnp.sin(angle), jnp.sin(angle)], 1)
    return (cosine, sine)


def turn_back(grads, cosine, sine):
    moved = grads * sine
    half = grads.shape[-1] // 2
    return grads * cosine + jnp.concatenate([moved[..., half:], moved[..., :half]], -1)


def row_norm(vals):
    scale = lax.rsqrt(jnp.mean(vals * vals, -1, keepdims=True) + EPS)
    return (vals * scale, scale)


def norm_back(grad_unit, unit, scale):
    return scale * (grad_unit - unit * jnp.mean(grad_unit * unit, -1, keepdims=True))


def mm(left, right):
    return jnp.dot(left, right, preferred_element_type=F32)


def mm_t(left, right):
    return lax.dot_general(left, right, (((1,), (1,)), ((), ())), preferred_element_type=F32)


def t_mm(left, right):
    return lax.dot_general(left, right, (((0,), (0,)), ((), ())), preferred_element_type=F32)


def gather(val, axes):
    return lax.all_gather(val, axes, axis=0, tiled=True)


def scatter(val, axes):
    return lax.psum_scatter(val, axes, scatter_dimension=0, tiled=True)


def to_sorted(val):
    a = val.reshape(8, 2, 64, -1)
    return jnp.concatenate([a[:, 0], a[::-1, 1]], 0).reshape(1024, -1)


def to_owner(val):
    a = val.reshape(16, 64, -1)
    return jnp.stack([a[:8], a[:7:-1]], 1).reshape(1024, -1)


def gather_tp(val):
    return to_sorted(gather(val, TP))


def scatter_tp(val):
    return scatter(to_owner(val.astype(BF)), TP).astype(F32)


def shards(
    tokens,
    gain_in,
    query_weight,
    key_weight,
    value_weight,
    gain_query,
    gain_key,
    out_weight,
    gain_mid,
    gate_weight,
    up_weight,
    down_weight,
    cotangent,
):
    width = tokens.shape[4]
    n_z, n_yl, n_core = (lax.axis_size(a) for a in ("z", "yl", "core"))
    n_tp = n_z * n_core
    n_fs = lax.axis_size("x") * lax.axis_size("yh")
    rows = 128
    head = 128
    qc, kc, fc = 256, 128, 768
    factor = head ** (-0.5)
    t = lax.axis_index(TP)
    yl = lax.axis_index("yl")

    def positions(lane):
        idx = jnp.arange(1024, dtype=jnp.int32)
        tile, spot = idx // 128, idx % 128
        place = jnp.where(tile < 4, 2 * tile + lane, 2 * tile + 1 - lane)
        return place * 128 + spot

    query_pos = positions(yl)
    key_pos = jnp.concatenate([query_pos, positions(1 - yl)])
    allowed = key_pos[None, :] <= query_pos[:, None]
    cosine, sine = rotary(query_pos, head)

    cut = lambda w, n: lax.dynamic_slice_in_dim(w, t * n, n, 1)
    gu_own = jnp.concatenate([cut(gate_weight, fc), cut(up_weight, fc)], 1)
    d_s = down_weight.shape[0] // n_tp
    rows_d = lax.ppermute(
        lax.dynamic_slice_in_dim(down_weight, t * d_s, d_s, 0),
        TP + FS,
        [(a * n_fs + b, b * n_fs + a) for a in range(n_tp) for b in range(n_fs)],
    )

    tok = tokens.reshape(2, 64, width)
    x = tokens.reshape(rows, width).astype(F32)
    unit_in, scale_in = row_norm(x)
    grad_l = cotangent.reshape(rows, width)
    h, w_qkv, query_b, kv, raw = front(
        tok,
        gain_in.reshape(1, -1),
        jnp.concatenate([cut(query_weight, qc), cut(key_weight, kc), cut(value_weight, kc)], 1),
        cosine,
        sine,
        gain_query.reshape(1, -1),
        gain_key.reshape(1, -1),
    )
    h = h.reshape(1024, width)
    attended, o_tok, kv_far, g, w_out, w_gu = attend(query_b, kv, cotangent.reshape(2, 64, width),
        lax.dynamic_slice_in_dim(out_weight, lax.axis_index("core") * 128, 128, 0),
        gu_own,
    )
    w_gu = w_gu.reshape(2048, 2 * fc)
    attended = attended.reshape(1024, qc)
    g = g.reshape(1024, width)
    w_out = w_out.reshape(2048, 2048)
    unit_q, scale_q = row_norm(raw[:, :qc].reshape(-1, 2, head))
    unit_k, scale_k = row_norm(raw[:, qc : qc + kc].reshape(-1, 1, head))
    y_mid = x + mm(o_tok.reshape(rows, width), w_out)
    unit_mid, scale_mid = row_norm(y_mid)
    h2, w_down = mid((unit_mid * gain_mid).astype(BF).reshape(2, 64, width), rows_d)
    h2, w_down = h2.reshape(1024, width), w_down.reshape(768, width)
    gu = mm(h2, w_gu)
    gate, upper = gu[:, :fc], gu[:, fc:]
    sig = jax.nn.sigmoid(gate)
    silu_gate = gate * sig
    act_b = (silu_gate * upper).astype(BF)
    mixed_part = mm(act_b, w_down).astype(BF).reshape(16, 64, width)
    grad_act = mm_t(g, w_down)
    dgate_b = (grad_act * upper * sig * (1.0 + gate * (1.0 - sig))).astype(BF)
    dup_b = (grad_act * silu_gate).astype(BF)
    dgu = jnp.concatenate([dgate_b, dup_b], 1)

    def rows_to_owners(part):
        cols = part.shape[1]
        part = part.astype(BF).reshape(2, 4, 2, -1, cols)
        return part.transpose(1, 2, 0, 3, 4).reshape(4, 4, -1, cols)

    def cols_to_owners(part):
        cols = part.shape[1]
        part = part.astype(BF).reshape(n_z, n_yl, n_core, 4, 2, 16, cols)
        return part.transpose(3, 4, 1, 0, 2, 5, 6).reshape(4, 4, 128, cols)

    grad_h2, down_mine = sums(
        mm_t(dgu, w_gu).astype(BF).reshape(16, 64, width), rows_to_owners(t_mm(act_b, g)), 3
    )
    grad_h2 = grad_h2.reshape(rows, width)
    term_mid = jnp.sum(grad_h2 * unit_mid, 0)
    grad_mid = grad_l.astype(F32) + norm_back(grad_h2 * gain_mid, unit_mid, scale_mid)
    dz_own = grad_mid.astype(BF)
    d_tok = mm_t(dz_own, w_out).astype(BF)
    grad_query, own, dz, mlp_out, gu_mine = attend_back(
        query_b,
        kv,
        kv_far,
        d_tok.reshape(2, 64, width),
        dz_own.reshape(2, 64, width),
        mixed_part,
        cols_to_owners(t_mm(h2, dgu)),
    )
    dz = dz.reshape(1024, width)
    mixed = (y_mid + mlp_out.reshape(rows, width)).astype(BF)
    dv_b = own[:, head:]
    cos3, sin3 = cosine[:, None, :], sine[:, None, :]
    grad_q_norm = turn_back(grad_query.astype(F32).reshape(-1, 2, head), cos3, sin3)
    grad_k_norm = turn_back(own[:, :head].astype(F32).reshape(-1, 1, head), cos3, sin3)
    term_query = jnp.sum(grad_q_norm * unit_q, (0, 1))
    term_key = jnp.sum(grad_k_norm * unit_k, (0, 1))
    dq_b = norm_back(grad_q_norm * gain_query, unit_q, scale_q).reshape(-1, qc).astype(BF)
    dk_b = norm_back(grad_k_norm * gain_key, unit_k, scale_k).reshape(-1, kc).astype(BF)
    dqkv = jnp.concatenate([dq_b, dk_b, dv_b], 1)
    grad_h, qkv_mine, out_mine = sums2(
        mm_t(dqkv, w_qkv).astype(BF).reshape(16, 64, width),
        cols_to_owners(t_mm(h, dqkv)),
        rows_to_owners(t_mm(attended, dz)),
        5,
    )
    grad_h = grad_h.reshape(rows, width)
    term_in = jnp.sum(grad_h * unit_in, 0)
    tokens_grad = (grad_mid + norm_back(grad_h * gain_in, unit_in, scale_in)).astype(BF)

    mine = jnp.concatenate([gu_mine, qkv_mine], 1).reshape(n_tp, 16, -1)
    late = jnp.concatenate([down_mine, out_mine], 0)
    terms = jnp.concatenate([term_in, term_mid, term_query, term_key, jnp.zeros((768,), F32)])
    mine, late, terms = last(mine, late, terms.reshape(40, 128))
    mine = mine.transpose(1, 0, 2).astype(F32)

    def take(at, n):
        return mine[:, :, at : at + n].reshape(-1, n_tp * n)

    grad_gate_w, grad_up_w = take(0, fc), take(fc, fc)
    grad_q_w, grad_k_w, grad_v_w = (
        take(2 * fc, qc),
        take(2 * fc + qc, kc),
        take(2 * fc + qc + kc, kc),
    )
    late = late.astype(F32)
    grad_down, grad_out = late[:48], late[48:]
    terms = terms.reshape(-1)
    sum_in, sum_mid = terms[:width], terms[width : 2 * width]
    sum_query, sum_key = terms[2 * width : 2 * width + head], terms[2 * width + head : 2 * width + 2 * head]
    return (
        mixed.reshape(tokens.shape),
        tokens_grad.reshape(tokens.shape),
        sum_in,
        grad_q_w,
        grad_k_w,
        grad_v_w,
        sum_query,
        sum_key,
        grad_out,
        sum_mid,
        grad_gate_w,
        grad_up_w,
        grad_down,
    )


def solution(mesh):
    fine = Mesh(mesh.devices.reshape(4, 2, 2, 4, 2), ALL)
    ctx, fsdp = ("z", "yl", "core"), FS
    act = P(fsdp, None, ctx, None, None)
    weight = P(fsdp, None)
    grad = P(ctx + fsdp, None)
    placed = (
        act, P(), weight, weight, weight, P(), P(), weight, P(), weight, weight, weight, act,
    )
    return jax.shard_map(
        shards,
        mesh=fine,
        in_specs=placed,
        out_specs=(act, act, P(), grad, grad, grad, P(), P(), grad, P(), grad, grad, grad),
        check_vma=False,
    )
```

```python
import functools

import jax
import jax.numpy as jnp
from jax import lax
from jax.experimental import pallas as pl
from jax.experimental.pallas import tpu as pltpu
from jax.sharding import Mesh, PartitionSpec as P

EPS = 1e-06
THETA = 1000000.0
BF = jnp.bfloat16
F32 = jnp.float32
TP = ("z", "core")
FS = ("x", "yh")
DP = ("yl", "x", "yh")
ALL = ("z", "yl", "core", "x", "yh")
MESH = pl.DeviceIdType.MESH
VMEM = pl.BlockSpec(memory_space=pltpu.VMEM)
HBM = pl.BlockSpec(memory_space=pl.ANY)
MB = 2**20
LOG2E = 1.4426950408889634


class Place:
    def __init__(self):
        self.z, self.yl, self.core, self.x, self.yh = (lax.axis_index(a) for a in ALL)
        self.t = 2 * self.z + self.core
        self.shard = 2 * self.x + self.yh
        self.y = 2 * self.yh + self.yl

    def at(self, z=None, yl=None, core=None, x=None, yh=None):
        here = (self.z, self.yl, self.core, self.x, self.yh)
        return tuple(h if n is None else n for h, n in zip(here, (z, yl, core, x, yh)))

    def up(self, n):
        return lax.rem(self.z + n, 4)

    def east(self, n):
        return lax.rem(self.x + n, 4)

    def north(self, n):
        y = lax.rem(self.y + n, 4)
        return self.at(yh=y // 2, yl=lax.rem(y, 2))

    def peers(self, which):
        table = {
            "z": [self.at(z=self.up(1)), self.at(z=self.up(3))],
            "sib": [self.at(core=1 - self.core)],
            "x": [self.at(x=self.east(1)), self.at(x=self.east(3))],
            "cross": [self.at(yl=1 - self.yl, yh=1 - self.yh)],
            "pair": [self.at(yl=1 - self.yl)],
            "plane": [self.at(x=self.east(d)) for d in (1, 2, 3)]
            + [self.north(d) for d in (1, 2, 3)],
            "swap": [self.at(yl=1 - self.yl, core=1 - self.core)],
            "tp": [
                self.at(z=self.up(dz), core=lax.rem(self.core + dc, 2))
                for dz in range(4)
                for dc in range(2)
                if dz or dc
            ],
        }
        return [p for name in which for p in table[name]]


class Wire:
    def __init__(self, send_sem, recv_sem, here_sem):
        self.send_sem, self.recv_sem, self.here_sem = send_sem, recv_sem, here_sem
        self.n = self.m = 0
        self.sent = []

    def send(self, src, dst, peer):
        copy = pltpu.make_async_remote_copy(
            src_ref=src,
            dst_ref=dst,
            send_sem=self.send_sem.at[self.n],
            recv_sem=self.recv_sem.at[self.n],
            device_id=peer,
            device_id_type=MESH,
        )
        self.n += 1
        assert self.n <= self.send_sem.shape[0]
        copy.start()
        self.sent.append(copy)
        return copy

    def here(self, src, dst):
        copy = pltpu.make_async_copy(src, dst, self.here_sem.at[self.m])
        self.m += 1
        assert self.m <= self.here_sem.shape[0]
        copy.start()
        return copy

    def settle(self, copies):
        for copy in copies:
            copy.wait_send()
        self.sent = [one for one in self.sent if all(one is not copy for copy in copies)]

    def finish(self):
        for copy in self.sent:
            copy.wait_send()


def sems(n, m):
    return [
        pltpu.SemaphoreType.DMA((n,)),
        pltpu.SemaphoreType.DMA((n,)),
        pltpu.SemaphoreType.DMA((m,)),
    ]


def meet(peers):
    barrier = pltpu.get_barrier_semaphore()
    for peer in peers:
        pl.semaphore_signal(barrier, inc=1, device_id=peer, device_id_type=MESH)
    pl.semaphore_wait(barrier, len(peers))


def run(*tasks):
    tasks = list(tasks)
    while tasks:
        advance(tasks)


def advance(tasks):
    for task in list(tasks):
        try:
            next(task)
        except StopIteration:
            tasks.remove(task)


def gather_z(w, p, own, dst):
    up, down, sib = p.at(z=p.up(1)), p.at(z=p.up(3)), p.at(core=1 - p.core)
    before, after, far = (2 * p.up(n) + p.core for n in (3, 1, 2))
    u0 = w.send(own(0), dst(p.t, 0), up)
    d1 = w.send(own(1), dst(p.t, 1), down)
    u1 = w.send(own(1), dst(p.t, 1), up)
    d0 = w.send(own(0), dst(p.t, 0), down)
    s = [w.send(own(k), dst(p.t, k), sib) for k in (0, 1)]

    def on(t, k):
        s.append(w.send(dst(t, k), dst(t, k), sib))

    yield
    u0.wait_recv()
    f0 = w.send(dst(before, 0), dst(before, 0), up)
    on(before, 0)
    d1.wait_recv()
    f1 = w.send(dst(after, 1), dst(after, 1), down)
    on(after, 1)
    yield
    u1.wait_recv()
    on(before, 1)
    d0.wait_recv()
    on(after, 0)
    yield
    f0.wait_recv()
    on(far, 0)
    f1.wait_recv()
    on(far, 1)
    yield
    for copy in s:
        copy.wait_recv()
    w.settle([u0, d1, u1, d0, f0, f1] + s)


def gather_xy(w, p, dst, n, ready=None):
    east, west = p.at(x=p.east(1)), p.at(x=p.east(3))
    cross, pair = p.at(yl=1 - p.yl, yh=1 - p.yh), p.at(yl=1 - p.yl)
    half = n // 2
    me = p.shard
    west_s, east_s, far_s = (2 * p.east(k) + p.yh for k in (3, 1, 2))
    mine = p.yl * half
    other = half - mine
    flip = 1 - 2 * p.yh

    def one(s, at, peer):
        return w.send(dst(s, at, half), dst(s, at, half), peer)

    def along(s):
        return one(s + flip, other, pair)

    e0 = one(me, mine, east)
    w0 = one(me, mine, west)
    c0 = one(me, mine, cross)
    w1 = one(me, other, west)
    yield
    e0.wait_recv()
    fe = one(west_s, mine, east)
    c1 = one(west_s, mine, cross)
    e1 = one(me, other, east)
    w0.wait_recv()
    c2 = one(east_s, mine, cross)
    yield
    c0.wait_recv()
    a0 = along(me)
    fe.wait_recv()
    c3 = one(far_s, mine, cross)
    w1.wait_recv()
    fw = one(east_s, other, west)
    if ready:
        ready(east_s)
    yield
    c1.wait_recv()
    a1 = along(west_s)
    e1.wait_recv()
    if ready:
        ready(west_s)
    c2.wait_recv()
    a2 = along(east_s)
    yield
    fw.wait_recv()
    if ready:
        ready(far_s)
    c3.wait_recv()
    a3 = along(far_s)
    yield
    for s, a in ((me, a0), (west_s, a1), (east_s, a2), (far_s, a3)):
        a.wait_recv()
        if ready:
            ready(s + flip)


def norm_rope(raw, gain, cosine, sine):
    unit = raw * lax.rsqrt(jnp.mean(raw * raw, -1, keepdims=True) + EPS)
    vals = unit * gain
    return vals * cosine + pltpu.roll(vals, 64, 1) * sine


SCALE = 128**-0.5 * LOG2E


def dot_t(a, b):
    return lax.dot_general(a, b, (((1,), (1,)), ((), ())), preferred_element_type=F32)


def t_dot(a, b):
    return lax.dot_general(a, b, (((0,), (0,)), ((), ())), preferred_element_type=F32)


def both(ref, at):
    return jnp.concatenate([ref[at, 0:128], ref[at, 128:256]], 0)


def weights_of(q, k, j, edge):
    s = jnp.exp2(dot_t(q, k) * SCALE)
    last = jnp.where(edge, s[:, j * 128 :], 0.0)
    return last if j == 0 else jnp.concatenate([s[:, : j * 128], last], 1)


def edges(p, j):
    row = lax.broadcasted_iota(jnp.int32, (256, 128), 0) % 128
    col = lax.broadcasted_iota(jnp.int32, (256, 128), 1)
    seen = (p.yl if j < 4 else 1 - p.yl) * 128
    return col <= row, col < seen


def shard_rows(ref, n):
    return lambda s, at, m: ref.at[pl.ds(pl.multiple_of(s * n + at, 16), m)]


def ahead_kernel(
    tok, gain, w_own, cosine, sine, gq, gk, cot, wo, gate_own, gain_mid,
    h_out, qkv_out, q, kv, kv_far, raw, o, g_out, out_out, gate_out, y1, h2,
    h, w_qkv, g, w_out, w_gate, o_tok, send_sem, recv_sem, here_sem
):
    p = Place()
    w = Wire(send_sem, recv_sem, here_sem)
    w_qkv[pl.ds(pl.multiple_of(p.shard * 256, 256), 256)] = w_own[...]
    for k in (0, 1):
        x = tok[k].astype(F32)
        unit = x * lax.rsqrt(jnp.mean(x * x, -1, keepdims=True) + EPS)
        h[p.t if k == 0 else 15 - p.t] = (unit * gain[...]).astype(BF)
    meet(p.peers(("tp", "x", "cross", "pair")))
    pair, sib = p.at(yl=1 - p.yl), p.at(core=1 - p.core)

    def block_of(ref):
        return lambda t, k: ref.at[t if k == 0 else 15 - t]

    def part_out(s, at, n):
        return w_out.at[s, p.core, pl.ds(pl.multiple_of(at, 64), n)]

    twin = []

    def ready(s):
        twin.append(w.send(w_out.at[s, p.core], w_out.at[s, p.core], sib))

    at_h, at_g = block_of(h), block_of(g)
    task_h = [gather_z(w, p, lambda k: at_h(p.t, k), at_h)]
    task_qkv = [gather_xy(w, p, shard_rows(w_qkv, 256), 256)]
    advance(task_qkv)
    advance(task_h)
    w_out[p.shard, p.core] = wo[...]
    g[p.t] = cot[0]
    g[15 - p.t] = cot[1]
    w_gate[pl.ds(pl.multiple_of(p.shard * 256, 256), 256)] = gate_own[...]
    task_out = [gather_xy(w, p, part_out, 128, ready)]
    task_gate = [gather_xy(w, p, shard_rows(w_gate, 256), 256)]
    task_g = [gather_z(w, p, lambda k: at_g(p.t, k), at_g)]
    ready(p.shard)
    advance(task_qkv)
    advance(task_h)
    advance(task_qkv)
    advance(task_out)
    advance(task_qkv)
    advance(task_h)
    advance(task_qkv)
    advance(task_qkv)
    advance(task_out)
    advance(task_h)
    advance(task_gate)
    advance(task_g)
    run(task_h[0])
    kept = [w.here(h, h_out), w.here(w_qkv, qkv_out)]
    swaps = []
    for j in range(4):
        at = pl.ds(j * 256, 256)
        out = jnp.dot(
            h[4 * j : 4 * j + 4].reshape(256, 2048), w_qkv[...], preferred_element_type=F32
        )
        cos, sin = cosine[at], sine[at]
        kv[at, 0:128] = norm_rope(out[:, 256:384], gk[...], cos, sin).astype(BF)
        kv[at, 128:256] = out[:, 384:].astype(BF)
        swaps.append(w.send(kv.at[at], kv_far.at[at], pair))
        for n in (0, 1):
            cols = slice(n * 128, n * 128 + 128)
            q[at, cols] = norm_rope(out[:, cols], gq[...], cos, sin).astype(BF)
        raw[at] = out[:, :384]
        if j in (1, 3):
            advance(task_out)
        if j == 2:
            advance(task_gate)
            advance(task_g)
    for j in range(8):
        at = pl.ds(j * 128, 128)
        keys = pl.ds(0, j * 128 + 128)
        if j % 2 == 0:
            swaps[j // 2].wait_recv()
        tri, seen = edges(p, j)
        qj = both(q, at)
        near = weights_of(qj, kv[keys, 0:128], j, tri)
        far = weights_of(qj, kv_far[keys, 0:128], j, seen)
        total = jnp.sum(near, -1, keepdims=True) + jnp.sum(far, -1, keepdims=True)
        out = jnp.dot(near.astype(BF), kv[keys, 128:256], preferred_element_type=F32)
        out += jnp.dot(far.astype(BF), kv_far[keys, 128:256], preferred_element_type=F32)
        out = (out / total).astype(BF)
        for n in (0, 1):
            o[2 * j : 2 * j + 2, :, n * 128 : n * 128 + 128] = out[
                n * 128 : n * 128 + 128
            ].reshape(2, 64, 128)
        if j == 1:
            advance(task_g)
        if j == 4:
            advance(task_out)
            advance(task_g)
        if j == 6:
            advance(task_gate)
    spread = []
    for dz in (2, 1, 3, 0):
        for dc in range(2):
            z, core = p.up(dz), lax.rem(p.core + dc, 2)
            t = 2 * z + core
            for k in (0, 1):
                src = o.at[t if k == 0 else 15 - t]
                if dz or dc:
                    spread.append(w.send(src, o_tok.at[p.t, k], p.at(z=z, core=core)))
                else:
                    o_tok[p.t, k] = o[t if k == 0 else 15 - t]
    run(*task_g)
    kept.append(w.here(g, g_out))
    advance(task_gate)
    run(*task_out)
    advance(task_gate)
    for copy in twin:
        copy.wait_recv()
    kept.append(w.here(w_out, out_out))
    for copy in spread:
        copy.wait_recv()
    for n in range(4):
        cols = slice(n * 512, n * 512 + 512)
        for k in (0, 1):
            y1[k, :, cols] = tok[k, :, cols].astype(F32)
        for t in range(8):
            part = jnp.dot(
                o_tok[t].reshape(128, 256),
                w_out[t, :, :, cols].reshape(256, 512),
                preferred_element_type=F32,
            )
            for k in (0, 1):
                y1[k, :, cols] += part[k * 64 : k * 64 + 64]
    for k in (0, 1):
        y = y1[k]
        unit = y * lax.rsqrt(jnp.mean(y * y, -1, keepdims=True) + EPS)
        h2[k] = (unit * gain_mid[...]).astype(BF)
    run(*task_gate)
    kept.append(w.here(w_gate, gate_out))
    w.finish()
    for copy in kept:
        copy.wait()


def ahead(*args):
    sds = jax.ShapeDtypeStruct
    return pl.pallas_call(
        ahead_kernel,
        out_shape=(
            sds((16, 64, 2048), BF),
            sds((2048, 512), BF),
            sds((1024, 256), BF),
            sds((1024, 256), BF),
            sds((1024, 256), BF),
            sds((1024, 384), F32),
            sds((16, 64, 256), BF),
            sds((16, 64, 2048), BF),
            sds((8, 2, 128, 2048), BF),
            sds((2048, 768), BF),
            sds((2, 64, 2048), F32),
            sds((2, 64, 2048), BF),
        ),
        in_specs=[VMEM] * 11,
        out_specs=[HBM, HBM, VMEM, VMEM, VMEM, VMEM, VMEM, HBM, HBM, HBM, VMEM, VMEM],
        scratch_shapes=[
            pltpu.VMEM((16, 64, 2048), BF),
            pltpu.VMEM((2048, 512), BF),
            pltpu.VMEM((16, 64, 2048), BF),
            pltpu.VMEM((8, 2, 128, 2048), BF),
            pltpu.VMEM((2048, 768), BF),
            pltpu.VMEM((8, 2, 64, 256), BF),
        ]
        + sems(128, 8),
        compiler_params=pltpu.CompilerParams(
            collective_id=0, has_side_effects=True, vmem_limit_bytes=56 * MB
        ),
        name="ahead",
    )(*args)


def add(*vals):
    total = vals[0].astype(F32)
    for val in vals[1:]:
        total = total + val.astype(F32)
    return total


def z_room():
    return [
        pltpu.VMEM((4, 2, 64, 2048), BF),
        pltpu.VMEM((4, 2, 64, 2048), BF),
        pltpu.VMEM((2, 64, 2048), BF),
        pltpu.VMEM((2, 2, 64, 2048), BF),
    ]


def reduce_z(w, p, part, room, out):
    near, mine, relay, last = room
    up, down, sib = p.at(z=p.up(1)), p.at(z=p.up(3)), p.at(core=1 - p.core)

    def block(n, core, k):
        t = 2 * p.up(n) + core
        return t if k == 0 else 15 - t

    first = {}

    def give(n):
        for k in (0, 1):
            first[n, k] = w.send(part.at[block(n, 1 - p.core, k)], near.at[n, k], sib)

    def fold(n, k):
        first[n, k].wait_recv()
        mine[n, k] = add(part[block(n, p.core, k)], near[n, k]).astype(BF)

    give(2)
    yield
    give(1)
    fold(2, 0)
    e0 = w.send(mine.at[2, 0], relay.at[0], up)
    fold(2, 1)
    e1 = w.send(mine.at[2, 1], relay.at[1], down)
    yield
    give(3)
    fold(1, 1)
    a1 = w.send(mine.at[1, 1], last.at[0, 1], up)
    fold(1, 0)
    yield
    give(0)
    fold(3, 0)
    b0 = w.send(mine.at[3, 0], last.at[1, 0], down)
    fold(3, 1)
    yield
    e0.wait_recv()
    mine[1, 0] = add(mine[1, 0], relay[0]).astype(BF)
    a0 = w.send(mine.at[1, 0], last.at[0, 0], up)
    e1.wait_recv()
    mine[3, 1] = add(mine[3, 1], relay[1]).astype(BF)
    b1 = w.send(mine.at[3, 1], last.at[1, 1], down)
    fold(0, 0)
    fold(0, 1)
    yield
    for k, (a, b) in enumerate(((a0, b0), (a1, b1))):
        a.wait_recv()
        b.wait_recv()
        out[k] = add(mine[0, k], last[0, k], last[1, k])


def xy_room(rows, cols):
    half = cols // 2
    return [
        pltpu.VMEM((3, 4, rows, half), BF),
        pltpu.VMEM((4, rows, half), BF),
        pltpu.VMEM((3, rows, half), BF),
    ] * 2


def reduce_xy(w, p, part, room, out):
    ra, sa, fa, rb, sb, fb = room
    half = part.shape[3] // 2
    left, right = pl.ds(0, half), pl.ds(half, half)
    spans = (1, 2, 3)
    easts = [p.at(x=p.east(d)) for d in spans]
    norths = [p.north(d) for d in spans]
    ca = [w.send(part.at[p.east(d), :, :, left], ra.at[d - 1], easts[d - 1]) for d in spans]
    cb = [
        w.send(part.at[:, lax.rem(p.y + d, 4), :, right], rb.at[d - 1], norths[d - 1])
        for d in spans
    ]
    yield
    for copy in ca:
        copy.wait_recv()

    @pl.loop(0, 4)
    def _(y):
        sa[y] = add(part[p.x, y, :, left], ra[0, y], ra[1, y], ra[2, y]).astype(BF)

    da = [w.send(sa.at[lax.rem(p.y + d, 4)], fa.at[d - 1], norths[d - 1]) for d in spans]
    yield
    for copy in cb:
        copy.wait_recv()

    @pl.loop(0, 4)
    def _(x):
        sb[x] = add(part[x, p.y, :, right], rb[0, x], rb[1, x], rb[2, x]).astype(BF)

    db = [w.send(sb.at[p.east(d)], fb.at[d - 1], easts[d - 1]) for d in spans]
    yield
    for copy in da:
        copy.wait_recv()
    out[:, left] = add(sa[p.y], fa[0], fa[1], fa[2]).astype(BF)
    yield
    for copy in db:
        copy.wait_recv()
    out[:, right] = add(sb[p.x], fb[0], fb[1], fb[2]).astype(BF)


def mlp_kernel(
    h2_own, up_own, down_own, gate_hbm, g_hbm, out_hbm, y1, cot, gain,
    h2_out, act_out, dgate_out, dup_out, mixed_out, grad_mid, dz, d_tok, term, down_mine,
    h2, w_gate, w_up, w_down, g, gate, upper, part, down_part, act, dgate, dup, mixed, *rest
):
    zr, xr, (send_sem, recv_sem, here_sem) = rest[:4], rest[4:10], rest[10:]
    p = Place()
    w = Wire(send_sem, recv_sem, here_sem)
    loads = [w.here(gate_hbm, w_gate), w.here(g_hbm, g)]
    h2[p.t] = h2_own[0]
    h2[15 - p.t] = h2_own[1]
    w_up[pl.ds(pl.multiple_of(p.shard * 256, 256), 256)] = up_own[...]
    w_down[pl.ds(pl.multiple_of(p.shard * 96, 96), 96)] = down_own[...]
    meet(p.peers(("z", "sib", "x", "plane", "cross")))

    def block(t, k):
        return h2.at[t if k == 0 else 15 - t]

    def rows_of(ref, zz):
        c = ref.shape[-1]
        return jnp.concatenate(
            [ref[pl.ds(2 * zz, 2)].reshape(128, c), ref[pl.ds(14 - 2 * zz, 2)].reshape(128, c)], 0
        )

    def put(ref, zz, val):
        c = ref.shape[-1]
        ref[pl.ds(2 * zz, 2)] = val[:128].reshape(2, 64, c)
        ref[pl.ds(14 - 2 * zz, 2)] = val[128:].reshape(2, 64, c)

    task_h = [gather_z(w, p, lambda k: block(p.t, k), block)]
    task_up = [gather_xy(w, p, shard_rows(w_up, 256), 256)]
    task_down = [gather_xy(w, p, shard_rows(w_down, 96), 96)]
    advance(task_up)
    advance(task_h)
    advance(task_up)
    advance(task_down)
    advance(task_h)
    advance(task_up)
    advance(task_up)
    advance(task_h)
    advance(task_down)
    advance(task_up)
    advance(task_h)
    run(*task_h)
    kept = [w.here(h2, h2_out)]
    loads[0].wait()

    @pl.loop(0, 4)
    def _(n):
        gate[n] = jnp.dot(rows_of(h2, n), w_gate[...], preferred_element_type=F32)

    run(*task_up)
    advance(task_down)

    @pl.loop(0, 4)
    def _(n):
        up_n = jnp.dot(rows_of(h2, n), w_up[...], preferred_element_type=F32)
        gate_n = gate[n]
        upper[n] = up_n
        put(act, n, (gate_n * jax.nn.sigmoid(gate_n) * up_n).astype(BF))

    kept.append(w.here(act, act_out))
    advance(task_down)
    loads[1].wait()
    kept[0].wait()
    loads.append(w.here(out_hbm.at[pl.ds(0, 16)], h2))

    @pl.loop(0, 6)
    def _(i):
        cols = pl.ds(pl.multiple_of(i * 128, 128), 128)
        left = act[:, :, cols].reshape(1024, 128)
        out = t_dot(left, g[...].reshape(1024, 2048)).astype(BF)
        for k in range(8):
            row = i * 8 + k
            piece = row // 3
            f = lax.rem(piece, 8)
            down_part[f // 2, 2 * lax.rem(f, 2) + piece // 8, pl.ds(pl.multiple_of(lax.rem(row, 3) * 16, 16), 16)] = out[
                k * 16 : k * 16 + 16
            ]

    run(*task_down)
    task_sum = [reduce_z(w, p, part, zr, grad_mid)]
    task_late = [reduce_xy(w, p, down_part, xr, down_mine)]
    advance(task_late)
    for n in (2, 1, 3, 0):
        zz = p.up(n)
        gate_n, up_n = gate[zz], upper[zz]
        sig = jax.nn.sigmoid(gate_n)
        da = dot_t(rows_of(g, zz), w_down[...])
        silu = gate_n * sig
        d_gate = (da * up_n * sig * (1.0 + gate_n * (1.0 - sig))).astype(BF)
        d_up = (da * silu).astype(BF)
        put(dgate, zz, d_gate)
        put(dup, zz, d_up)
        total = dot_t(d_gate, w_gate[...]) + dot_t(d_up, w_up[...])
        put(part, zz, total.astype(BF))
        advance(task_sum)
    loads.append(w.here(out_hbm.at[pl.ds(16, 16)], g))
    kept += [w.here(dgate, dgate_out), w.here(dup, dup_out)]
    advance(task_late)
    advance(task_sum)

    @pl.loop(0, 4)
    def _(n):
        out = jnp.dot(rows_of(act, n), w_down[...], preferred_element_type=F32)
        put(mixed, n, out.astype(BF))

    kept.append(w.here(mixed, mixed_out))
    run(*task_sum)
    advance(task_late)
    loads[2].wait()
    loads[3].wait()
    term[...] = jnp.zeros_like(term)
    for k in (0, 1):
        y = y1[k]
        scale = lax.rsqrt(jnp.mean(y * y, -1, keepdims=True) + EPS)
        unit = y * scale
        dh = grad_mid[k]
        term[...] += jnp.sum(dh * unit, 0, keepdims=True)
        wv = dh * gain[...]
        dy = cot[k].astype(F32) + scale * (wv - unit * jnp.mean(wv * unit, -1, keepdims=True))
        grad_mid[k] = dy
        dz[k] = dy.astype(BF)
    dz_rows = dz[...].reshape(128, 2048)
    for t in range(8):
        half = h2 if t < 4 else g
        out = dot_t(dz_rows, half[4 * (t % 4) : 4 * (t % 4) + 4].reshape(256, 2048)).astype(BF)
        d_tok[t] = out.reshape(2, 64, 256)
    run(*task_late)
    w.finish()
    for copy in kept[1:]:
        copy.wait()


def mlp(*args):
    sds = jax.ShapeDtypeStruct
    return pl.pallas_call(
        mlp_kernel,
        out_shape=(
            sds((16, 64, 2048), BF),
            sds((16, 64, 768), BF),
            sds((16, 64, 768), BF),
            sds((16, 64, 768), BF),
            sds((16, 64, 2048), BF),
            sds((2, 64, 2048), F32),
            sds((2, 64, 2048), BF),
            sds((8, 2, 64, 256), BF),
            sds((1, 2048), F32),
            sds((48, 2048), BF),
        ),
        in_specs=[VMEM] * 3 + [HBM] * 3 + [VMEM] * 3,
        out_specs=[HBM] * 5 + [VMEM] * 5,
        scratch_shapes=[
            pltpu.VMEM((16, 64, 2048), BF),
            pltpu.VMEM((2048, 768), BF),
            pltpu.VMEM((2048, 768), BF),
            pltpu.VMEM((768, 2048), BF),
            pltpu.VMEM((16, 64, 2048), BF),
            pltpu.VMEM((4, 256, 768), F32),
            pltpu.VMEM((4, 256, 768), F32),
            pltpu.VMEM((16, 64, 2048), BF),
            pltpu.VMEM((4, 4, 48, 2048), BF),
            pltpu.VMEM((16, 64, 768), BF),
            pltpu.VMEM((16, 64, 768), BF),
            pltpu.VMEM((16, 64, 768), BF),
            pltpu.VMEM((16, 64, 2048), BF),
        ]
        + z_room()
        + xy_room(48, 2048)
        + sems(96, 12),
        compiler_params=pltpu.CompilerParams(
            collective_id=2, has_side_effects=True, vmem_limit_bytes=63 * MB
        ),
        name="mlp",
    )(*args)


def sums2_kernel(part, grads, more, out, mine, mine2, *rest):
    zr, xr, yr, (send_sem, recv_sem, here_sem) = rest[:4], rest[4:10], rest[10:16], rest[16:]
    p = Place()
    w = Wire(send_sem, recv_sem, here_sem)
    meet(p.peers(("z", "sib", "plane")))
    run(
        reduce_z(w, p, part, zr, out),
        reduce_xy(w, p, grads, xr, mine),
        reduce_xy(w, p, more, yr, mine2),
    )
    w.finish()


def sums2(part, grads, more, cid):
    sds = jax.ShapeDtypeStruct
    (_, _, r1, c1), (_, _, r2, c2) = grads.shape, more.shape
    return pl.pallas_call(
        sums2_kernel,
        out_shape=(sds((2, 64, 2048), F32), sds((r1, c1), BF), sds((r2, c2), BF)),
        in_specs=[VMEM] * 3,
        out_specs=[VMEM] * 3,
        scratch_shapes=z_room() + xy_room(r1, c1) + xy_room(r2, c2) + sems(48, 1),
        compiler_params=pltpu.CompilerParams(
            collective_id=cid, has_side_effects=True, vmem_limit_bytes=40 * MB
        ),
        name="sums2",
    )(part, grads, more)


def attend_back_kernel(
    q, kv, kv_far, d_tok, dz_own, mixed_part, gu_part, dq, dkv, dz, mixed, gu_mine,
    do, acc, acc_far, out_far, in_far, *rest
):
    zr, xr, (send_sem, recv_sem, here_sem) = rest[:4], rest[4:10], rest[10:]
    p = Place()
    w = Wire(send_sem, recv_sem, here_sem)
    dz[p.t] = dz_own[0]
    dz[15 - p.t] = dz_own[1]
    meet(p.peers(("tp", "plane")))
    pair = p.at(yl=1 - p.yl)
    spread = []
    for dz_ in (2, 1, 3, 0):
        for dc in (0, 1):
            z, core = p.up(dz_), lax.rem(p.core + dc, 2)
            for k in (0, 1):
                if dz_ or dc:
                    dst = do.at[p.t if k == 0 else 15 - p.t]
                    spread.append(w.send(d_tok.at[2 * z + core, k], dst, p.at(z=z, core=core)))
                else:
                    do[p.t if k == 0 else 15 - p.t] = d_tok[p.t, k]

    def block(t, k):
        return dz.at[t if k == 0 else 15 - t]

    tasks = [
        reduce_xy(w, p, gu_part, xr, gu_mine),
        gather_z(w, p, lambda k: block(p.t, k), block),
        reduce_z(w, p, mixed_part, zr, mixed),
    ]
    advance(tasks)
    acc[...] = jnp.zeros_like(acc)
    acc_far[...] = jnp.zeros_like(acc_far)
    for copy in spread:
        copy.wait_recv()
    back = []
    for j in range(7, -1, -1):
        at = pl.ds(j * 128, 128)
        keys = pl.ds(0, j * 128 + 128)
        tri, seen = edges(p, j)
        qj = both(q, at)
        dj = jnp.concatenate(
            [do[2 * j : 2 * j + 2, :, n * 128 : n * 128 + 128].reshape(128, 128) for n in (0, 1)], 0
        )
        near = weights_of(qj, kv[keys, 0:128], j, tri)
        far = weights_of(qj, kv_far[keys, 0:128], j, seen)
        scale = 1.0 / (jnp.sum(near, -1, keepdims=True) + jnp.sum(far, -1, keepdims=True))
        near = near * scale
        far = far * scale
        d_near = dot_t(dj, kv[keys, 128:256])
        d_far = dot_t(dj, kv_far[keys, 128:256])
        delta = jnp.sum(near * d_near, -1, keepdims=True) + jnp.sum(
            far * d_far, -1, keepdims=True
        )
        s_near = (near * (d_near - delta)).astype(BF)
        s_far = (far * (d_far - delta)).astype(BF)
        grad = jnp.dot(s_near, kv[keys, 0:128], preferred_element_type=F32)
        grad += jnp.dot(s_far, kv_far[keys, 0:128], preferred_element_type=F32)
        grad = (grad * 128**-0.5).astype(BF)
        dq[at, 0:128] = grad[:128]
        dq[at, 128:256] = grad[128:]
        acc[keys, 0:128] += t_dot(s_near, qj)
        acc_far[keys, 0:128] += t_dot(s_far, qj)
        acc[keys, 128:256] += t_dot(near.astype(BF), dj)
        acc_far[keys, 128:256] += t_dot(far.astype(BF), dj)
        out_far[at, 0:128] = (acc_far[at, 0:128] * 128**-0.5).astype(BF)
        out_far[at, 128:256] = acc_far[at, 128:256].astype(BF)
        back.append((at, w.send(out_far.at[at], in_far.at[at], pair)))
        advance(tasks)
    run(*tasks)
    for at, copy in back:
        copy.wait_recv()
        dkv[at, 0:128] = add(acc[at, 0:128] * 128**-0.5, in_far[at, 0:128]).astype(BF)
        dkv[at, 128:256] = add(acc[at, 128:256], in_far[at, 128:256]).astype(BF)
    w.finish()


def attend_back(q, kv, kv_far, d_tok, dz_own, mixed_part, gu_part):
    sds = jax.ShapeDtypeStruct
    return pl.pallas_call(
        attend_back_kernel,
        out_shape=(
            sds((1024, 256), BF),
            sds((1024, 256), BF),
            sds((16, 64, 2048), BF),
            sds((2, 64, 2048), F32),
            sds((128, 1536), BF),
        ),
        in_specs=[VMEM] * 7,
        out_specs=[VMEM] * 5,
        scratch_shapes=[
            pltpu.VMEM((16, 64, 256), BF),
            pltpu.VMEM((1024, 256), F32),
            pltpu.VMEM((1024, 256), F32),
            pltpu.VMEM((1024, 256), BF),
            pltpu.VMEM((1024, 256), BF),
        ]
        + z_room()
        + xy_room(128, 1536)
        + sems(80, 1),
        compiler_params=pltpu.CompilerParams(
            collective_id=4, has_side_effects=True, vmem_limit_bytes=58 * MB
        ),
        name="attend_back",
    )(q, kv, kv_far, d_tok, dz_own, mixed_part, gu_part)


def last_kernel(cols, rows, vec, cols_out, rows_out, vec_out, ra, rb, rc, send_sem, recv_sem, here_sem):
    p = Place()
    w = Wire(send_sem, recv_sem, here_sem)
    meet(p.peers(("tp", "plane", "swap")))
    stay = p.yl == p.core
    cols_out[p.t] = cols[p.t]
    ra[p.t] = vec[...]
    moves = []
    for dz in range(4):
        for dc in range(2):
            if dz or dc:
                z, core = p.up(dz), lax.rem(p.core + dc, 2)
                peer = p.at(z=z, core=core)
                moves.append(w.send(vec, ra.at[p.t], peer))
                moves.append(w.send(cols.at[2 * z + core], cols_out.at[p.t], peer))
    n = w.n
    swap = pltpu.make_async_remote_copy(
        src_ref=rows,
        dst_ref=rows_out,
        send_sem=send_sem.at[n],
        recv_sem=recv_sem.at[n],
        device_id=p.at(yl=1 - p.yl, core=1 - p.core),
        device_id_type=MESH,
    )
    w.n += 1

    @pl.when(jnp.logical_not(stay))
    def _():
        swap.start()

    @pl.when(stay)
    def _():
        rows_out[...] = rows[...]

    for copy in moves[0::2]:
        copy.wait_recv()
    rb[p.x] = sum((ra[i] for i in range(1, 8)), ra[0])
    xs = [w.send(rb.at[p.x], rb.at[p.x], p.at(x=p.east(d))) for d in (1, 2, 3)]
    for copy in xs:
        copy.wait_recv()
    rc[p.y] = sum((rb[i] for i in range(1, 4)), rb[0])
    ys = [w.send(rc.at[p.y], rc.at[p.y], p.north(d)) for d in (1, 2, 3)]
    for copy in ys:
        copy.wait_recv()
    vec_out[...] = sum((rc[i] for i in range(1, 4)), rc[0])
    for copy in moves[1::2]:
        copy.wait_recv()

    @pl.when(jnp.logical_not(stay))
    def _():
        swap.wait()

    w.finish()


def last(cols, rows, vec):
    sds = jax.ShapeDtypeStruct
    n = vec.shape
    return pl.pallas_call(
        last_kernel,
        out_shape=(sds(cols.shape, BF), sds(rows.shape, BF), sds(n, F32)),
        in_specs=[VMEM] * 3,
        out_specs=[VMEM] * 3,
        scratch_shapes=[
            pltpu.VMEM((8,) + n, F32),
            pltpu.VMEM((4,) + n, F32),
            pltpu.VMEM((4,) + n, F32),
        ]
        + sems(32, 1),
        compiler_params=pltpu.CompilerParams(
            collective_id=6, has_side_effects=True, vmem_limit_bytes=32 * MB
        ),
        name="last",
    )(cols, rows, vec)


def rotary(positions, width):
    half = width // 2
    freq = THETA ** (-2.0 * jnp.arange(half, dtype=F32) / width)
    angle = positions.astype(F32)[:, None] * freq[None, :]
    cosine = jnp.concatenate([jnp.cos(angle), jnp.cos(angle)], 1)
    sine = jnp.concatenate([-jnp.sin(angle), jnp.sin(angle)], 1)
    return (cosine, sine)


def turn_back(grads, cosine, sine):
    moved = grads * sine
    half = grads.shape[-1] // 2
    return grads * cosine + jnp.concatenate([moved[..., half:], moved[..., :half]], -1)


def row_norm(vals):
    scale = lax.rsqrt(jnp.mean(vals * vals, -1, keepdims=True) + EPS)
    return (vals * scale, scale)


def norm_back(grad_unit, unit, scale):
    return scale * (grad_unit - unit * jnp.mean(grad_unit * unit, -1, keepdims=True))


def mm(left, right):
    return jnp.dot(left, right, preferred_element_type=F32)


def mm_t(left, right):
    return lax.dot_general(left, right, (((1,), (1,)), ((), ())), preferred_element_type=F32)


def t_mm(left, right):
    return lax.dot_general(left, right, (((0,), (0,)), ((), ())), preferred_element_type=F32)


def gather(val, axes):
    return lax.all_gather(val, axes, axis=0, tiled=True)


def scatter(val, axes):
    return lax.psum_scatter(val, axes, scatter_dimension=0, tiled=True)


def to_sorted(val):
    a = val.reshape(8, 2, 64, -1)
    return jnp.concatenate([a[:, 0], a[::-1, 1]], 0).reshape(1024, -1)


def to_owner(val):
    a = val.reshape(16, 64, -1)
    return jnp.stack([a[:8], a[:7:-1]], 1).reshape(1024, -1)


def gather_tp(val):
    return to_sorted(gather(val, TP))


def scatter_tp(val):
    return scatter(to_owner(val.astype(BF)), TP).astype(F32)


def shards(
    tokens,
    gain_in,
    query_weight,
    key_weight,
    value_weight,
    gain_query,
    gain_key,
    out_weight,
    gain_mid,
    gate_weight,
    up_weight,
    down_weight,
    cotangent,
):
    width = tokens.shape[4]
    n_z, n_yl, n_core = (lax.axis_size(a) for a in ("z", "yl", "core"))
    n_tp = n_z * n_core
    n_fs = lax.axis_size("x") * lax.axis_size("yh")
    rows = 128
    head = 128
    qc, kc, fc = 256, 128, 768
    factor = head ** (-0.5)
    t = lax.axis_index(TP)
    yl = lax.axis_index("yl")

    def positions(lane):
        idx = jnp.arange(1024, dtype=jnp.int32)
        tile, spot = idx // 128, idx % 128
        place = jnp.where(tile < 4, 2 * tile + lane, 2 * tile + 1 - lane)
        return place * 128 + spot

    query_pos = positions(yl)
    key_pos = jnp.concatenate([query_pos, positions(1 - yl)])
    allowed = key_pos[None, :] <= query_pos[:, None]
    cosine, sine = rotary(query_pos, head)

    cut = lambda w, n: lax.dynamic_slice_in_dim(w, t * n, n, 1)
    d_s = down_weight.shape[0] // n_tp
    rows_d = lax.ppermute(
        lax.dynamic_slice_in_dim(down_weight, t * d_s, d_s, 0),
        TP + FS,
        [(a * n_fs + b, b * n_fs + a) for a in range(n_tp) for b in range(n_fs)],
    )

    tok = tokens.reshape(2, 64, width)
    x = tokens.reshape(rows, width).astype(F32)
    unit_in, scale_in = row_norm(x)
    h, w_qkv, query_b, kv, kv_far, raw, attended, g, w_out, w_gate, y_mid, h2_own = ahead(
        tok,
        gain_in.reshape(1, -1),
        jnp.concatenate([cut(query_weight, qc), cut(key_weight, kc), cut(value_weight, kc)], 1),
        cosine,
        sine,
        gain_query.reshape(1, -1),
        gain_key.reshape(1, -1),
        cotangent.reshape(2, 64, width),
        lax.dynamic_slice_in_dim(out_weight, lax.axis_index("core") * 128, 128, 0),
        cut(gate_weight, fc),
        gain_mid.reshape(1, -1),
    )
    h = h.reshape(1024, width)
    attended = attended.reshape(1024, qc)
    unit_q, scale_q = row_norm(raw[:, :qc].reshape(-1, 2, head))
    unit_k, scale_k = row_norm(raw[:, qc : qc + kc].reshape(-1, 1, head))
    h2, act_b, dgate_b, dup_b, mixed_part, grad_mid, dz_own, d_tok, term_mid, down_mine = mlp(
        h2_own,
        cut(up_weight, fc),
        rows_d,
        w_gate,
        g,
        w_out.reshape(32, 64, width),
        y_mid,
        cotangent.reshape(2, 64, width),
        gain_mid.reshape(1, -1),
    )
    h2 = h2.reshape(1024, width)
    y_mid, grad_mid = y_mid.reshape(rows, width), grad_mid.reshape(rows, width)
    dgu = jnp.concatenate([dgate_b.reshape(1024, fc), dup_b.reshape(1024, fc)], 1)

    def rows_to_owners(part):
        cols = part.shape[1]
        part = part.astype(BF).reshape(2, 4, 2, -1, cols)
        return part.transpose(1, 2, 0, 3, 4).reshape(4, 4, -1, cols)

    def cols_to_owners(part):
        cols = part.shape[1]
        part = part.astype(BF).reshape(n_z, n_yl, n_core, 4, 2, 16, cols)
        return part.transpose(3, 4, 1, 0, 2, 5, 6).reshape(4, 4, 128, cols)

    grad_query, own, dz, mlp_out, gu_mine = attend_back(
        query_b,
        kv,
        kv_far,
        d_tok,
        dz_own,
        mixed_part,
        cols_to_owners(t_mm(h2, dgu)),
    )
    dz = dz.reshape(1024, width)
    mixed = (y_mid + mlp_out.reshape(rows, width)).astype(BF)
    dv_b = own[:, head:]
    cos3, sin3 = cosine[:, None, :], sine[:, None, :]
    grad_q_norm = turn_back(grad_query.astype(F32).reshape(-1, 2, head), cos3, sin3)
    grad_k_norm = turn_back(own[:, :head].astype(F32).reshape(-1, 1, head), cos3, sin3)
    term_query = jnp.sum(grad_q_norm * unit_q, (0, 1))
    term_key = jnp.sum(grad_k_norm * unit_k, (0, 1))
    dq_b = norm_back(grad_q_norm * gain_query, unit_q, scale_q).reshape(-1, qc).astype(BF)
    dk_b = norm_back(grad_k_norm * gain_key, unit_k, scale_k).reshape(-1, kc).astype(BF)
    dqkv = jnp.concatenate([dq_b, dk_b, dv_b], 1)
    grad_h, qkv_mine, out_mine = sums2(
        mm_t(dqkv, w_qkv).astype(BF).reshape(16, 64, width),
        cols_to_owners(t_mm(h, dqkv)),
        rows_to_owners(t_mm(attended, dz)),
        5,
    )
    grad_h = grad_h.reshape(rows, width)
    term_in = jnp.sum(grad_h * unit_in, 0)
    tokens_grad = (grad_mid + norm_back(grad_h * gain_in, unit_in, scale_in)).astype(BF)

    mine = jnp.concatenate([gu_mine, qkv_mine], 1).reshape(n_tp, 16, -1)
    late = jnp.concatenate([down_mine, out_mine], 0)
    terms = jnp.concatenate([term_in, term_mid.reshape(-1), term_query, term_key, jnp.zeros((768,), F32)])
    mine, late, terms = last(mine, late, terms.reshape(40, 128))
    mine = mine.transpose(1, 0, 2).astype(F32)

    def take(at, n):
        return mine[:, :, at : at + n].reshape(-1, n_tp * n)

    grad_gate_w, grad_up_w = take(0, fc), take(fc, fc)
    grad_q_w, grad_k_w, grad_v_w = (
        take(2 * fc, qc),
        take(2 * fc + qc, kc),
        take(2 * fc + qc + kc, kc),
    )
    late = late.astype(F32)
    grad_down, grad_out = late[:48], late[48:]
    terms = terms.reshape(-1)
    sum_in, sum_mid = terms[:width], terms[width : 2 * width]
    sum_query, sum_key = terms[2 * width : 2 * width + head], terms[2 * width + head : 2 * width + 2 * head]
    return (
        mixed.reshape(tokens.shape),
        tokens_grad.reshape(tokens.shape),
        sum_in,
        grad_q_w,
        grad_k_w,
        grad_v_w,
        sum_query,
        sum_key,
        grad_out,
        sum_mid,
        grad_gate_w,
        grad_up_w,
        grad_down,
    )


def solution(mesh):
    fine = Mesh(mesh.devices.reshape(4, 2, 2, 4, 2), ALL)
    ctx, fsdp = ("z", "yl", "core"), FS
    act = P(fsdp, None, ctx, None, None)
    weight = P(fsdp, None)
    grad = P(ctx + fsdp, None)
    placed = (
        act, P(), weight, weight, weight, P(), P(), weight, P(), weight, weight, weight, act,
    )
    return jax.shard_map(
        shards,
        mesh=fine,
        in_specs=placed,
        out_specs=(act, act, P(), grad, grad, grad, P(), P(), grad, P(), grad, grad, grad),
        check_vma=False,
    )
```

```python
import functools

import jax
import jax.numpy as jnp
from jax import lax
from jax.experimental import pallas as pl
from jax.experimental.pallas import tpu as pltpu
from jax.sharding import Mesh, PartitionSpec as P

EPS = 1e-06
THETA = 1000000.0
BF = jnp.bfloat16
F32 = jnp.float32
TP = ("z", "core")
FS = ("x", "yh")
DP = ("yl", "x", "yh")
ALL = ("z", "yl", "core", "x", "yh")
MESH = pl.DeviceIdType.MESH
VMEM = pl.BlockSpec(memory_space=pltpu.VMEM)
HBM = pl.BlockSpec(memory_space=pl.ANY)
MB = 2**20
LOG2E = 1.4426950408889634


class Place:
    def __init__(self):
        self.z, self.yl, self.core, self.x, self.yh = (lax.axis_index(a) for a in ALL)
        self.t = 2 * self.z + self.core
        self.shard = 2 * self.x + self.yh
        self.y = 2 * self.yh + self.yl

    def at(self, z=None, yl=None, core=None, x=None, yh=None):
        here = (self.z, self.yl, self.core, self.x, self.yh)
        return tuple(h if n is None else n for h, n in zip(here, (z, yl, core, x, yh)))

    def up(self, n):
        return lax.rem(self.z + n, 4)

    def east(self, n):
        return lax.rem(self.x + n, 4)

    def north(self, n):
        y = lax.rem(self.y + n, 4)
        return self.at(yh=y // 2, yl=lax.rem(y, 2))

    def peers(self, which):
        table = {
            "z": [self.at(z=self.up(1)), self.at(z=self.up(3))],
            "sib": [self.at(core=1 - self.core)],
            "x": [self.at(x=self.east(1)), self.at(x=self.east(3))],
            "cross": [self.at(yl=1 - self.yl, yh=1 - self.yh)],
            "pair": [self.at(yl=1 - self.yl)],
            "plane": [self.at(x=self.east(d)) for d in (1, 2, 3)]
            + [self.north(d) for d in (1, 2, 3)],
            "swap": [self.at(yl=1 - self.yl, core=1 - self.core)],
            "tp": [
                self.at(z=self.up(dz), core=lax.rem(self.core + dc, 2))
                for dz in range(4)
                for dc in range(2)
                if dz or dc
            ],
        }
        return [p for name in which for p in table[name]]


class Wire:
    def __init__(self, send_sem, recv_sem, here_sem):
        self.send_sem, self.recv_sem, self.here_sem = send_sem, recv_sem, here_sem
        self.n = self.m = 0
        self.sent = []

    def send(self, src, dst, peer):
        copy = pltpu.make_async_remote_copy(
            src_ref=src,
            dst_ref=dst,
            send_sem=self.send_sem.at[self.n],
            recv_sem=self.recv_sem.at[self.n],
            device_id=peer,
            device_id_type=MESH,
        )
        self.n += 1
        assert self.n <= self.send_sem.shape[0]
        copy.start()
        self.sent.append(copy)
        return copy

    def here(self, src, dst):
        copy = pltpu.make_async_copy(src, dst, self.here_sem.at[self.m])
        self.m += 1
        assert self.m <= self.here_sem.shape[0]
        copy.start()
        return copy

    def settle(self, copies):
        for copy in copies:
            copy.wait_send()
        self.sent = [one for one in self.sent if all(one is not copy for copy in copies)]

    def finish(self):
        for copy in self.sent:
            copy.wait_send()


def sems(n, m):
    return [
        pltpu.SemaphoreType.DMA((n,)),
        pltpu.SemaphoreType.DMA((n,)),
        pltpu.SemaphoreType.DMA((m,)),
    ]


def meet(peers):
    barrier = pltpu.get_barrier_semaphore()
    for peer in peers:
        pl.semaphore_signal(barrier, inc=1, device_id=peer, device_id_type=MESH)
    pl.semaphore_wait(barrier, len(peers))


def run(*tasks):
    tasks = list(tasks)
    while tasks:
        advance(tasks)


def advance(tasks):
    for task in list(tasks):
        try:
            next(task)
        except StopIteration:
            tasks.remove(task)


def gather_z(w, p, own, dst):
    up, down, sib = p.at(z=p.up(1)), p.at(z=p.up(3)), p.at(core=1 - p.core)
    before, after, far = (2 * p.up(n) + p.core for n in (3, 1, 2))
    u0 = w.send(own(0), dst(p.t, 0), up)
    d1 = w.send(own(1), dst(p.t, 1), down)
    u1 = w.send(own(1), dst(p.t, 1), up)
    d0 = w.send(own(0), dst(p.t, 0), down)
    s = [w.send(own(k), dst(p.t, k), sib) for k in (0, 1)]

    def on(t, k):
        s.append(w.send(dst(t, k), dst(t, k), sib))

    yield
    u0.wait_recv()
    f0 = w.send(dst(before, 0), dst(before, 0), up)
    on(before, 0)
    d1.wait_recv()
    f1 = w.send(dst(after, 1), dst(after, 1), down)
    on(after, 1)
    yield
    u1.wait_recv()
    on(before, 1)
    d0.wait_recv()
    on(after, 0)
    yield
    f0.wait_recv()
    on(far, 0)
    f1.wait_recv()
    on(far, 1)
    yield
    for copy in s:
        copy.wait_recv()
    w.settle([u0, d1, u1, d0, f0, f1] + s)


def gather_xy(w, p, dst, n, ready=None):
    east, west = p.at(x=p.east(1)), p.at(x=p.east(3))
    cross, pair = p.at(yl=1 - p.yl, yh=1 - p.yh), p.at(yl=1 - p.yl)
    half = n // 2
    me = p.shard
    west_s, east_s, far_s = (2 * p.east(k) + p.yh for k in (3, 1, 2))
    mine = p.yl * half
    other = half - mine
    flip = 1 - 2 * p.yh

    def one(s, at, peer):
        return w.send(dst(s, at, half), dst(s, at, half), peer)

    def along(s):
        return one(s + flip, other, pair)

    e0 = one(me, mine, east)
    w0 = one(me, mine, west)
    c0 = one(me, mine, cross)
    w1 = one(me, other, west)
    yield
    e0.wait_recv()
    fe = one(west_s, mine, east)
    c1 = one(west_s, mine, cross)
    e1 = one(me, other, east)
    w0.wait_recv()
    c2 = one(east_s, mine, cross)
    yield
    c0.wait_recv()
    a0 = along(me)
    fe.wait_recv()
    c3 = one(far_s, mine, cross)
    w1.wait_recv()
    fw = one(east_s, other, west)
    if ready:
        ready(east_s)
    yield
    c1.wait_recv()
    a1 = along(west_s)
    e1.wait_recv()
    if ready:
        ready(west_s)
    c2.wait_recv()
    a2 = along(east_s)
    yield
    fw.wait_recv()
    if ready:
        ready(far_s)
    c3.wait_recv()
    a3 = along(far_s)
    yield
    for s, a in ((me, a0), (west_s, a1), (east_s, a2), (far_s, a3)):
        a.wait_recv()
        if ready:
            ready(s + flip)


def norm_rope(raw, gain, cosine, sine):
    unit = raw * lax.rsqrt(jnp.mean(raw * raw, -1, keepdims=True) + EPS)
    vals = unit * gain
    return vals * cosine + pltpu.roll(vals, 64, 1) * sine


SCALE = 128**-0.5 * LOG2E


def dot_t(a, b):
    return lax.dot_general(a, b, (((1,), (1,)), ((), ())), preferred_element_type=F32)


def t_dot(a, b):
    return lax.dot_general(a, b, (((0,), (0,)), ((), ())), preferred_element_type=F32)


def both(ref, at):
    return jnp.concatenate([ref[at, 0:128], ref[at, 128:256]], 0)


def weights_of(q, k, j, edge):
    s = jnp.exp2(dot_t(q, k) * SCALE)
    last = jnp.where(edge, s[:, j * 128 :], 0.0)
    return last if j == 0 else jnp.concatenate([s[:, : j * 128], last], 1)


def edges(p, j):
    row = lax.broadcasted_iota(jnp.int32, (256, 128), 0) % 128
    col = lax.broadcasted_iota(jnp.int32, (256, 128), 1)
    seen = (p.yl if j < 4 else 1 - p.yl) * 128
    return col <= row, col < seen


def shard_rows(ref, n):
    return lambda s, at, m: ref.at[pl.ds(pl.multiple_of(s * n + at, 16), m)]


def ahead_kernel(
    tok, gain, w_own, cosine, sine, gq, gk, cot, wo, gate_own, gain_mid,
    h_out, qkv_out, q, kv, kv_far, raw, o, g_out, out_out, gate_out, y1, h2,
    h, w_qkv, g, w_out, w_gate, o_tok, send_sem, recv_sem, here_sem
):
    p = Place()
    w = Wire(send_sem, recv_sem, here_sem)
    w_qkv[pl.ds(pl.multiple_of(p.shard * 256, 256), 256)] = w_own[...]
    for k in (0, 1):
        x = tok[k].astype(F32)
        unit = x * lax.rsqrt(jnp.mean(x * x, -1, keepdims=True) + EPS)
        h[p.t if k == 0 else 15 - p.t] = (unit * gain[...]).astype(BF)
    meet(p.peers(("tp", "x", "cross", "pair")))
    pair, sib = p.at(yl=1 - p.yl), p.at(core=1 - p.core)

    def block_of(ref):
        return lambda t, k: ref.at[t if k == 0 else 15 - t]

    def part_out(s, at, n):
        return w_out.at[s, p.core, pl.ds(pl.multiple_of(at, 64), n)]

    twin = []

    def ready(s):
        twin.append(w.send(w_out.at[s, p.core], w_out.at[s, p.core], sib))

    at_h, at_g = block_of(h), block_of(g)
    task_h = [gather_z(w, p, lambda k: at_h(p.t, k), at_h)]
    task_qkv = [gather_xy(w, p, shard_rows(w_qkv, 256), 256)]
    advance(task_qkv)
    advance(task_h)
    w_out[p.shard, p.core] = wo[...]
    g[p.t] = cot[0]
    g[15 - p.t] = cot[1]
    w_gate[pl.ds(pl.multiple_of(p.shard * 256, 256), 256)] = gate_own[...]
    task_out = [gather_xy(w, p, part_out, 128, ready)]
    task_gate = [gather_xy(w, p, shard_rows(w_gate, 256), 256)]
    task_g = [gather_z(w, p, lambda k: at_g(p.t, k), at_g)]
    ready(p.shard)
    advance(task_qkv)
    advance(task_h)
    advance(task_qkv)
    advance(task_out)
    advance(task_qkv)
    advance(task_h)
    advance(task_qkv)
    advance(task_qkv)
    advance(task_out)
    advance(task_h)
    advance(task_gate)
    advance(task_g)
    run(task_h[0])
    kept = [w.here(h, h_out), w.here(w_qkv, qkv_out)]
    swaps = []
    for j in range(4):
        at = pl.ds(j * 256, 256)
        out = jnp.dot(
            h[4 * j : 4 * j + 4].reshape(256, 2048), w_qkv[...], preferred_element_type=F32
        )
        cos, sin = cosine[at], sine[at]
        kv[at, 0:128] = norm_rope(out[:, 256:384], gk[...], cos, sin).astype(BF)
        kv[at, 128:256] = out[:, 384:].astype(BF)
        swaps.append(w.send(kv.at[at], kv_far.at[at], pair))
        for n in (0, 1):
            cols = slice(n * 128, n * 128 + 128)
            q[at, cols] = norm_rope(out[:, cols], gq[...], cos, sin).astype(BF)
        raw[at] = out[:, :384]
        if j in (1, 3):
            advance(task_out)
        if j == 2:
            advance(task_gate)
            advance(task_g)
    for j in range(8):
        at = pl.ds(j * 128, 128)
        keys = pl.ds(0, j * 128 + 128)
        if j % 2 == 0:
            swaps[j // 2].wait_recv()
        tri, seen = edges(p, j)
        qj = both(q, at)
        near = weights_of(qj, kv[keys, 0:128], j, tri)
        far = weights_of(qj, kv_far[keys, 0:128], j, seen)
        total = jnp.sum(near, -1, keepdims=True) + jnp.sum(far, -1, keepdims=True)
        out = jnp.dot(near.astype(BF), kv[keys, 128:256], preferred_element_type=F32)
        out += jnp.dot(far.astype(BF), kv_far[keys, 128:256], preferred_element_type=F32)
        out = (out / total).astype(BF)
        for n in (0, 1):
            o[2 * j : 2 * j + 2, :, n * 128 : n * 128 + 128] = out[
                n * 128 : n * 128 + 128
            ].reshape(2, 64, 128)
        if j == 1:
            advance(task_g)
        if j == 4:
            advance(task_out)
            advance(task_g)
        if j == 6:
            advance(task_gate)
    spread = []
    for dz in (2, 1, 3, 0):
        for dc in range(2):
            z, core = p.up(dz), lax.rem(p.core + dc, 2)
            t = 2 * z + core
            for k in (0, 1):
                src = o.at[t if k == 0 else 15 - t]
                if dz or dc:
                    spread.append(w.send(src, o_tok.at[p.t, k], p.at(z=z, core=core)))
                else:
                    o_tok[p.t, k] = o[t if k == 0 else 15 - t]
    run(*task_g)
    kept.append(w.here(g, g_out))
    advance(task_gate)
    run(*task_out)
    advance(task_gate)
    for copy in twin:
        copy.wait_recv()
    kept.append(w.here(w_out, out_out))
    for copy in spread:
        copy.wait_recv()
    for n in range(4):
        cols = slice(n * 512, n * 512 + 512)
        for k in (0, 1):
            y1[k, :, cols] = tok[k, :, cols].astype(F32)
        for t in range(8):
            part = jnp.dot(
                o_tok[t].reshape(128, 256),
                w_out[t, :, :, cols].reshape(256, 512),
                preferred_element_type=F32,
            )
            for k in (0, 1):
                y1[k, :, cols] += part[k * 64 : k * 64 + 64]
    for k in (0, 1):
        y = y1[k]
        unit = y * lax.rsqrt(jnp.mean(y * y, -1, keepdims=True) + EPS)
        h2[k] = (unit * gain_mid[...]).astype(BF)
    run(*task_gate)
    kept.append(w.here(w_gate, gate_out))
    w.finish()
    for copy in kept:
        copy.wait()


def ahead(*args):
    sds = jax.ShapeDtypeStruct
    return pl.pallas_call(
        ahead_kernel,
        out_shape=(
            sds((16, 64, 2048), BF),
            sds((2048, 512), BF),
            sds((1024, 256), BF),
            sds((1024, 256), BF),
            sds((1024, 256), BF),
            sds((1024, 384), F32),
            sds((16, 64, 256), BF),
            sds((16, 64, 2048), BF),
            sds((8, 2, 128, 2048), BF),
            sds((2048, 768), BF),
            sds((2, 64, 2048), F32),
            sds((2, 64, 2048), BF),
        ),
        in_specs=[VMEM] * 11,
        out_specs=[HBM, HBM, VMEM, VMEM, VMEM, VMEM, VMEM, HBM, HBM, HBM, VMEM, VMEM],
        scratch_shapes=[
            pltpu.VMEM((16, 64, 2048), BF),
            pltpu.VMEM((2048, 512), BF),
            pltpu.VMEM((16, 64, 2048), BF),
            pltpu.VMEM((8, 2, 128, 2048), BF),
            pltpu.VMEM((2048, 768), BF),
            pltpu.VMEM((8, 2, 64, 256), BF),
        ]
        + sems(128, 8),
        compiler_params=pltpu.CompilerParams(
            collective_id=0, has_side_effects=True, vmem_limit_bytes=56 * MB
        ),
        name="ahead",
    )(*args)


def rows_of(ref, zz):
    c = ref.shape[-1]
    return jnp.concatenate(
        [ref[pl.ds(2 * zz, 2)].reshape(128, c), ref[pl.ds(14 - 2 * zz, 2)].reshape(128, c)], 0
    )


def put(ref, zz, val):
    c = ref.shape[-1]
    ref[pl.ds(2 * zz, 2)] = val[:128].reshape(2, 64, c)
    ref[pl.ds(14 - 2 * zz, 2)] = val[128:].reshape(2, 64, c)


def add(*vals):
    total = vals[0].astype(F32)
    for val in vals[1:]:
        total = total + val.astype(F32)
    return total


def z_room():
    return [
        pltpu.VMEM((4, 2, 64, 2048), BF),
        pltpu.VMEM((2, 64, 2048), BF),
        pltpu.VMEM((2, 2, 64, 2048), BF),
    ]


def reduce_z(w, p, part, room, out):
    mine, relay, last = room
    near = mine
    up, down, sib = p.at(z=p.up(1)), p.at(z=p.up(3)), p.at(core=1 - p.core)

    def block(n, core, k):
        t = 2 * p.up(n) + core
        return t if k == 0 else 15 - t

    first = {}

    def give(n):
        for k in (0, 1):
            first[n, k] = w.send(part.at[block(n, 1 - p.core, k)], near.at[n, k], sib)

    def fold(n, k):
        first[n, k].wait_recv()
        mine[n, k] = add(part[block(n, p.core, k)], near[n, k]).astype(BF)

    give(2)
    yield
    give(1)
    fold(2, 0)
    e0 = w.send(mine.at[2, 0], relay.at[0], up)
    fold(2, 1)
    e1 = w.send(mine.at[2, 1], relay.at[1], down)
    yield
    give(3)
    fold(1, 1)
    a1 = w.send(mine.at[1, 1], last.at[0, 1], up)
    fold(1, 0)
    yield
    give(0)
    fold(3, 0)
    b0 = w.send(mine.at[3, 0], last.at[1, 0], down)
    fold(3, 1)
    yield
    e0.wait_recv()
    mine[1, 0] = add(mine[1, 0], relay[0]).astype(BF)
    a0 = w.send(mine.at[1, 0], last.at[0, 0], up)
    e1.wait_recv()
    mine[3, 1] = add(mine[3, 1], relay[1]).astype(BF)
    b1 = w.send(mine.at[3, 1], last.at[1, 1], down)
    fold(0, 0)
    fold(0, 1)
    w.settle(list(first.values()))
    yield
    for k, (a, b) in enumerate(((a0, b0), (a1, b1))):
        a.wait_recv()
        b.wait_recv()
        out[k] = add(mine[0, k], last[0, k], last[1, k])


def xy_room(rows, cols, left=None):
    left = left or cols // 2
    return [
        pltpu.VMEM(lead + (rows, n), BF)
        for n in (left, cols - left)
        for lead in ((3, 4), (4,), (3,))
    ]


def put_half(out, cols, val):
    if len(out.shape) == 3:
        out[:, :, cols] = val.reshape(out.shape[0], out.shape[1], val.shape[1])
    else:
        out[:, cols] = val


def reduce_xy(w, p, part, room, out):
    ra, sa, fa, rb, sb, fb = room
    cols = part.shape[3]
    n_left = sa.shape[2]
    left, right = pl.ds(0, n_left), pl.ds(n_left, cols - n_left)
    spans = (1, 2, 3)
    easts = [p.at(x=p.east(d)) for d in spans]
    norths = [p.north(d) for d in spans]
    ca = [w.send(part.at[p.east(d), :, :, left], ra.at[d - 1], easts[d - 1]) for d in spans]
    yield
    cb = [
        w.send(part.at[:, lax.rem(p.y + d, 4), :, right], rb.at[d - 1], norths[d - 1])
        for d in spans
    ]
    yield
    for copy in ca:
        copy.wait_recv()

    @pl.loop(0, 4)
    def _(y):
        sa[y] = add(part[p.x, y, :, left], ra[0, y], ra[1, y], ra[2, y]).astype(BF)

    da = [w.send(sa.at[lax.rem(p.y + d, 4)], fa.at[d - 1], norths[d - 1]) for d in spans]
    yield
    for copy in cb:
        copy.wait_recv()

    @pl.loop(0, 4)
    def _(x):
        sb[x] = add(part[x, p.y, :, right], rb[0, x], rb[1, x], rb[2, x]).astype(BF)

    db = [w.send(sb.at[p.east(d)], fb.at[d - 1], easts[d - 1]) for d in spans]
    yield
    for copy in da:
        copy.wait_recv()
    put_half(out, left, add(sa[p.y], fa[0], fa[1], fa[2]).astype(BF))
    yield
    for copy in db:
        copy.wait_recv()
    put_half(out, right, add(sb[p.x], fb[0], fb[1], fb[2]).astype(BF))


def mlp_kernel(
    h2_own, up_own, down_own, gate_hbm, g_hbm, out_hbm, y1, cot, gain,
    h2_out, dgate_out, dup_out, mixed_out, grad_mid, dz, d_tok, term, down_mine,
    h2, w_gate, w_up, w_down, g, gate, upper, part, down_part, act, dgate, dup, mixed, *rest
):
    zr, xr, (send_sem, recv_sem, here_sem) = rest[:3], rest[3:9], rest[9:]
    p = Place()
    w = Wire(send_sem, recv_sem, here_sem)
    loads = [w.here(gate_hbm, w_gate), w.here(g_hbm, g)]
    h2[p.t] = h2_own[0]
    h2[15 - p.t] = h2_own[1]
    w_up[pl.ds(pl.multiple_of(p.shard * 256, 256), 256)] = up_own[...]
    w_down[pl.ds(pl.multiple_of(p.shard * 96, 96), 96)] = down_own[...]
    meet(p.peers(("z", "sib", "x", "plane", "cross")))

    def block(t, k):
        return h2.at[t if k == 0 else 15 - t]

    task_h = [gather_z(w, p, lambda k: block(p.t, k), block)]
    task_up = [gather_xy(w, p, shard_rows(w_up, 256), 256)]
    task_down = [gather_xy(w, p, shard_rows(w_down, 96), 96)]
    advance(task_up)
    advance(task_h)
    advance(task_up)
    advance(task_down)
    advance(task_h)
    advance(task_up)
    advance(task_up)
    advance(task_h)
    advance(task_down)
    advance(task_up)
    advance(task_h)
    run(*task_h)
    kept = [w.here(h2, h2_out)]
    loads[0].wait()

    @pl.loop(0, 4)
    def _(n):
        gate[n] = jnp.dot(rows_of(h2, n), w_gate[...], preferred_element_type=F32)

    run(*task_up)
    advance(task_down)

    @pl.loop(0, 4)
    def _(n):
        up_n = jnp.dot(rows_of(h2, n), w_up[...], preferred_element_type=F32)
        gate_n = gate[n]
        upper[n] = up_n
        put(act, n, (gate_n * jax.nn.sigmoid(gate_n) * up_n).astype(BF))

    advance(task_down)
    loads[1].wait()
    kept[0].wait()
    loads.append(w.here(out_hbm.at[pl.ds(0, 16)], h2))

    @pl.loop(0, 6)
    def _(i):
        cols = pl.ds(pl.multiple_of(i * 128, 128), 128)
        left = act[:, :, cols].reshape(1024, 128)
        out = t_dot(left, g[...].reshape(1024, 2048)).astype(BF)
        for k in range(8):
            row = i * 8 + k
            piece = row // 3
            f = lax.rem(piece, 8)
            down_part[f // 2, 2 * lax.rem(f, 2) + piece // 8, pl.ds(pl.multiple_of(lax.rem(row, 3) * 16, 16), 16)] = out[
                k * 16 : k * 16 + 16
            ]

    run(*task_down)
    task_sum = [reduce_z(w, p, part, zr, grad_mid)]
    task_late = [reduce_xy(w, p, down_part, xr, down_mine)]
    advance(task_late)
    advance(task_late)
    for n in (2, 1, 3, 0):
        zz = p.up(n)
        gate_n, up_n = gate[zz], upper[zz]
        sig = jax.nn.sigmoid(gate_n)
        da = dot_t(rows_of(g, zz), w_down[...])
        silu = gate_n * sig
        d_gate = (da * up_n * sig * (1.0 + gate_n * (1.0 - sig))).astype(BF)
        d_up = (da * silu).astype(BF)
        put(dgate, zz, d_gate)
        put(dup, zz, d_up)
        total = dot_t(d_gate, w_gate[...]) + dot_t(d_up, w_up[...])
        put(part, zz, total.astype(BF))
        advance(task_sum)
    loads.append(w.here(out_hbm.at[pl.ds(16, 16)], g))
    kept += [w.here(dgate, dgate_out), w.here(dup, dup_out)]
    advance(task_late)
    advance(task_sum)

    @pl.loop(0, 4)
    def _(n):
        out = jnp.dot(rows_of(act, n), w_down[...], preferred_element_type=F32)
        put(mixed, n, out.astype(BF))

    kept.append(w.here(mixed, mixed_out))
    run(*task_sum)
    advance(task_late)
    loads[2].wait()
    loads[3].wait()
    term[...] = jnp.zeros_like(term)
    for k in (0, 1):
        y = y1[k]
        scale = lax.rsqrt(jnp.mean(y * y, -1, keepdims=True) + EPS)
        unit = y * scale
        dh = grad_mid[k]
        term[...] += jnp.sum(dh * unit, 0, keepdims=True)
        wv = dh * gain[...]
        dy = cot[k].astype(F32) + scale * (wv - unit * jnp.mean(wv * unit, -1, keepdims=True))
        grad_mid[k] = dy
        dz[k] = dy.astype(BF)
    dz_rows = dz[...].reshape(128, 2048)
    for t in range(8):
        half = h2 if t < 4 else g
        out = dot_t(dz_rows, half[4 * (t % 4) : 4 * (t % 4) + 4].reshape(256, 2048)).astype(BF)
        d_tok[t] = out.reshape(2, 64, 256)
    run(*task_late)
    w.finish()
    for copy in kept[1:]:
        copy.wait()


def mlp(*args):
    sds = jax.ShapeDtypeStruct
    return pl.pallas_call(
        mlp_kernel,
        out_shape=(
            sds((16, 64, 2048), BF),
            sds((16, 64, 768), BF),
            sds((16, 64, 768), BF),
            sds((16, 64, 2048), BF),
            sds((2, 64, 2048), F32),
            sds((2, 64, 2048), BF),
            sds((8, 2, 64, 256), BF),
            sds((1, 2048), F32),
            sds((48, 2048), BF),
        ),
        in_specs=[VMEM] * 3 + [HBM] * 3 + [VMEM] * 3,
        out_specs=[HBM] * 4 + [VMEM] * 5,
        scratch_shapes=[
            pltpu.VMEM((16, 64, 2048), BF),
            pltpu.VMEM((2048, 768), BF),
            pltpu.VMEM((2048, 768), BF),
            pltpu.VMEM((768, 2048), BF),
            pltpu.VMEM((16, 64, 2048), BF),
            pltpu.VMEM((4, 256, 768), F32),
            pltpu.VMEM((4, 256, 768), F32),
            pltpu.VMEM((16, 64, 2048), BF),
            pltpu.VMEM((4, 4, 48, 2048), BF),
            pltpu.VMEM((16, 64, 768), BF),
            pltpu.VMEM((16, 64, 768), BF),
            pltpu.VMEM((16, 64, 768), BF),
            pltpu.VMEM((16, 64, 2048), BF),
        ]
        + z_room()
        + xy_room(48, 2048)
        + sems(96, 12),
        compiler_params=pltpu.CompilerParams(
            collective_id=2, has_side_effects=True, vmem_limit_bytes=63 * MB
        ),
        name="mlp",
    )(*args)


def sum_all(w, p, vec, slots, out):
    ra, rb, rc = slots
    ra[p.t] = vec[...]
    first = [w.send(ra.at[p.t], ra.at[p.t], peer) for peer in p.peers(("tp",))]
    yield
    for copy in first:
        copy.wait_recv()
    rb[p.x] = sum((ra[i] for i in range(1, 8)), ra[0])
    xs = [w.send(rb.at[p.x], rb.at[p.x], p.at(x=p.east(d))) for d in (1, 2, 3)]
    yield
    for copy in xs:
        copy.wait_recv()
    rc[p.y] = sum((rb[i] for i in range(1, 4)), rb[0])
    ys = [w.send(rc.at[p.y], rc.at[p.y], p.north(d)) for d in (1, 2, 3)]
    yield
    for copy in ys:
        copy.wait_recv()
    out[...] = sum((rc[i] for i in range(1, 4)), rc[0])


def deal(w, p, src, dst):
    dst[p.t] = src[p.t]
    copies = []
    for dz in (2, 1, 3, 0):
        for dc in range(2):
            if dz or dc:
                z, core = p.up(dz), lax.rem(p.core + dc, 2)
                copies.append(w.send(src.at[2 * z + core], dst.at[p.t], p.at(z=z, core=core)))
    return copies


def to_pieces(part, i, out, cols):
    z, yl = i // 2, lax.rem(i, 2)
    for r in range(16):
        core, f = r // 8, r % 8
        at = pl.ds(pl.multiple_of((2 * z + core) * 16, 16), 16)
        part[f // 2, 2 * (f % 2) + yl, at, cols] = out[r * 16 : r * 16 + 16]


def turn_norm_back(grad, raw, gain, cosine, sine):
    scale = lax.rsqrt(jnp.mean(raw * raw, -1, keepdims=True) + EPS)
    unit = raw * scale
    back = grad * cosine + pltpu.roll(grad * sine, 64, 1)
    term = jnp.sum(back * unit, 0, keepdims=True)
    back = back * gain
    return scale * (back - unit * jnp.mean(back * unit, -1, keepdims=True)), term


def behind_kernel(
    q, kv, kv_far, cosine, sine, gq, gk, d_tok, dz_own, o, tok, gain, term_mid, down_mine,
    raw_hbm, qkv_hbm, mid_hbm, y1_hbm, h2_hbm, dgate_hbm, dup_hbm, mixed_hbm, h_hbm,
    mixed, tokens_grad, cols_gu, cols_qkv, rows_out, vec_out,
    do, acc, acc_far, out_far, in_far, dz, big_x, big_y, dqkv, gu_part, qkv_part, out_part,
    gu_mine, qkv_mine, rows, vec, ra, rb, rc, dh, raw, w_qkv, grad_mid, y1, *rest
):
    mix_room, dh_room = rest[:3], rest[3:6]
    gu_room, qkv_room, out_room = rest[6:12], rest[12:18], rest[18:24]
    send_sem, recv_sem, here_sem = rest[24:]
    p = Place()
    w = Wire(send_sem, recv_sem, here_sem)
    loads = [
        w.here(h2_hbm, big_y),
        w.here(dgate_hbm, big_x.at[:, :, pl.ds(0, 768)]),
        w.here(dup_hbm, big_x.at[:, :, pl.ds(768, 768)]),
        w.here(raw_hbm, raw),
        w.here(qkv_hbm, w_qkv),
        w.here(mid_hbm, grad_mid),
        w.here(y1_hbm, y1),
    ]
    dz[p.t] = dz_own[0]
    dz[15 - p.t] = dz_own[1]
    vec[...] = jnp.zeros_like(vec)
    vec[2:3] = term_mid[...]
    rows[0:48] = down_mine[...]
    meet(p.peers(("tp", "plane", "swap")))
    pair = p.at(yl=1 - p.yl)
    spread = []
    for far in (2, 1, 3, 0):
        for dc in (0, 1):
            z, core = p.up(far), lax.rem(p.core + dc, 2)
            for k in (0, 1):
                if far or dc:
                    dst = do.at[p.t if k == 0 else 15 - p.t]
                    spread.append(w.send(d_tok.at[2 * z + core, k], dst, p.at(z=z, core=core)))
                else:
                    do[p.t if k == 0 else 15 - p.t] = d_tok[p.t, k]

    def block(t, k):
        return dz.at[t if k == 0 else 15 - t]

    task_dz = [gather_z(w, p, lambda k: block(p.t, k), block)]
    advance(task_dz)
    for copy in loads[:3]:
        copy.wait()

    def grad_gu(i):
        cols = pl.ds(pl.multiple_of(i * 256, 256), 256)
        left = big_y[:, :, cols].reshape(1024, 256)
        for n in (0, 1):
            at = slice(n * 768, n * 768 + 768)
            to_pieces(gu_part, i, t_dot(left, big_x[:, :, at].reshape(1024, 768)).astype(BF), at)

    pl.loop(0, 8)(grad_gu)
    task_gu = [reduce_xy(w, p, gu_part, gu_room, gu_mine)]
    advance(task_gu)
    load = w.here(mixed_hbm, big_y)
    acc[...] = jnp.zeros_like(acc)
    acc_far[...] = jnp.zeros_like(acc_far)
    for copy in loads[3:]:
        copy.wait()
    for copy in spread:
        copy.wait_recv()
    back = []
    for j in range(7, -1, -1):
        at = pl.ds(j * 128, 128)
        keys = pl.ds(0, j * 128 + 128)
        tri, seen = edges(p, j)
        qj = both(q, at)
        dj = jnp.concatenate(
            [do[2 * j : 2 * j + 2, :, n * 128 : n * 128 + 128].reshape(128, 128) for n in (0, 1)], 0
        )
        near = weights_of(qj, kv[keys, 0:128], j, tri)
        far = weights_of(qj, kv_far[keys, 0:128], j, seen)
        scale = 1.0 / (jnp.sum(near, -1, keepdims=True) + jnp.sum(far, -1, keepdims=True))
        near = near * scale
        far = far * scale
        d_near = dot_t(dj, kv[keys, 128:256])
        d_far = dot_t(dj, kv_far[keys, 128:256])
        delta = jnp.sum(near * d_near, -1, keepdims=True) + jnp.sum(
            far * d_far, -1, keepdims=True
        )
        s_near = (near * (d_near - delta)).astype(BF)
        s_far = (far * (d_far - delta)).astype(BF)
        acc_far[keys, 0:128] += t_dot(s_far, qj)
        acc_far[keys, 128:256] += t_dot(far.astype(BF), dj)
        out_far[at, 0:128] = (acc_far[at, 0:128] * 128**-0.5).astype(BF)
        out_far[at, 128:256] = acc_far[at, 128:256].astype(BF)
        back.append((j, w.send(out_far.at[at], in_far.at[at], pair)))
        acc[keys, 0:128] += t_dot(s_near, qj)
        acc[keys, 128:256] += t_dot(near.astype(BF), dj)
        grad = jnp.dot(s_near, kv[keys, 0:128], preferred_element_type=F32)
        grad += jnp.dot(s_far, kv_far[keys, 0:128], preferred_element_type=F32)
        grad = (grad * 128**-0.5).astype(BF).astype(F32)
        for n in (0, 1):
            cols = slice(n * 128, n * 128 + 128)
            val, term = turn_norm_back(grad[cols], raw[at, cols], gq[...], cosine[at], sine[at])
            dqkv[2 * j : 2 * j + 2, :, cols] = val.astype(BF).reshape(2, 64, 128)
            vec[4:5, 0:128] += term
        if j in (7, 4, 1):
            advance(task_dz)
    advance(task_gu)
    run(*task_dz)
    for i in range(2):
        out = t_dot(
            o[:, :, i * 128 : i * 128 + 128].reshape(1024, 128), dz[...].reshape(1024, 2048)
        ).astype(BF)
        for f in range(8):
            out_part[f // 2, 2 * (f % 2) + i] = out[f * 16 : f * 16 + 16]
    load.wait()
    load = w.here(h_hbm, dz)
    task_out = [reduce_xy(w, p, out_part, out_room, rows.at[pl.ds(48, 16)])]
    advance(task_out)
    advance(task_out)
    for j, copy in back:
        at = pl.ds(j * 128, 128)
        copy.wait_recv()
        grad = add(acc[at, 0:128] * 128**-0.5, in_far[at, 0:128]).astype(BF).astype(F32)
        val, term = turn_norm_back(grad, raw[at, 256:384], gk[...], cosine[at], sine[at])
        dqkv[2 * j : 2 * j + 2, :, 256:384] = val.astype(BF).reshape(2, 64, 128)
        vec[5:6, 0:128] += term
        dv = add(acc[at, 128:256], in_far[at, 128:256]).astype(BF)
        dqkv[2 * j : 2 * j + 2, :, 384:512] = dv.reshape(2, 64, 128)
    task_dh = [reduce_z(w, p, big_x, dh_room, dh)]
    for n in (2, 1, 3, 0):
        zz = p.up(n)
        put(big_x, zz, dot_t(rows_of(dqkv, zz), w_qkv[...]).astype(BF))
        advance(task_dh)
    load.wait()

    def grad_qkv(i):
        cols = pl.ds(pl.multiple_of(i * 256, 256), 256)
        out = t_dot(dz[:, :, cols].reshape(1024, 256), dqkv[...].reshape(1024, 512))
        to_pieces(qkv_part, i, out.astype(BF), slice(0, 512))

    pl.loop(0, 8)(grad_qkv)
    task_qkv = [reduce_xy(w, p, qkv_part, qkv_room, qkv_mine)]
    advance(task_qkv)
    advance(task_qkv)
    advance(task_dh)
    run(*task_dh)
    total = jnp.zeros((1, 2048), F32)
    for k in (0, 1):
        x = tok[k].astype(F32)
        scale = lax.rsqrt(jnp.mean(x * x, -1, keepdims=True) + EPS)
        unit = x * scale
        total += jnp.sum(dh[k] * unit, 0, keepdims=True)
        wv = dh[k] * gain[...]
        dx = grad_mid[k] + scale * (wv - unit * jnp.mean(wv * unit, -1, keepdims=True))
        tokens_grad[k] = dx.astype(BF)
    vec[0:1] = total
    task_vec = [sum_all(w, p, vec, (ra, rb, rc), vec_out)]
    task_mix = [reduce_z(w, p, big_y, mix_room, dh)]
    advance(task_vec)
    for _ in range(4):
        advance(task_mix)
    advance(task_gu)
    advance(task_gu)
    advance(task_out)
    advance(task_out)
    advance(task_vec)
    advance(task_mix)
    run(*task_gu)
    dealt = deal(w, p, gu_mine, cols_gu)
    advance(task_vec)
    advance(task_qkv)
    advance(task_qkv)
    run(*task_out)
    stay = p.yl == p.core
    n = w.n
    w.n += 1
    swap = pltpu.make_async_remote_copy(
        src_ref=rows,
        dst_ref=rows_out,
        send_sem=send_sem.at[n],
        recv_sem=recv_sem.at[n],
        device_id=p.at(yl=1 - p.yl, core=1 - p.core),
        device_id_type=MESH,
    )

    @pl.when(jnp.logical_not(stay))
    def _():
        swap.start()

    @pl.when(stay)
    def _():
        rows_out[...] = rows[...]

    run(*task_qkv)
    dealt += deal(w, p, qkv_mine, cols_qkv)
    run(*task_mix)
    for k in (0, 1):
        mixed[k] = (y1[k] + dh[k]).astype(BF)
    run(*task_vec)
    for copy in dealt:
        copy.wait_recv()

    @pl.when(jnp.logical_not(stay))
    def _():
        swap.wait()

    w.finish()


def behind(*args):
    sds = jax.ShapeDtypeStruct
    return pl.pallas_call(
        behind_kernel,
        out_shape=(
            sds((2, 64, 2048), BF),
            sds((2, 64, 2048), BF),
            sds((8, 16, 1536), BF),
            sds((8, 16, 512), BF),
            sds((64, 2048), BF),
            sds((8, 2048), F32),
        ),
        in_specs=[VMEM] * 14 + [HBM] * 9,
        out_specs=[VMEM] * 6,
        scratch_shapes=[
            pltpu.VMEM((16, 64, 256), BF),
            pltpu.VMEM((1024, 256), F32),
            pltpu.VMEM((1024, 256), F32),
            pltpu.VMEM((1024, 256), BF),
            pltpu.VMEM((1024, 256), BF),
            pltpu.VMEM((16, 64, 2048), BF),
            pltpu.VMEM((16, 64, 2048), BF),
            pltpu.VMEM((16, 64, 2048), BF),
            pltpu.VMEM((16, 64, 512), BF),
            pltpu.VMEM((4, 4, 128, 1536), BF),
            pltpu.VMEM((4, 4, 128, 512), BF),
            pltpu.VMEM((4, 4, 16, 2048), BF),
            pltpu.VMEM((8, 16, 1536), BF),
            pltpu.VMEM((8, 16, 512), BF),
            pltpu.VMEM((64, 2048), BF),
            pltpu.VMEM((8, 2048), F32),
            pltpu.VMEM((8, 8, 2048), F32),
            pltpu.VMEM((4, 8, 2048), F32),
            pltpu.VMEM((4, 8, 2048), F32),
            pltpu.VMEM((2, 64, 2048), F32),
            pltpu.VMEM((1024, 384), F32),
            pltpu.VMEM((2048, 512), BF),
            pltpu.VMEM((2, 64, 2048), F32),
            pltpu.VMEM((2, 64, 2048), F32),
        ]
        + z_room()
        + z_room()
        + xy_room(128, 1536, 1024)
        + xy_room(128, 512)
        + xy_room(16, 2048)
        + sems(160, 12),
        compiler_params=pltpu.CompilerParams(
            collective_id=1, has_side_effects=True, vmem_limit_bytes=63 * MB
        ),
        name="behind",
    )(*args)


def rotary(positions, width):
    half = width // 2
    freq = THETA ** (-2.0 * jnp.arange(half, dtype=F32) / width)
    angle = positions.astype(F32)[:, None] * freq[None, :]
    cosine = jnp.concatenate([jnp.cos(angle), jnp.cos(angle)], 1)
    sine = jnp.concatenate([-jnp.sin(angle), jnp.sin(angle)], 1)
    return (cosine, sine)


def row_norm(vals):
    scale = lax.rsqrt(jnp.mean(vals * vals, -1, keepdims=True) + EPS)
    return (vals * scale, scale)


def norm_back(grad_unit, unit, scale):
    return scale * (grad_unit - unit * jnp.mean(grad_unit * unit, -1, keepdims=True))


def mm(left, right):
    return jnp.dot(left, right, preferred_element_type=F32)


def mm_t(left, right):
    return lax.dot_general(left, right, (((1,), (1,)), ((), ())), preferred_element_type=F32)


def t_mm(left, right):
    return lax.dot_general(left, right, (((0,), (0,)), ((), ())), preferred_element_type=F32)


def shards(
    tokens,
    gain_in,
    query_weight,
    key_weight,
    value_weight,
    gain_query,
    gain_key,
    out_weight,
    gain_mid,
    gate_weight,
    up_weight,
    down_weight,
    cotangent,
):
    width = tokens.shape[4]
    n_tp = lax.axis_size("z") * lax.axis_size("core")
    n_fs = lax.axis_size("x") * lax.axis_size("yh")
    head = 128
    qc, kc, fc = 256, 128, 768
    t = lax.axis_index(TP)

    idx = jnp.arange(1024, dtype=jnp.int32)
    tile, spot = idx // 128, idx % 128
    lane = lax.axis_index("yl")
    place = jnp.where(tile < 4, 2 * tile + lane, 2 * tile + 1 - lane)
    cosine, sine = rotary(place * 128 + spot, head)

    cut = lambda w, n: lax.dynamic_slice_in_dim(w, t * n, n, 1)
    d_s = down_weight.shape[0] // n_tp
    rows_d = lax.ppermute(
        lax.dynamic_slice_in_dim(down_weight, t * d_s, d_s, 0),
        TP + FS,
        [(a * n_fs + b, b * n_fs + a) for a in range(n_tp) for b in range(n_fs)],
    )
    tok = tokens.reshape(2, 64, width)
    cot = cotangent.reshape(2, 64, width)
    gain_q, gain_k = gain_query.reshape(1, -1), gain_key.reshape(1, -1)
    h, w_qkv, query_b, kv, kv_far, raw, attended, g, w_out, w_gate, y_mid, h2_own = ahead(
        tok,
        gain_in.reshape(1, -1),
        jnp.concatenate([cut(query_weight, qc), cut(key_weight, kc), cut(value_weight, kc)], 1),
        cosine,
        sine,
        gain_q,
        gain_k,
        cot,
        lax.dynamic_slice_in_dim(out_weight, lax.axis_index("core") * 128, 128, 0),
        cut(gate_weight, fc),
        gain_mid.reshape(1, -1),
    )
    h2, dgate_b, dup_b, mixed_part, grad_mid, dz_own, d_tok, term_mid, down_mine = mlp(
        h2_own,
        cut(up_weight, fc),
        rows_d,
        w_gate,
        g,
        w_out.reshape(32, 64, width),
        y_mid,
        cot,
        gain_mid.reshape(1, -1),
    )
    mixed, tokens_grad, cols_gu, cols_qkv, late, terms = behind(
        query_b,
        kv,
        kv_far,
        cosine,
        sine,
        gain_q,
        gain_k,
        d_tok,
        dz_own,
        attended,
        tok,
        gain_in.reshape(1, -1),
        term_mid,
        down_mine,
        raw,
        w_qkv,
        grad_mid,
        y_mid,
        h2,
        dgate_b,
        dup_b,
        mixed_part,
        h,
    )

    def take(part, at, n):
        return part[:, :, at : at + n].transpose(1, 0, 2).astype(F32).reshape(-1, n_tp * n)

    late = late.astype(F32)
    return (
        mixed.reshape(tokens.shape),
        tokens_grad.reshape(tokens.shape),
        terms[0],
        take(cols_qkv, 0, qc),
        take(cols_qkv, qc, kc),
        take(cols_qkv, qc + kc, kc),
        terms[4, :head],
        terms[5, :head],
        late[48:],
        terms[2],
        take(cols_gu, 0, fc),
        take(cols_gu, fc, fc),
        late[:48],
    )


def solution(mesh):
    fine = Mesh(mesh.devices.reshape(4, 2, 2, 4, 2), ALL)
    ctx, fsdp = ("z", "yl", "core"), FS
    act = P(fsdp, None, ctx, None, None)
    weight = P(fsdp, None)
    grad = P(ctx + fsdp, None)
    placed = (
        act, P(), weight, weight, weight, P(), P(), weight, P(), weight, weight, weight, act,
    )
    return jax.shard_map(
        shards,
        mesh=fine,
        in_specs=placed,
        out_specs=(act, act, P(), grad, grad, grad, P(), P(), grad, P(), grad, grad, grad),
        check_vma=False,
    )
```

```python
import functools

import jax
import jax.numpy as jnp
import numpy as np
from jax import lax
from jax.experimental import pallas as pl
from jax.experimental.pallas import tpu as pltpu
from jax.sharding import Mesh, PartitionSpec as P

EPS = 1e-06
THETA = 1000000.0
BF = jnp.bfloat16
F32 = jnp.float32
TP = ("z", "core")
FS = ("x", "yh")
DP = ("yl", "x", "yh")
ALL = ("z", "yl", "core", "x", "yh")
MESH = pl.DeviceIdType.MESH
VMEM = pl.BlockSpec(memory_space=pltpu.VMEM)
HBM = pl.BlockSpec(memory_space=pl.ANY)
MB = 2**20
LOG2E = 1.4426950408889634


class Place:
    def __init__(self):
        self.z, self.yl, self.core, self.x, self.yh = (lax.axis_index(a) for a in ALL)
        self.t = 2 * self.z + self.core
        self.shard = 2 * self.x + self.yh
        self.y = 2 * self.yh + self.yl

    def at(self, z=None, yl=None, core=None, x=None, yh=None):
        here = (self.z, self.yl, self.core, self.x, self.yh)
        return tuple(h if n is None else n for h, n in zip(here, (z, yl, core, x, yh)))

    def up(self, n):
        return lax.rem(self.z + n, 4)

    def east(self, n):
        return lax.rem(self.x + n, 4)

    def north(self, n):
        y = lax.rem(self.y + n, 4)
        return self.at(yh=y // 2, yl=lax.rem(y, 2))

    def peers(self, which):
        table = {
            "z": [self.at(z=self.up(1)), self.at(z=self.up(3))],
            "sib": [self.at(core=1 - self.core)],
            "x": [self.at(x=self.east(1)), self.at(x=self.east(3))],
            "cross": [self.at(yl=1 - self.yl, yh=1 - self.yh)],
            "pair": [self.at(yl=1 - self.yl)],
            "plane": [self.at(x=self.east(d)) for d in (1, 2, 3)]
            + [self.north(d) for d in (1, 2, 3)],
            "swap": [self.at(yl=1 - self.yl, core=1 - self.core)],
            "tp": [
                self.at(z=self.up(dz), core=lax.rem(self.core + dc, 2))
                for dz in range(4)
                for dc in range(2)
                if dz or dc
            ],
        }
        return [p for name in which for p in table[name]]


class Wire:
    def __init__(self, send_sem, recv_sem, here_sem):
        self.send_sem, self.recv_sem, self.here_sem = send_sem, recv_sem, here_sem
        self.n = self.m = 0
        self.sent = []

    def send(self, src, dst, peer):
        copy = pltpu.make_async_remote_copy(
            src_ref=src,
            dst_ref=dst,
            send_sem=self.send_sem.at[self.n],
            recv_sem=self.recv_sem.at[self.n],
            device_id=peer,
            device_id_type=MESH,
        )
        self.n += 1
        assert self.n <= self.send_sem.shape[0]
        copy.start()
        self.sent.append(copy)
        return copy

    def here(self, src, dst):
        copy = pltpu.make_async_copy(src, dst, self.here_sem.at[self.m])
        self.m += 1
        assert self.m <= self.here_sem.shape[0]
        copy.start()
        return copy

    def settle(self, copies):
        for copy in copies:
            copy.wait_send()
        self.sent = [one for one in self.sent if all(one is not copy for copy in copies)]

    def finish(self):
        for copy in self.sent:
            copy.wait_send()


def sems(n, m):
    return [
        pltpu.SemaphoreType.DMA((n,)),
        pltpu.SemaphoreType.DMA((n,)),
        pltpu.SemaphoreType.DMA((m,)),
    ]


def meet(peers):
    barrier = pltpu.get_barrier_semaphore()
    for peer in peers:
        pl.semaphore_signal(barrier, inc=1, device_id=peer, device_id_type=MESH)
    pl.semaphore_wait(barrier, len(peers))


def run(*tasks):
    tasks = list(tasks)
    while tasks:
        advance(tasks)


def advance(tasks):
    for task in list(tasks):
        try:
            next(task)
        except StopIteration:
            tasks.remove(task)


def gather_z(w, p, own, dst):
    up, down, sib = p.at(z=p.up(1)), p.at(z=p.up(3)), p.at(core=1 - p.core)
    before, after, far = (2 * p.up(n) + p.core for n in (3, 1, 2))
    u0 = w.send(own(0), dst(p.t, 0), up)
    d1 = w.send(own(1), dst(p.t, 1), down)
    u1 = w.send(own(1), dst(p.t, 1), up)
    d0 = w.send(own(0), dst(p.t, 0), down)
    s = [w.send(own(k), dst(p.t, k), sib) for k in (0, 1)]

    def on(t, k):
        s.append(w.send(dst(t, k), dst(t, k), sib))

    yield
    for copy in s[:2]:
        copy.wait_recv()
    yield
    u0.wait_recv()
    f0 = w.send(dst(before, 0), dst(before, 0), up)
    on(before, 0)
    d1.wait_recv()
    f1 = w.send(dst(after, 1), dst(after, 1), down)
    on(after, 1)
    yield
    u1.wait_recv()
    on(before, 1)
    d0.wait_recv()
    on(after, 0)
    yield
    for copy in s[2:6]:
        copy.wait_recv()
    yield
    f0.wait_recv()
    on(far, 0)
    f1.wait_recv()
    on(far, 1)
    yield
    for copy in s[6:]:
        copy.wait_recv()
    w.settle([u0, d1, u1, d0, f0, f1] + s)


def gather_yx(w, p, dst, n):
    east, west = p.at(x=p.east(1)), p.at(x=p.east(3))
    cross, pair = p.at(yl=1 - p.yl, yh=1 - p.yh), p.at(yl=1 - p.yl)
    half = n // 2
    me, flip = p.shard, 1 - 2 * p.yh
    west_s, east_s, far_s = (2 * p.east(k) + p.yh for k in (3, 1, 2))
    mine = p.yl * half
    other = half - mine

    def one(s, at, peer):
        return w.send(dst(s, at, half), dst(s, at, half), peer)

    c0 = one(me, mine, cross)
    e0 = one(me, 0, east)
    w1 = one(me, half, west)
    e1 = one(me, half, east)
    w0 = one(me, 0, west)
    yield
    c0.wait_recv()
    a0 = one(me + flip, other, pair)
    e0.wait_recv()
    f0 = one(west_s, 0, east)
    w1.wait_recv()
    f1 = one(east_s, half, west)
    yield
    a0.wait_recv()
    g0 = one(me + flip, 0, east)
    h1 = one(me + flip, half, west)
    g1 = one(me + flip, half, east)
    h0 = one(me + flip, 0, west)
    yield
    for copy in (e1, w0, f0, f1):
        copy.wait_recv()
    g0.wait_recv()
    i0 = one(west_s + flip, 0, east)
    h1.wait_recv()
    i1 = one(east_s + flip, half, west)
    yield
    for copy in (g1, h0, i0, i1):
        copy.wait_recv()


def gather_xy(w, p, dst, n, ready=None):
    east, west = p.at(x=p.east(1)), p.at(x=p.east(3))
    cross, pair = p.at(yl=1 - p.yl, yh=1 - p.yh), p.at(yl=1 - p.yl)
    half = n // 2
    me = p.shard
    west_s, east_s, far_s = (2 * p.east(k) + p.yh for k in (3, 1, 2))
    mine = p.yl * half
    other = half - mine
    flip = 1 - 2 * p.yh

    def one(s, at, peer):
        return w.send(dst(s, at, half), dst(s, at, half), peer)

    def along(s):
        return one(s + flip, other, pair)

    e0 = one(me, mine, east)
    w0 = one(me, mine, west)
    c0 = one(me, mine, cross)
    w1 = one(me, other, west)
    yield
    e0.wait_recv()
    fe = one(west_s, mine, east)
    c1 = one(west_s, mine, cross)
    e1 = one(me, other, east)
    w0.wait_recv()
    c2 = one(east_s, mine, cross)
    c0.wait_recv()
    a0 = along(me)
    yield
    fe.wait_recv()
    c3 = one(far_s, mine, cross)
    w1.wait_recv()
    fw = one(east_s, other, west)
    if ready:
        ready(east_s)
    yield
    c1.wait_recv()
    a1 = along(west_s)
    e1.wait_recv()
    if ready:
        ready(west_s)
    c2.wait_recv()
    a2 = along(east_s)
    yield
    fw.wait_recv()
    if ready:
        ready(far_s)
    c3.wait_recv()
    a3 = along(far_s)
    yield
    for s, a in ((me, a0), (west_s, a1), (east_s, a2), (far_s, a3)):
        a.wait_recv()
        if ready:
            ready(s + flip)


def norm_rope(raw, gain, cosine, sine):
    unit = raw * lax.rsqrt(jnp.mean(raw * raw, -1, keepdims=True) + EPS)
    vals = unit * gain
    return vals * cosine + pltpu.roll(vals, 64, 1) * sine


SCALE = 128**-0.5 * LOG2E


def dot_t(a, b):
    return lax.dot_general(a, b, (((1,), (1,)), ((), ())), preferred_element_type=F32)


def t_dot(a, b):
    return lax.dot_general(a, b, (((0,), (0,)), ((), ())), preferred_element_type=F32)


def both(ref, at):
    return jnp.concatenate([ref[at, 0:128], ref[at, 128:256]], 0)


def weights_of(q, k, j, edge):
    s = jnp.exp2(dot_t(q, k) * SCALE)
    last = jnp.where(edge, s[:, j * 128 :], 0.0)
    return last if j == 0 else jnp.concatenate([s[:, : j * 128], last], 1)


def edges(p, j):
    row = lax.broadcasted_iota(jnp.int32, (256, 128), 0) % 128
    col = lax.broadcasted_iota(jnp.int32, (256, 128), 1)
    seen = (p.yl if j < 4 else 1 - p.yl) * 128
    return col <= row, col < seen


def shard_rows(ref, n):
    return lambda s, at, m: ref.at[pl.ds(pl.multiple_of(s * n + at, 16), m)]


def ahead_kernel(
    tok, gain, w_own, cosine, sine, gq, gk, cot, wo, gate_own, up_own, gain_mid,
    h_out, qkv_out, q_out, kv_out, kv_far_out, raw_out, o_out, g_out, out_out, gate_out, up_out,
    y1_out, h2, q, kv, kv_far, raw, o, y1, h, w_qkv, g, w_out, w_gate, w_up, o_tok, send_sem, recv_sem, here_sem
):
    p = Place()
    w = Wire(send_sem, recv_sem, here_sem)
    w_qkv[pl.ds(pl.multiple_of(p.shard * 256, 256), 256)] = w_own[...]
    for k in (0, 1):
        x = tok[k].astype(F32)
        unit = x * lax.rsqrt(jnp.mean(x * x, -1, keepdims=True) + EPS)
        h[p.t if k == 0 else 15 - p.t] = (unit * gain[...]).astype(BF)
    meet(p.peers(("tp", "x", "cross", "pair")))
    pair, sib = p.at(yl=1 - p.yl), p.at(core=1 - p.core)

    def block_of(ref):
        return lambda t, k: ref.at[t if k == 0 else 15 - t]

    def part_out(s, at, n):
        return w_out.at[s, p.core, pl.ds(pl.multiple_of(at, 64), n)]

    twin = []

    def ready(s):
        twin.append(w.send(w_out.at[s, p.core], w_out.at[s, p.core], sib))

    at_h, at_g = block_of(h), block_of(g)
    task_h = [gather_z(w, p, lambda k: at_h(p.t, k), at_h)]
    task_qkv = [gather_xy(w, p, shard_rows(w_qkv, 256), 256)]
    advance(task_qkv)
    advance(task_h)
    w_out[p.shard, p.core] = wo[...]
    g[p.t] = cot[0]
    g[15 - p.t] = cot[1]
    w_gate[pl.ds(pl.multiple_of(p.shard * 256, 256), 256)] = gate_own[...]
    w_up[pl.ds(pl.multiple_of(p.shard * 256, 256), 256)] = up_own[...]
    task_up = [gather_xy(w, p, shard_rows(w_up, 256), 256)]
    task_out = [gather_xy(w, p, part_out, 128, ready)]
    task_gate = [gather_yx(w, p, shard_rows(w_gate, 256), 256)]
    task_g = [gather_z(w, p, lambda k: at_g(p.t, k), at_g)]
    ready(p.shard)
    advance(task_h)
    advance(task_qkv)
    advance(task_h)
    advance(task_qkv)
    advance(task_out)
    advance(task_qkv)
    advance(task_h)
    advance(task_qkv)
    advance(task_h)
    advance(task_h)
    advance(task_qkv)
    advance(task_out)
    advance(task_gate)
    advance(task_g)
    run(*task_h)
    kept = [w.here(h, h_out), w.here(w_qkv, qkv_out)]
    swaps = []
    for j in range(4):
        at = pl.ds(j * 256, 256)
        out = jnp.dot(
            h[4 * j : 4 * j + 4].reshape(256, 2048), w_qkv[...], preferred_element_type=F32
        )
        cos, sin = cosine[at], sine[at]
        kv[at, 0:128] = norm_rope(out[:, 256:384], gk[...], cos, sin).astype(BF)
        kv[at, 128:256] = out[:, 384:].astype(BF)
        swaps.append(w.send(kv.at[at], kv_far.at[at], pair))
        for n in (0, 1):
            cols = slice(n * 128, n * 128 + 128)
            q[at, cols] = norm_rope(out[:, cols], gq[...], cos, sin).astype(BF)
        raw[at] = out[:, :384]
        if j == 0:
            advance(task_out)
        if j == 1:
            advance(task_g)
            advance(task_gate)
        if j == 2:
            advance(task_up)
        if j == 3:
            advance(task_out)
            advance(task_g)
    for j in range(8):
        at = pl.ds(j * 128, 128)
        keys = pl.ds(0, j * 128 + 128)
        if j % 2 == 0:
            swaps[j // 2].wait_recv()
        tri, seen = edges(p, j)
        qj = both(q, at)
        near = weights_of(qj, kv[keys, 0:128], j, tri)
        far = weights_of(qj, kv_far[keys, 0:128], j, seen)
        total = jnp.sum(near, -1, keepdims=True) + jnp.sum(far, -1, keepdims=True)
        out = jnp.dot(near.astype(BF), kv[keys, 128:256], preferred_element_type=F32)
        out += jnp.dot(far.astype(BF), kv_far[keys, 128:256], preferred_element_type=F32)
        out = (out / total).astype(BF)
        for n in (0, 1):
            o[2 * j : 2 * j + 2, :, n * 128 : n * 128 + 128] = out[
                n * 128 : n * 128 + 128
            ].reshape(2, 64, 128)
        if j == 1:
            advance(task_gate)
        if j == 2:
            advance(task_g)
            advance(task_g)
        if j == 3:
            advance(task_up)
        if j == 4:
            advance(task_out)
            advance(task_g)
        if j == 5:
            advance(task_gate)
        if j == 7:
            advance(task_up)
    spread = []
    for dz in (2, 1, 3, 0):
        for dc in range(2):
            z, core = p.up(dz), lax.rem(p.core + dc, 2)
            t = 2 * z + core
            for k in (0, 1):
                src = o.at[t if k == 0 else 15 - t]
                if dz or dc:
                    spread.append(w.send(src, o_tok.at[p.t, k], p.at(z=z, core=core)))
                else:
                    o_tok[p.t, k] = o[t if k == 0 else 15 - t]
    kept += [
        w.here(q, q_out),
        w.here(kv, kv_out),
        w.here(kv_far, kv_far_out),
        w.here(raw, raw_out),
        w.here(o, o_out),
    ]
    run(*task_g)
    kept.append(w.here(g, g_out))
    advance(task_up)
    run(*task_out)
    run(*task_gate)
    kept.append(w.here(w_gate, gate_out))
    advance(task_up)
    for copy in twin:
        copy.wait_recv()
    kept.append(w.here(w_out, out_out))
    for copy in spread:
        copy.wait_recv()
    for n in range(4):
        cols = slice(n * 512, n * 512 + 512)
        for k in (0, 1):
            y1[k, :, cols] = tok[k, :, cols].astype(F32)
        for t in range(8):
            part = jnp.dot(
                o_tok[t].reshape(128, 256),
                w_out[t, :, :, cols].reshape(256, 512),
                preferred_element_type=F32,
            )
            for k in (0, 1):
                y1[k, :, cols] += part[k * 64 : k * 64 + 64]
    for k in (0, 1):
        y = y1[k]
        unit = y * lax.rsqrt(jnp.mean(y * y, -1, keepdims=True) + EPS)
        h2[k] = (unit * gain_mid[...]).astype(BF)
    kept.append(w.here(y1, y1_out))
    run(*task_up)
    kept.append(w.here(w_up, up_out))
    w.finish()
    for copy in kept:
        copy.wait()


def ahead(*args):
    sds = jax.ShapeDtypeStruct
    return pl.pallas_call(
        ahead_kernel,
        out_shape=(
            sds((16, 64, 2048), BF),
            sds((2048, 512), BF),
            sds((1024, 256), BF),
            sds((1024, 256), BF),
            sds((1024, 256), BF),
            sds((1024, 384), F32),
            sds((16, 64, 256), BF),
            sds((16, 64, 2048), BF),
            sds((8, 2, 128, 2048), BF),
            sds((2048, 768), BF),
            sds((2048, 768), BF),
            sds((2, 64, 2048), F32),
            sds((2, 64, 2048), BF),
        ),
        in_specs=[VMEM] * 12,
        out_specs=[HBM] * 12 + [VMEM],
        scratch_shapes=[
            pltpu.VMEM((1024, 256), BF),
            pltpu.VMEM((1024, 256), BF),
            pltpu.VMEM((1024, 256), BF),
            pltpu.VMEM((1024, 384), F32),
            pltpu.VMEM((16, 64, 256), BF),
            pltpu.VMEM((2, 64, 2048), F32),
            pltpu.VMEM((16, 64, 2048), BF),
            pltpu.VMEM((2048, 512), BF),
            pltpu.VMEM((16, 64, 2048), BF),
            pltpu.VMEM((8, 2, 128, 2048), BF),
            pltpu.VMEM((2048, 768), BF),
            pltpu.VMEM((2048, 768), BF),
            pltpu.VMEM((8, 2, 64, 256), BF),
        ]
        + sems(160, 16),
        compiler_params=pltpu.CompilerParams(
            collective_id=0, has_side_effects=True, vmem_limit_bytes=56 * MB
        ),
        name="ahead",
    )(*args)


def rows_of(ref, zz):
    c = ref.shape[-1]
    return jnp.concatenate(
        [ref[pl.ds(2 * zz, 2)].reshape(128, c), ref[pl.ds(14 - 2 * zz, 2)].reshape(128, c)], 0
    )


def put(ref, zz, val):
    c = ref.shape[-1]
    ref[pl.ds(2 * zz, 2)] = val[:128].reshape(2, 64, c)
    ref[pl.ds(14 - 2 * zz, 2)] = val[128:].reshape(2, 64, c)


def add(*vals):
    total = vals[0].astype(F32)
    for val in vals[1:]:
        total = total + val.astype(F32)
    return total


def z_room():
    return [
        pltpu.VMEM((4, 2, 64, 2048), BF),
        pltpu.VMEM((2, 64, 2048), BF),
        pltpu.VMEM((2, 2, 64, 2048), BF),
    ]


def reduce_z(w, p, part, room, out):
    mine, relay, last = room
    near = mine
    up, down, sib = p.at(z=p.up(1)), p.at(z=p.up(3)), p.at(core=1 - p.core)

    def block(n, core, k):
        t = 2 * p.up(n) + core
        return t if k == 0 else 15 - t

    first = {}

    def give(n):
        for k in (0, 1):
            first[n, k] = w.send(part.at[block(n, 1 - p.core, k)], near.at[n, k], sib)

    def fold(n, k):
        first[n, k].wait_recv()
        mine[n, k] = add(part[block(n, p.core, k)], near[n, k]).astype(BF)

    give(2)
    yield
    give(1)
    fold(2, 0)
    e0 = w.send(mine.at[2, 0], relay.at[0], up)
    fold(2, 1)
    e1 = w.send(mine.at[2, 1], relay.at[1], down)
    yield
    give(3)
    fold(1, 1)
    a1 = w.send(mine.at[1, 1], last.at[0, 1], up)
    fold(1, 0)
    yield
    give(0)
    fold(3, 0)
    b0 = w.send(mine.at[3, 0], last.at[1, 0], down)
    fold(3, 1)
    yield
    e0.wait_recv()
    mine[1, 0] = add(mine[1, 0], relay[0]).astype(BF)
    a0 = w.send(mine.at[1, 0], last.at[0, 0], up)
    e1.wait_recv()
    mine[3, 1] = add(mine[3, 1], relay[1]).astype(BF)
    b1 = w.send(mine.at[3, 1], last.at[1, 1], down)
    fold(0, 0)
    fold(0, 1)
    w.settle(list(first.values()))
    yield
    for k, (a, b) in enumerate(((a0, b0), (a1, b1))):
        a.wait_recv()
        b.wait_recv()
        out[k] = add(mine[0, k], last[0, k], last[1, k])


def xy_room(rows, cols, left=None):
    left = left or cols // 2
    return [
        pltpu.VMEM(lead + (rows, n), BF)
        for n in (left, cols - left)
        for lead in ((4,), (2, 4), (4,), (3,))
    ]


def put_half(out, cols, val):
    if len(out.shape) == 3:
        out[:, :, cols] = val.reshape(out.shape[0], out.shape[1], val.shape[1])
    else:
        out[:, cols] = val


def reduce_xy(w, p, part, room, out):
    ra, ta, sa, fa, rb, tb, sb, fb = room
    n_left = sa.shape[2]
    left, right = pl.ds(0, n_left), pl.ds(n_left, part.shape[3] - n_left)
    low, high = pl.ds(0, 2), pl.ds(2, 2)
    spans = (1, 2, 3)
    easts = [p.at(x=p.east(d)) for d in spans]
    norths = [p.north(d) for d in spans]
    xs = [p.east(d) for d in spans]
    ys = [lax.rem(p.y + d, 4) for d in spans]

    def start(bundle, r, t, peers):
        return [
            w.send(bundle(1, low), r.at[low], peers[0]),
            w.send(bundle(1, high), r.at[high], peers[2]),
            w.send(bundle(0, high), t.at[0, high], peers[0]),
            w.send(bundle(2, low), t.at[1, low], peers[2]),
        ]

    def of_x(d, some):
        return part.at[xs[d], some, :, left]

    def of_y(d, some):
        return part.at[some, ys[d], :, right]

    ca = start(of_x, ra, ta, easts)
    yield
    cb = start(of_y, rb, tb, norths)
    yield
    ca[0].wait_recv()
    for k in (0, 1):
        ra[k] = add(ra[k], part[xs[0], k, :, left]).astype(BF)
    ca.append(w.send(ra.at[low], ta.at[0, low], easts[0]))
    ca[1].wait_recv()
    for k in (2, 3):
        ra[k] = add(ra[k], part[xs[2], k, :, left]).astype(BF)
    ca.append(w.send(ra.at[high], ta.at[1, high], easts[2]))
    yield
    cb[0].wait_recv()
    for k in (0, 1):
        rb[k] = add(rb[k], part[k, ys[0], :, right]).astype(BF)
    cb.append(w.send(rb.at[low], tb.at[0, low], norths[0]))
    cb[1].wait_recv()
    for k in (2, 3):
        rb[k] = add(rb[k], part[k, ys[2], :, right]).astype(BF)
    cb.append(w.send(rb.at[high], tb.at[1, high], norths[2]))
    yield
    for copy in ca[2:]:
        copy.wait_recv()

    @pl.loop(0, 4)
    def _(y):
        sa[y] = add(part[p.x, y, :, left], ta[0, y], ta[1, y]).astype(BF)

    da = [w.send(sa.at[lax.rem(p.y + d, 4)], fa.at[d - 1], norths[d - 1]) for d in spans]
    yield
    for copy in cb[2:]:
        copy.wait_recv()

    @pl.loop(0, 4)
    def _(x):
        sb[x] = add(part[x, p.y, :, right], tb[0, x], tb[1, x]).astype(BF)

    db = [w.send(sb.at[p.east(d)], fb.at[d - 1], easts[d - 1]) for d in spans]
    yield
    for copy in da:
        copy.wait_recv()
    put_half(out, left, add(sa[p.y], fa[0], fa[1], fa[2]).astype(BF))
    yield
    for copy in db:
        copy.wait_recv()
    put_half(out, right, add(sb[p.x], fb[0], fb[1], fb[2]).astype(BF))


def mlp_kernel(
    h2_own, down_own, gate_hbm, up_hbm, g_hbm, out_hbm, y1, cot, gain,
    h2_out, dgate_out, dup_out, mixed_out, grad_mid, dz, d_tok, term, down_mine,
    h2, w_gate, w_up, w_down, g, gate, upper, part, down_part, act, dgate, dup, mixed, *rest
):
    zr, xr, (send_sem, recv_sem, here_sem) = rest[:3], rest[3:11], rest[11:]
    p = Place()
    w = Wire(send_sem, recv_sem, here_sem)
    loads = [w.here(gate_hbm, w_gate), w.here(up_hbm, w_up), w.here(g_hbm, g)]
    h2[p.t] = h2_own[0]
    h2[15 - p.t] = h2_own[1]
    w_down[pl.ds(pl.multiple_of(p.shard * 96, 96), 96)] = down_own[...]
    meet(p.peers(("z", "sib", "x", "plane", "cross")))

    def block(t, k):
        return h2.at[t if k == 0 else 15 - t]

    task_h = [gather_z(w, p, lambda k: block(p.t, k), block)]
    task_down = [gather_xy(w, p, shard_rows(w_down, 96), 96)]
    def forward(zz):
        left = rows_of(h2, zz)
        gate_n = jnp.dot(left, w_gate[...], preferred_element_type=F32)
        up_n = jnp.dot(left, w_up[...], preferred_element_type=F32)
        gate[zz] = gate_n
        upper[zz] = up_n
        put(act, zz, (gate_n * jax.nn.sigmoid(gate_n) * up_n).astype(BF))

    advance(task_h)
    advance(task_down)
    advance(task_h)
    for copy in loads:
        copy.wait()
    forward(p.z)
    advance(task_down)
    advance(task_h)
    advance(task_down)
    advance(task_h)
    advance(task_h)
    advance(task_down)
    forward(p.up(3))
    advance(task_h)
    forward(p.up(1))
    advance(task_down)
    run(*task_h)
    kept = [w.here(h2, h2_out)]
    forward(p.up(2))
    kept[0].wait()
    load = w.here(out_hbm.at[pl.ds(0, 16)], h2)

    @pl.loop(0, 6)
    def _(i):
        cols = pl.ds(pl.multiple_of(i * 128, 128), 128)
        left = act[:, :, cols].reshape(1024, 128)
        out = t_dot(left, g[...].reshape(1024, 2048)).astype(BF)
        for k in range(8):
            row = i * 8 + k
            piece = row // 3
            f = lax.rem(piece, 8)
            down_part[f // 2, 2 * lax.rem(f, 2) + piece // 8, pl.ds(pl.multiple_of(lax.rem(row, 3) * 16, 16), 16)] = out[
                k * 16 : k * 16 + 16
            ]

    run(*task_down)
    task_sum = [reduce_z(w, p, part, zr, grad_mid)]
    task_late = [reduce_xy(w, p, down_part, xr, down_mine)]
    advance(task_late)
    advance(task_late)
    for n in (2, 1, 3, 0):
        zz = p.up(n)
        gate_n, up_n = gate[zz], upper[zz]
        sig = jax.nn.sigmoid(gate_n)
        da = dot_t(rows_of(g, zz), w_down[...])
        silu = gate_n * sig
        d_gate = (da * up_n * sig * (1.0 + gate_n * (1.0 - sig))).astype(BF)
        d_up = (da * silu).astype(BF)
        put(dgate, zz, d_gate)
        put(dup, zz, d_up)
        total = dot_t(d_gate, w_gate[...]) + dot_t(d_up, w_up[...])
        put(part, zz, total.astype(BF))
        advance(task_sum)
        if n == 3:
            advance(task_late)
            advance(task_late)
    load2 = w.here(out_hbm.at[pl.ds(16, 16)], g)
    kept += [w.here(dgate, dgate_out), w.here(dup, dup_out)]
    advance(task_sum)

    @pl.loop(0, 4)
    def _(n):
        out = jnp.dot(rows_of(act, n), w_down[...], preferred_element_type=F32)
        put(mixed, n, out.astype(BF))

    kept.append(w.here(mixed, mixed_out))
    advance(task_late)
    run(*task_sum)
    advance(task_late)
    load.wait()
    load2.wait()
    term[...] = jnp.zeros_like(term)
    for k in (0, 1):
        y = y1[k]
        scale = lax.rsqrt(jnp.mean(y * y, -1, keepdims=True) + EPS)
        unit = y * scale
        dh = grad_mid[k]
        term[...] += jnp.sum(dh * unit, 0, keepdims=True)
        wv = dh * gain[...]
        dy = cot[k].astype(F32) + scale * (wv - unit * jnp.mean(wv * unit, -1, keepdims=True))
        grad_mid[k] = dy
        dz[k] = dy.astype(BF)
    dz_rows = dz[...].reshape(128, 2048)
    for t in range(8):
        half = h2 if t < 4 else g
        out = dot_t(dz_rows, half[4 * (t % 4) : 4 * (t % 4) + 4].reshape(256, 2048)).astype(BF)
        d_tok[t] = out.reshape(2, 64, 256)
    run(*task_late)
    w.finish()
    for copy in kept[1:]:
        copy.wait()


def mlp(*args):
    sds = jax.ShapeDtypeStruct
    return pl.pallas_call(
        mlp_kernel,
        out_shape=(
            sds((16, 64, 2048), BF),
            sds((16, 64, 768), BF),
            sds((16, 64, 768), BF),
            sds((16, 64, 2048), BF),
            sds((2, 64, 2048), F32),
            sds((2, 64, 2048), BF),
            sds((8, 2, 64, 256), BF),
            sds((1, 2048), F32),
            sds((48, 2048), BF),
        ),
        in_specs=[VMEM] * 2 + [HBM] * 4 + [VMEM] * 3,
        out_specs=[HBM] * 4 + [VMEM] * 5,
        scratch_shapes=[
            pltpu.VMEM((16, 64, 2048), BF),
            pltpu.VMEM((2048, 768), BF),
            pltpu.VMEM((2048, 768), BF),
            pltpu.VMEM((768, 2048), BF),
            pltpu.VMEM((16, 64, 2048), BF),
            pltpu.VMEM((4, 256, 768), F32),
            pltpu.VMEM((4, 256, 768), F32),
            pltpu.VMEM((16, 64, 2048), BF),
            pltpu.VMEM((4, 4, 48, 2048), BF),
            pltpu.VMEM((16, 64, 768), BF),
            pltpu.VMEM((16, 64, 768), BF),
            pltpu.VMEM((16, 64, 768), BF),
            pltpu.VMEM((16, 64, 2048), BF),
        ]
        + z_room()
        + xy_room(48, 2048)
        + sems(96, 12),
        compiler_params=pltpu.CompilerParams(
            collective_id=2, has_side_effects=True, vmem_limit_bytes=63 * MB
        ),
        name="mlp",
    )(*args)


def sum_all(w, p, vec, slots, out):
    ra, rb, rc = slots
    ra[p.t] = vec[...]
    first = [w.send(ra.at[p.t], ra.at[p.t], peer) for peer in p.peers(("tp",))]
    yield
    for copy in first:
        copy.wait_recv()
    rb[p.x] = sum((ra[i] for i in range(1, 8)), ra[0])
    xs = [w.send(rb.at[p.x], rb.at[p.x], p.at(x=p.east(d))) for d in (1, 2, 3)]
    yield
    for copy in xs:
        copy.wait_recv()
    rc[p.y] = sum((rb[i] for i in range(1, 4)), rb[0])
    ys = [w.send(rc.at[p.y], rc.at[p.y], p.north(d)) for d in (1, 2, 3)]
    yield
    for copy in ys:
        copy.wait_recv()
    out[...] = sum((rc[i] for i in range(1, 4)), rc[0])


def deal(w, p, src, dst):
    dst[p.t] = src[p.t]
    copies = []
    for dz in (2, 1, 3, 0):
        for dc in range(2):
            if dz or dc:
                z, core = p.up(dz), lax.rem(p.core + dc, 2)
                copies.append(w.send(src.at[2 * z + core], dst.at[p.t], p.at(z=z, core=core)))
    return copies


def to_pieces(part, i, out, cols):
    z, yl = i // 2, lax.rem(i, 2)
    for r in range(16):
        core, f = r // 8, r % 8
        at = pl.ds(pl.multiple_of((2 * z + core) * 16, 16), 16)
        part[f // 2, 2 * (f % 2) + yl, at, cols] = out[r * 16 : r * 16 + 16]


def turn_norm_back(grad, raw, gain, cosine, sine):
    scale = lax.rsqrt(jnp.mean(raw * raw, -1, keepdims=True) + EPS)
    unit = raw * scale
    back = grad * cosine + pltpu.roll(grad * sine, 64, 1)
    term = jnp.sum(back * unit, 0, keepdims=True)
    back = back * gain
    return scale * (back - unit * jnp.mean(back * unit, -1, keepdims=True)), term


def behind_kernel(
    q, kv, kv_far, cosine, sine, gq, gk, d_tok, dz_own, o, tok, gain, term_mid, down_mine,
    raw_hbm, qkv_hbm, mid_hbm, y1_hbm, h2_hbm, dgate_hbm, dup_hbm, mixed_hbm, h_hbm,
    mixed, tokens_grad, g_gate, g_up, g_q, g_k, g_v, g_down, g_out, s_in, s_mid, s_q, s_k,
    mix_buf, dx_buf, cols_gu, cols_qkv, rows_out, vec_out, do, acc, acc_far, out_far, in_far, dz, big_x, big_y, dqkv, gu_part, qkv_part, out_part,
    gu_mine, qkv_mine, rows, vec, ra, rb, rc, dh, raw, w_qkv, grad_mid, y1, *rest
):
    mix_room, dh_room = rest[:3], rest[3:6]
    gu_room, qkv_room, out_room = rest[6:14], rest[14:22], rest[22:30]
    send_sem, recv_sem, here_sem = rest[30:]
    p = Place()
    w = Wire(send_sem, recv_sem, here_sem)
    loads = [
        w.here(h2_hbm, big_y),
        w.here(dgate_hbm, big_x.at[:, :, pl.ds(0, 768)]),
        w.here(dup_hbm, big_x.at[:, :, pl.ds(768, 768)]),
        w.here(raw_hbm, raw),
        w.here(qkv_hbm, w_qkv),
        w.here(mid_hbm, grad_mid),
        w.here(y1_hbm, y1),
    ]
    dz[p.t] = dz_own[0]
    dz[15 - p.t] = dz_own[1]
    vec[...] = jnp.zeros_like(vec)
    vec[2:3] = term_mid[...]
    rows[0:48] = down_mine[...]
    meet(p.peers(("tp", "plane", "swap")))
    pair = p.at(yl=1 - p.yl)
    spread = []
    for far in (2, 1, 3, 0):
        for dc in (0, 1):
            z, core = p.up(far), lax.rem(p.core + dc, 2)
            for k in (0, 1):
                if far or dc:
                    dst = do.at[p.t if k == 0 else 15 - p.t]
                    spread.append(w.send(d_tok.at[2 * z + core, k], dst, p.at(z=z, core=core)))
                else:
                    do[p.t if k == 0 else 15 - p.t] = d_tok[p.t, k]

    def block(t, k):
        return dz.at[t if k == 0 else 15 - t]

    task_dz = [gather_z(w, p, lambda k: block(p.t, k), block)]
    advance(task_dz)
    for copy in loads[:3]:
        copy.wait()

    def grad_gu(i):
        cols = pl.ds(pl.multiple_of(i * 256, 256), 256)
        left = big_y[:, :, cols].reshape(1024, 256)
        for n in (0, 1):
            at = slice(n * 768, n * 768 + 768)
            to_pieces(gu_part, i, t_dot(left, big_x[:, :, at].reshape(1024, 768)).astype(BF), at)

    pl.loop(0, 8)(grad_gu)
    task_gu = [reduce_xy(w, p, gu_part, gu_room, gu_mine)]
    advance(task_gu)
    load = w.here(mixed_hbm, big_y)
    acc[...] = jnp.zeros_like(acc)
    acc_far[...] = jnp.zeros_like(acc_far)
    for copy in loads[3:]:
        copy.wait()
    for copy in spread:
        copy.wait_recv()
    back = []
    for j in range(7, -1, -1):
        at = pl.ds(j * 128, 128)
        keys = pl.ds(0, j * 128 + 128)
        tri, seen = edges(p, j)
        qj = both(q, at)
        dj = jnp.concatenate(
            [do[2 * j : 2 * j + 2, :, n * 128 : n * 128 + 128].reshape(128, 128) for n in (0, 1)], 0
        )
        near = weights_of(qj, kv[keys, 0:128], j, tri)
        far = weights_of(qj, kv_far[keys, 0:128], j, seen)
        scale = 1.0 / (jnp.sum(near, -1, keepdims=True) + jnp.sum(far, -1, keepdims=True))
        near = near * scale
        far = far * scale
        d_near = dot_t(dj, kv[keys, 128:256])
        d_far = dot_t(dj, kv_far[keys, 128:256])
        delta = jnp.sum(near * d_near, -1, keepdims=True) + jnp.sum(
            far * d_far, -1, keepdims=True
        )
        s_near = (near * (d_near - delta)).astype(BF)
        s_far = (far * (d_far - delta)).astype(BF)
        acc_far[keys, 0:128] += t_dot(s_far, qj)
        acc_far[keys, 128:256] += t_dot(far.astype(BF), dj)
        out_far[at, 0:128] = (acc_far[at, 0:128] * 128**-0.5).astype(BF)
        out_far[at, 128:256] = acc_far[at, 128:256].astype(BF)
        back.append((j, w.send(out_far.at[at], in_far.at[at], pair)))
        acc[keys, 0:128] += t_dot(s_near, qj)
        acc[keys, 128:256] += t_dot(near.astype(BF), dj)
        grad = jnp.dot(s_near, kv[keys, 0:128], preferred_element_type=F32)
        grad += jnp.dot(s_far, kv_far[keys, 0:128], preferred_element_type=F32)
        grad = (grad * 128**-0.5).astype(BF).astype(F32)
        for n in (0, 1):
            cols = slice(n * 128, n * 128 + 128)
            val, term = turn_norm_back(grad[cols], raw[at, cols], gq[...], cosine[at], sine[at])
            dqkv[2 * j : 2 * j + 2, :, cols] = val.astype(BF).reshape(2, 64, 128)
            vec[4:5, 0:128] += term
        if j in (7, 5, 3, 1, 0):
            advance(task_dz)
    advance(task_gu)
    advance(task_gu)
    run(*task_dz)
    for i in range(2):
        out = t_dot(
            o[:, :, i * 128 : i * 128 + 128].reshape(1024, 128), dz[...].reshape(1024, 2048)
        ).astype(BF)
        for f in range(8):
            out_part[f // 2, 2 * (f % 2) + i] = out[f * 16 : f * 16 + 16]
    load.wait()
    load = w.here(h_hbm, dz)
    task_out = [reduce_xy(w, p, out_part, out_room, rows.at[pl.ds(48, 16)])]
    advance(task_out)
    advance(task_out)
    for j, copy in back:
        at = pl.ds(j * 128, 128)
        copy.wait_recv()
        grad = add(acc[at, 0:128] * 128**-0.5, in_far[at, 0:128]).astype(BF).astype(F32)
        val, term = turn_norm_back(grad, raw[at, 256:384], gk[...], cosine[at], sine[at])
        dqkv[2 * j : 2 * j + 2, :, 256:384] = val.astype(BF).reshape(2, 64, 128)
        vec[5:6, 0:128] += term
        dv = add(acc[at, 128:256], in_far[at, 128:256]).astype(BF)
        dqkv[2 * j : 2 * j + 2, :, 384:512] = dv.reshape(2, 64, 128)
    task_dh = [reduce_z(w, p, big_x, dh_room, dh)]
    for n in (2, 1, 3, 0):
        zz = p.up(n)
        put(big_x, zz, dot_t(rows_of(dqkv, zz), w_qkv[...]).astype(BF))
        advance(task_dh)
    load.wait()

    def grad_qkv(i):
        cols = pl.ds(pl.multiple_of(i * 256, 256), 256)
        out = t_dot(dz[:, :, cols].reshape(1024, 256), dqkv[...].reshape(1024, 512))
        to_pieces(qkv_part, i, out.astype(BF), slice(0, 512))

    pl.loop(0, 8)(grad_qkv)
    task_qkv = [reduce_xy(w, p, qkv_part, qkv_room, qkv_mine)]
    advance(task_qkv)
    advance(task_qkv)
    advance(task_gu)
    advance(task_dh)
    advance(task_out)
    advance(task_out)
    advance(task_gu)
    run(*task_dh)
    total = jnp.zeros((1, 2048), F32)
    for k in (0, 1):
        x = tok[k].astype(F32)
        scale = lax.rsqrt(jnp.mean(x * x, -1, keepdims=True) + EPS)
        unit = x * scale
        total += jnp.sum(dh[k] * unit, 0, keepdims=True)
        wv = dh[k] * gain[...]
        dx = grad_mid[k] + scale * (wv - unit * jnp.mean(wv * unit, -1, keepdims=True))
        dx_buf[k] = dx.astype(BF)
    vec[0:1] = total
    task_vec = [sum_all(w, p, vec, (ra, rb, rc), vec_out)]
    task_mix = [reduce_z(w, p, big_y, mix_room, dh)]
    advance(task_vec)
    advance(task_qkv)
    advance(task_qkv)
    advance(task_gu)
    for _ in range(4):
        advance(task_mix)
    advance(task_out)
    advance(task_out)
    advance(task_vec)
    run(*task_gu)
    dealt = deal(w, p, gu_mine, cols_gu)
    advance(task_qkv)
    advance(task_qkv)
    advance(task_vec)
    advance(task_mix)
    run(*task_out)
    stay = p.yl == p.core
    n = w.n
    w.n += 1
    swap = pltpu.make_async_remote_copy(
        src_ref=rows,
        dst_ref=rows_out,
        send_sem=send_sem.at[n],
        recv_sem=recv_sem.at[n],
        device_id=p.at(yl=1 - p.yl, core=1 - p.core),
        device_id_type=MESH,
    )

    @pl.when(jnp.logical_not(stay))
    def _():
        swap.start()

    @pl.when(stay)
    def _():
        rows_out[...] = rows[...]

    run(*task_qkv)
    dealt += deal(w, p, qkv_mine, cols_qkv)
    run(*task_mix)
    for k in (0, 1):
        mix_buf[k] = (y1[k] + dh[k]).astype(BF)
    run(*task_vec)
    kept = [
        w.here(mix_buf, mixed),
        w.here(dx_buf, tokens_grad),
        w.here(vec_out.at[pl.ds(0, 1)], s_in),
        w.here(vec_out.at[pl.ds(2, 1)], s_mid),
        w.here(vec_out.at[pl.ds(4, 1), pl.ds(0, 128)], s_q),
        w.here(vec_out.at[pl.ds(5, 1), pl.ds(0, 128)], s_k),
    ]

    def place(first, at, val):
        end = at + val.shape[1]
        while at < end:
            stop = min(end, (at // 2048 + 1) * 2048)
            slot, begin = first + at // 2048, end - val.shape[1]
            grad_mid[slot // 4, slot % 4 * 16 : slot % 4 * 16 + 16, at % 2048 : (stop - 1) % 2048 + 1] = val[
                :, at - begin : stop - begin
            ].astype(F32)
            at = stop

    def piece(slot):
        return grad_mid.at[slot // 4, pl.ds(slot % 4 * 16, 16)]

    for copy in dealt[:7]:
        copy.wait_recv()
    for t in range(8):
        place(0, t * 768, cols_gu[t, :, 0:768])
        place(3, t * 768, cols_gu[t, :, 768:1536])
    for i in range(3):
        kept.append(w.here(piece(i), g_gate.at[:, pl.ds(i * 2048, 2048)]))
        kept.append(w.here(piece(3 + i), g_up.at[:, pl.ds(i * 2048, 2048)]))

    @pl.when(jnp.logical_not(stay))
    def _():
        swap.wait()

    y1[0] = rows_out[...].astype(F32)
    kept.append(w.here(y1.at[0, pl.ds(0, 48)], g_down))
    kept.append(w.here(y1.at[0, pl.ds(48, 16)], g_out))
    for copy in dealt[7:]:
        copy.wait_recv()
    for t in range(8):
        place(6, t * 256, cols_qkv[t, :, 0:256])
        place(7, t * 128, cols_qkv[t, :, 256:384])
        place(7, 1024 + t * 128, cols_qkv[t, :, 384:512])
    kept += [
        w.here(piece(6), g_q),
        w.here(grad_mid.at[1, pl.ds(48, 16), pl.ds(0, 1024)], g_k),
        w.here(grad_mid.at[1, pl.ds(48, 16), pl.ds(1024, 1024)], g_v),
    ]
    for copy in kept:
        copy.wait()
    w.finish()


def behind(*args):
    sds = jax.ShapeDtypeStruct
    return pl.pallas_call(
        behind_kernel,
        out_shape=(
            sds((2, 64, 2048), BF),
            sds((2, 64, 2048), BF),
            sds((16, 6144), F32),
            sds((16, 6144), F32),
            sds((16, 2048), F32),
            sds((16, 1024), F32),
            sds((16, 1024), F32),
            sds((48, 2048), F32),
            sds((16, 2048), F32),
            sds((1, 2048), F32),
            sds((1, 2048), F32),
            sds((1, 128), F32),
            sds((1, 128), F32),
        ),
        in_specs=[VMEM] * 14 + [HBM] * 9,
        out_specs=[HBM] * 13,
        scratch_shapes=[
            pltpu.VMEM((2, 64, 2048), BF),
            pltpu.VMEM((2, 64, 2048), BF),
            pltpu.VMEM((8, 16, 1536), BF),
            pltpu.VMEM((8, 16, 512), BF),
            pltpu.VMEM((64, 2048), BF),
            pltpu.VMEM((8, 2048), F32),
            pltpu.VMEM((16, 64, 256), BF),
            pltpu.VMEM((1024, 256), F32),
            pltpu.VMEM((1024, 256), F32),
            pltpu.VMEM((1024, 256), BF),
            pltpu.VMEM((1024, 256), BF),
            pltpu.VMEM((16, 64, 2048), BF),
            pltpu.VMEM((16, 64, 2048), BF),
            pltpu.VMEM((16, 64, 2048), BF),
            pltpu.VMEM((16, 64, 512), BF),
            pltpu.VMEM((4, 4, 128, 1536), BF),
            pltpu.VMEM((4, 4, 128, 512), BF),
            pltpu.VMEM((4, 4, 16, 2048), BF),
            pltpu.VMEM((8, 16, 1536), BF),
            pltpu.VMEM((8, 16, 512), BF),
            pltpu.VMEM((64, 2048), BF),
            pltpu.VMEM((8, 2048), F32),
            pltpu.VMEM((8, 8, 2048), F32),
            pltpu.VMEM((4, 8, 2048), F32),
            pltpu.VMEM((4, 8, 2048), F32),
            pltpu.VMEM((2, 64, 2048), F32),
            pltpu.VMEM((1024, 384), F32),
            pltpu.VMEM((2048, 512), BF),
            pltpu.VMEM((2, 64, 2048), F32),
            pltpu.VMEM((2, 64, 2048), F32),
        ]
        + z_room()
        + z_room()
        + xy_room(128, 1536, 1024)
        + xy_room(128, 512)
        + xy_room(16, 2048)
        + sems(160, 32),
        compiler_params=pltpu.CompilerParams(
            collective_id=1, has_side_effects=True, vmem_limit_bytes=63 * MB
        ),
        name="behind",
    )(*args)


def rotary(width):
    half = width // 2
    freq = np.float32(THETA) ** (-2.0 * np.arange(half, dtype=np.float32) / np.float32(width))
    row = np.arange(1024)
    tile = row // 128
    tables = []
    for lane in (0, 1):
        place = np.where(tile < 4, 2 * tile + lane, 2 * tile + 1 - lane)
        angle = (place * 128 + row % 128).astype(np.float32)[:, None] * freq.astype(np.float32)
        angle = angle.astype(np.float64)
        cos, sin = np.cos(angle), np.sin(angle)
        tables.append(
            (np.concatenate([cos, cos], 1), np.concatenate([-sin, sin], 1))
        )
    return np.array(tables, dtype=np.float32)


def shards(
    tokens,
    gain_in,
    query_weight,
    key_weight,
    value_weight,
    gain_query,
    gain_key,
    out_weight,
    gain_mid,
    gate_weight,
    up_weight,
    down_weight,
    cotangent,
):
    width = tokens.shape[4]
    n_tp = lax.axis_size("z") * lax.axis_size("core")
    n_fs = lax.axis_size("x") * lax.axis_size("yh")
    head = 128
    qc, kc, fc = 256, 128, 768
    t = lax.axis_index(TP)

    table = lax.dynamic_index_in_dim(jnp.asarray(rotary(head)), lax.axis_index("yl"), 0, False)
    cosine, sine = table[0], table[1]

    cut = lambda w, n: lax.dynamic_slice_in_dim(w, t * n, n, 1)
    d_s = down_weight.shape[0] // n_tp
    rows_d = lax.ppermute(
        lax.dynamic_slice_in_dim(down_weight, t * d_s, d_s, 0),
        TP + FS,
        [(a * n_fs + b, b * n_fs + a) for a in range(n_tp) for b in range(n_fs)],
    )
    tok = tokens.reshape(2, 64, width)
    cot = cotangent.reshape(2, 64, width)
    gain_q, gain_k = gain_query.reshape(1, -1), gain_key.reshape(1, -1)
    h, w_qkv, query_b, kv, kv_far, raw, attended, g, w_out, w_gate, w_up, y_mid, h2_own = ahead(
        tok,
        gain_in.reshape(1, -1),
        jnp.concatenate([cut(query_weight, qc), cut(key_weight, kc), cut(value_weight, kc)], 1),
        cosine,
        sine,
        gain_q,
        gain_k,
        cot,
        lax.dynamic_slice_in_dim(out_weight, lax.axis_index("core") * 128, 128, 0),
        cut(gate_weight, fc),
        cut(up_weight, fc),
        gain_mid.reshape(1, -1),
    )
    h2, dgate_b, dup_b, mixed_part, grad_mid, dz_own, d_tok, term_mid, down_mine = mlp(
        h2_own,
        rows_d,
        w_gate,
        w_up,
        g,
        w_out.reshape(32, 64, width),
        y_mid,
        cot,
        gain_mid.reshape(1, -1),
    )
    mixed, tokens_grad, g_gate, g_up, g_q, g_k, g_v, g_down, g_out, s_in, s_mid, s_q, s_k = behind(
        query_b,
        kv,
        kv_far,
        cosine,
        sine,
        gain_q,
        gain_k,
        d_tok,
        dz_own,
        attended,
        tok,
        gain_in.reshape(1, -1),
        term_mid,
        down_mine,
        raw,
        w_qkv,
        grad_mid,
        y_mid,
        h2,
        dgate_b,
        dup_b,
        mixed_part,
        h,
    )

    return (
        mixed.reshape(tokens.shape),
        tokens_grad.reshape(tokens.shape),
        s_in.reshape(-1),
        g_q,
        g_k,
        g_v,
        s_q.reshape(-1),
        s_k.reshape(-1),
        g_out,
        s_mid.reshape(-1),
        g_gate,
        g_up,
        g_down,
    )


def solution(mesh):
    fine = Mesh(mesh.devices.reshape(4, 2, 2, 4, 2), ALL)
    ctx, fsdp = ("z", "yl", "core"), FS
    act = P(fsdp, None, ctx, None, None)
    weight = P(fsdp, None)
    grad = P(ctx + fsdp, None)
    placed = (
        act, P(), weight, weight, weight, P(), P(), weight, P(), weight, weight, weight, act,
    )
    return jax.shard_map(
        shards,
        mesh=fine,
        in_specs=placed,
        out_specs=(act, act, P(), grad, grad, grad, P(), P(), grad, P(), grad, grad, grad),
        check_vma=False,
    )
```

```python
import functools

import jax
import jax.numpy as jnp
import numpy as np
from jax import lax
from jax.experimental import pallas as pl
from jax.experimental.pallas import tpu as pltpu
from jax.sharding import Mesh, PartitionSpec as P

EPS = 1e-06
THETA = 1000000.0
BF = jnp.bfloat16
F32 = jnp.float32
TP = ("z", "core")
FS = ("x", "yh")
DP = ("yl", "x", "yh")
ALL = ("z", "yl", "core", "x", "yh")
MESH = pl.DeviceIdType.MESH
VMEM = pl.BlockSpec(memory_space=pltpu.VMEM)
HBM = pl.BlockSpec(memory_space=pl.ANY)
MB = 2**20
LOG2E = 1.4426950408889634


class Place:
    def __init__(self):
        self.z, self.yl, self.core, self.x, self.yh = (lax.axis_index(a) for a in ALL)
        self.t = 2 * self.z + self.core
        self.shard = 2 * self.x + self.yh
        self.y = 2 * self.yh + self.yl

    def at(self, z=None, yl=None, core=None, x=None, yh=None):
        here = (self.z, self.yl, self.core, self.x, self.yh)
        return tuple(h if n is None else n for h, n in zip(here, (z, yl, core, x, yh)))

    def up(self, n):
        return lax.rem(self.z + n, 4)

    def east(self, n):
        return lax.rem(self.x + n, 4)

    def north(self, n):
        y = lax.rem(self.y + n, 4)
        return self.at(yh=y // 2, yl=lax.rem(y, 2))

    def turned(self):
        to_x = lax.rem(self.z + self.x, 4)
        goal = self.at(z=self.x, core=self.yh, x=to_x, yh=self.core)
        source = self.at(z=lax.rem(self.x + 4 - self.z, 4), core=self.yh, x=self.z, yh=self.core)
        stay = (self.x == 0) & (self.z == 0) & (self.core == self.yh)
        return goal, source, stay, 2 * to_x + self.core

    def peers(self, which):
        table = {
            "z": [self.at(z=self.up(1)), self.at(z=self.up(3))],
            "sib": [self.at(core=1 - self.core)],
            "x": [self.at(x=self.east(1)), self.at(x=self.east(3))],
            "cross": [self.at(yl=1 - self.yl, yh=1 - self.yh)],
            "pair": [self.at(yl=1 - self.yl)],
            "plane": [self.at(x=self.east(d)) for d in (1, 2, 3)]
            + [self.north(d) for d in (1, 2, 3)],
            "swap": [self.at(yl=1 - self.yl, core=1 - self.core)],

            "tp": [
                self.at(z=self.up(dz), core=lax.rem(self.core + dc, 2))
                for dz in range(4)
                for dc in range(2)
                if dz or dc
            ],
        }
        return [p for name in which for p in table[name]]


class Wire:
    def __init__(self, send_sem, recv_sem, here_sem):
        self.send_sem, self.recv_sem, self.here_sem = send_sem, recv_sem, here_sem
        self.n = self.m = 0
        self.sent = []

    def send(self, src, dst, peer):
        copy = pltpu.make_async_remote_copy(
            src_ref=src,
            dst_ref=dst,
            send_sem=self.send_sem.at[self.n],
            recv_sem=self.recv_sem.at[self.n],
            device_id=peer,
            device_id_type=MESH,
        )
        self.n += 1
        assert self.n <= self.send_sem.shape[0]
        copy.start()
        self.sent.append(copy)
        return copy

    def here(self, src, dst):
        copy = pltpu.make_async_copy(src, dst, self.here_sem.at[self.m])
        self.m += 1
        assert self.m <= self.here_sem.shape[0]
        copy.start()
        return copy

    def settle(self, copies):
        for copy in copies:
            copy.wait_send()
        self.sent = [one for one in self.sent if all(one is not copy for copy in copies)]

    def finish(self):
        for copy in self.sent:
            copy.wait_send()


def sems(n, m):
    return [
        pltpu.SemaphoreType.DMA((n,)),
        pltpu.SemaphoreType.DMA((n,)),
        pltpu.SemaphoreType.DMA((m,)),
    ]


def meet(peers, source=None, stay=None):
    barrier = pltpu.get_barrier_semaphore()
    for peer in peers:
        pl.semaphore_signal(barrier, inc=1, device_id=peer, device_id_type=MESH)
    if source is not None:

        @pl.when(jnp.logical_not(stay))
        def _():
            pl.semaphore_signal(barrier, inc=1, device_id=source, device_id_type=MESH)

        pl.semaphore_wait(barrier, jnp.where(stay, len(peers), len(peers) + 1))
    else:
        pl.semaphore_wait(barrier, len(peers))


def run(*tasks):
    tasks = list(tasks)
    while tasks:
        advance(tasks)


def advance(tasks):
    for task in list(tasks):
        try:
            next(task)
        except StopIteration:
            tasks.remove(task)


def gather_z(w, p, own, dst):
    up, down, sib = p.at(z=p.up(1)), p.at(z=p.up(3)), p.at(core=1 - p.core)
    before, after, far = (2 * p.up(n) + p.core for n in (3, 1, 2))
    u0 = w.send(own(0), dst(p.t, 0), up)
    d1 = w.send(own(1), dst(p.t, 1), down)
    u1 = w.send(own(1), dst(p.t, 1), up)
    d0 = w.send(own(0), dst(p.t, 0), down)
    s = [w.send(own(k), dst(p.t, k), sib) for k in (0, 1)]

    def on(t, k):
        s.append(w.send(dst(t, k), dst(t, k), sib))

    yield
    for copy in s[:2]:
        copy.wait_recv()
    yield
    u0.wait_recv()
    f0 = w.send(dst(before, 0), dst(before, 0), up)
    on(before, 0)
    d1.wait_recv()
    f1 = w.send(dst(after, 1), dst(after, 1), down)
    on(after, 1)
    yield
    u1.wait_recv()
    on(before, 1)
    d0.wait_recv()
    on(after, 0)
    yield
    for copy in s[2:6]:
        copy.wait_recv()
    yield
    f0.wait_recv()
    on(far, 0)
    f1.wait_recv()
    on(far, 1)
    yield
    for copy in s[6:]:
        copy.wait_recv()
    w.settle([u0, d1, u1, d0, f0, f1] + s)


def gather_yx(w, p, dst, n):
    east, west = p.at(x=p.east(1)), p.at(x=p.east(3))
    cross, pair = p.at(yl=1 - p.yl, yh=1 - p.yh), p.at(yl=1 - p.yl)
    half = n // 2
    me, flip = p.shard, 1 - 2 * p.yh
    west_s, east_s, far_s = (2 * p.east(k) + p.yh for k in (3, 1, 2))
    mine = p.yl * half
    other = half - mine

    def one(s, at, peer):
        return w.send(dst(s, at, half), dst(s, at, half), peer)

    c0 = one(me, mine, cross)
    e0 = one(me, 0, east)
    w1 = one(me, half, west)
    e1 = one(me, half, east)
    w0 = one(me, 0, west)
    yield
    c0.wait_recv()
    a0 = one(me + flip, other, pair)
    e0.wait_recv()
    f0 = one(west_s, 0, east)
    w1.wait_recv()
    f1 = one(east_s, half, west)
    yield
    a0.wait_recv()
    g0 = one(me + flip, 0, east)
    h1 = one(me + flip, half, west)
    g1 = one(me + flip, half, east)
    h0 = one(me + flip, 0, west)
    yield
    for copy in (e1, w0, f0, f1):
        copy.wait_recv()
    g0.wait_recv()
    i0 = one(west_s + flip, 0, east)
    h1.wait_recv()
    i1 = one(east_s + flip, half, west)
    yield
    for copy in (g1, h0, i0, i1):
        copy.wait_recv()


def gather_xy(w, p, dst, n, ready=None):
    east, west = p.at(x=p.east(1)), p.at(x=p.east(3))
    cross, pair = p.at(yl=1 - p.yl, yh=1 - p.yh), p.at(yl=1 - p.yl)
    half = n // 2
    me = p.shard
    west_s, east_s, far_s = (2 * p.east(k) + p.yh for k in (3, 1, 2))
    mine = p.yl * half
    other = half - mine
    flip = 1 - 2 * p.yh

    def one(s, at, peer):
        return w.send(dst(s, at, half), dst(s, at, half), peer)

    def along(s):
        return one(s + flip, other, pair)

    e0 = one(me, mine, east)
    w0 = one(me, mine, west)
    c0 = one(me, mine, cross)
    w1 = one(me, other, west)
    yield
    e0.wait_recv()
    fe = one(west_s, mine, east)
    c1 = one(west_s, mine, cross)
    e1 = one(me, other, east)
    w0.wait_recv()
    c2 = one(east_s, mine, cross)
    c0.wait_recv()
    a0 = along(me)
    yield
    fe.wait_recv()
    c3 = one(far_s, mine, cross)
    w1.wait_recv()
    fw = one(east_s, other, west)
    if ready:
        ready(east_s)
    yield
    c1.wait_recv()
    a1 = along(west_s)
    e1.wait_recv()
    if ready:
        ready(west_s)
    c2.wait_recv()
    a2 = along(east_s)
    yield
    fw.wait_recv()
    if ready:
        ready(far_s)
    c3.wait_recv()
    a3 = along(far_s)
    yield
    for s, a in ((me, a0), (west_s, a1), (east_s, a2), (far_s, a3)):
        a.wait_recv()
        if ready:
            ready(s + flip)


def norm_rope(raw, gain, cosine, sine):
    unit = raw * lax.rsqrt(jnp.mean(raw * raw, -1, keepdims=True) + EPS)
    vals = unit * gain
    return vals * cosine + pltpu.roll(vals, 64, 1) * sine


SCALE = 128**-0.5 * LOG2E


def dot_t(a, b):
    return lax.dot_general(a, b, (((1,), (1,)), ((), ())), preferred_element_type=F32)


def t_dot(a, b):
    return lax.dot_general(a, b, (((0,), (0,)), ((), ())), preferred_element_type=F32)


def both(ref, at):
    return jnp.concatenate([ref[at, 0:128], ref[at, 128:256]], 0)


def weights_of(q, k, j, edge):
    s = jnp.exp2(dot_t(q, k) * SCALE)
    last = jnp.where(edge, s[:, j * 128 :], 0.0)
    return last if j == 0 else jnp.concatenate([s[:, : j * 128], last], 1)


def edges(p, j):
    row = lax.broadcasted_iota(jnp.int32, (256, 128), 0) % 128
    col = lax.broadcasted_iota(jnp.int32, (256, 128), 1)
    seen = (p.yl if j < 4 else 1 - p.yl) * 128
    return col <= row, col < seen


def shard_rows(ref, n):
    return lambda s, at, m: ref.at[pl.ds(pl.multiple_of(s * n + at, 16), m)]


def ahead_kernel(
    tok, gain, gq, gk, cot, gain_mid, table, wq, wk, wv, wo, wg, wu, wd,
    h_out, qkv_out, q_out, kv_out, kv_far_out, raw_out, o_out, g_out, out_out, gate_out, up_out,
    y1_out, down_out, h2, q, kv, kv_far, raw, o, y1, h, w_qkv, g, w_out, w_gate, w_up, o_tok,
    cosine, sine, down, down_in, send_sem, recv_sem, here_sem
):
    p = Place()
    w = Wire(send_sem, recv_sem, here_sem)
    own = pl.ds(pl.multiple_of(p.shard * 256, 256), 256)

    def cut(n):
        return pl.ds(pl.multiple_of(p.t * n, n), n)

    load_qkv = [
        w.here(wq.at[:, cut(256)], w_qkv.at[own, pl.ds(0, 256)]),
        w.here(wk.at[:, cut(128)], w_qkv.at[own, pl.ds(256, 128)]),
        w.here(wv.at[:, cut(128)], w_qkv.at[own, pl.ds(384, 128)]),
    ]
    load_out = w.here(wo.at[pl.ds(pl.multiple_of(p.core * 128, 128), 128)], w_out.at[p.shard, p.core])
    load_gate = w.here(wg.at[:, cut(768)], w_gate.at[own])
    load_up = w.here(wu.at[:, cut(768)], w_up.at[own])
    goal, source, stay, at_down = p.turned()
    load_down = w.here(wd.at[pl.ds(pl.multiple_of(at_down * 96, 96), 96)], down)
    load_table = [w.here(table.at[p.yl, 0], cosine), w.here(table.at[p.yl, 1], sine)]
    for k in (0, 1):
        x = tok[k].astype(F32)
        unit = x * lax.rsqrt(jnp.mean(x * x, -1, keepdims=True) + EPS)
        h[p.t if k == 0 else 15 - p.t] = (unit * gain[...]).astype(BF)
    meet(p.peers(("tp", "x", "cross", "pair")), source, stay)
    pair, sib = p.at(yl=1 - p.yl), p.at(core=1 - p.core)

    def block_of(ref):
        return lambda t, k: ref.at[t if k == 0 else 15 - t]

    def part_out(s, at, n):
        return w_out.at[s, p.core, pl.ds(pl.multiple_of(at, 64), n)]

    twin = []

    def ready(s):
        twin.append(w.send(w_out.at[s, p.core], w_out.at[s, p.core], sib))

    at_h, at_g = block_of(h), block_of(g)
    task_h = [gather_z(w, p, lambda k: at_h(p.t, k), at_h)]
    task_qkv = [gather_xy(w, p, shard_rows(w_qkv, 256), 256)]
    for copy in load_qkv:
        copy.wait()
    advance(task_qkv)
    advance(task_h)
    g[p.t] = cot[0]
    g[15 - p.t] = cot[1]
    task_up = [gather_xy(w, p, shard_rows(w_up, 256), 256)]
    task_out = [gather_xy(w, p, part_out, 128, ready)]
    task_gate = [gather_yx(w, p, shard_rows(w_gate, 256), 256)]
    task_g = [gather_z(w, p, lambda k: at_g(p.t, k), at_g)]
    load_out.wait()
    ready(p.shard)
    load_down.wait()
    n = w.n
    w.n += 1
    turn = pltpu.make_async_remote_copy(
        src_ref=down,
        dst_ref=down_in,
        send_sem=send_sem.at[n],
        recv_sem=recv_sem.at[n],
        device_id=goal,
        device_id_type=MESH,
    )
    advance(task_h)
    advance(task_qkv)
    advance(task_h)
    advance(task_qkv)
    advance(task_out)
    advance(task_qkv)
    advance(task_h)
    advance(task_qkv)
    advance(task_h)
    advance(task_h)
    advance(task_qkv)
    advance(task_out)
    load_gate.wait()
    load_up.wait()
    advance(task_gate)
    advance(task_g)
    run(*task_h)
    kept = [w.here(h, h_out), w.here(w_qkv, qkv_out)]
    for copy in load_table:
        copy.wait()
    swaps = []
    for j in range(4):
        at = pl.ds(j * 256, 256)
        out = jnp.dot(
            h[4 * j : 4 * j + 4].reshape(256, 2048), w_qkv[...], preferred_element_type=F32
        )
        cos, sin = cosine[at], sine[at]
        kv[at, 0:128] = norm_rope(out[:, 256:384], gk[...], cos, sin).astype(BF)
        kv[at, 128:256] = out[:, 384:].astype(BF)
        swaps.append(w.send(kv.at[at], kv_far.at[at], pair))
        for n in (0, 1):
            cols = slice(n * 128, n * 128 + 128)
            q[at, cols] = norm_rope(out[:, cols], gq[...], cos, sin).astype(BF)
        raw[at] = out[:, :384]
        if j == 0:
            advance(task_out)
        if j == 1:
            advance(task_g)
            advance(task_gate)
        if j == 2:
            advance(task_up)
        if j == 3:
            advance(task_out)
            advance(task_g)
    for j in range(8):
        at = pl.ds(j * 128, 128)
        keys = pl.ds(0, j * 128 + 128)
        if j % 2 == 0:
            swaps[j // 2].wait_recv()
        tri, seen = edges(p, j)
        qj = both(q, at)
        near = weights_of(qj, kv[keys, 0:128], j, tri)
        far = weights_of(qj, kv_far[keys, 0:128], j, seen)
        total = jnp.sum(near, -1, keepdims=True) + jnp.sum(far, -1, keepdims=True)
        out = jnp.dot(near.astype(BF), kv[keys, 128:256], preferred_element_type=F32)
        out += jnp.dot(far.astype(BF), kv_far[keys, 128:256], preferred_element_type=F32)
        out = (out / total).astype(BF)
        for n in (0, 1):
            o[2 * j : 2 * j + 2, :, n * 128 : n * 128 + 128] = out[
                n * 128 : n * 128 + 128
            ].reshape(2, 64, 128)
        if j == 1:
            advance(task_gate)
        if j == 2:
            advance(task_g)
            advance(task_g)
        if j == 3:
            advance(task_up)
        if j == 4:
            advance(task_out)
            advance(task_g)
        if j == 5:
            advance(task_gate)
        if j == 7:
            advance(task_up)
    spread = []
    for dz in (2, 1, 3, 0):
        for dc in range(2):
            z, core = p.up(dz), lax.rem(p.core + dc, 2)
            t = 2 * z + core
            for k in (0, 1):
                src = o.at[t if k == 0 else 15 - t]
                if dz or dc:
                    spread.append(w.send(src, o_tok.at[p.t, k], p.at(z=z, core=core)))
                else:
                    o_tok[p.t, k] = o[t if k == 0 else 15 - t]
    @pl.when(jnp.logical_not(stay))
    def _():
        turn.start()

    @pl.when(stay)
    def _():
        down_in[...] = down[...]

    kept += [
        w.here(q, q_out),
        w.here(kv, kv_out),
        w.here(kv_far, kv_far_out),
        w.here(raw, raw_out),
        w.here(o, o_out),
    ]
    run(*task_g)
    kept.append(w.here(g, g_out))
    advance(task_up)
    run(*task_out)
    run(*task_gate)
    kept.append(w.here(w_gate, gate_out))
    advance(task_up)
    for copy in twin:
        copy.wait_recv()
    kept.append(w.here(w_out, out_out))
    for copy in spread:
        copy.wait_recv()
    for n in range(4):
        cols = slice(n * 512, n * 512 + 512)
        for k in (0, 1):
            y1[k, :, cols] = tok[k, :, cols].astype(F32)
        for t in range(8):
            part = jnp.dot(
                o_tok[t].reshape(128, 256),
                w_out[t, :, :, cols].reshape(256, 512),
                preferred_element_type=F32,
            )
            for k in (0, 1):
                y1[k, :, cols] += part[k * 64 : k * 64 + 64]
    for k in (0, 1):
        y = y1[k]
        unit = y * lax.rsqrt(jnp.mean(y * y, -1, keepdims=True) + EPS)
        h2[k] = (unit * gain_mid[...]).astype(BF)
    kept.append(w.here(y1, y1_out))
    run(*task_up)
    kept.append(w.here(w_up, up_out))

    @pl.when(jnp.logical_not(stay))
    def _():
        turn.wait()

    kept.append(w.here(down_in, down_out))
    w.finish()
    for copy in kept:
        copy.wait()


def ahead(*args):
    sds = jax.ShapeDtypeStruct
    return pl.pallas_call(
        ahead_kernel,
        out_shape=(
            sds((16, 64, 2048), BF),
            sds((2048, 512), BF),
            sds((1024, 256), BF),
            sds((1024, 256), BF),
            sds((1024, 256), BF),
            sds((1024, 384), F32),
            sds((16, 64, 256), BF),
            sds((16, 64, 2048), BF),
            sds((8, 2, 128, 2048), BF),
            sds((2048, 768), BF),
            sds((2048, 768), BF),
            sds((2, 64, 2048), F32),
            sds((96, 2048), BF),
            sds((2, 64, 2048), BF),
        ),
        in_specs=[VMEM] * 6 + [HBM] * 8,
        out_specs=[HBM] * 13 + [VMEM],
        scratch_shapes=[
            pltpu.VMEM((1024, 256), BF),
            pltpu.VMEM((1024, 256), BF),
            pltpu.VMEM((1024, 256), BF),
            pltpu.VMEM((1024, 384), F32),
            pltpu.VMEM((16, 64, 256), BF),
            pltpu.VMEM((2, 64, 2048), F32),
            pltpu.VMEM((16, 64, 2048), BF),
            pltpu.VMEM((2048, 512), BF),
            pltpu.VMEM((16, 64, 2048), BF),
            pltpu.VMEM((8, 2, 128, 2048), BF),
            pltpu.VMEM((2048, 768), BF),
            pltpu.VMEM((2048, 768), BF),
            pltpu.VMEM((8, 2, 64, 256), BF),
            pltpu.VMEM((1024, 128), F32),
            pltpu.VMEM((1024, 128), F32),
            pltpu.VMEM((96, 2048), BF),
            pltpu.VMEM((96, 2048), BF),
        ]
        + sems(160, 32),
        compiler_params=pltpu.CompilerParams(
            collective_id=0, has_side_effects=True, vmem_limit_bytes=56 * MB
        ),
        name="ahead",
    )(*args)


def rows_of(ref, zz):
    c = ref.shape[-1]
    return jnp.concatenate(
        [ref[pl.ds(2 * zz, 2)].reshape(128, c), ref[pl.ds(14 - 2 * zz, 2)].reshape(128, c)], 0
    )


def put(ref, zz, val):
    c = ref.shape[-1]
    ref[pl.ds(2 * zz, 2)] = val[:128].reshape(2, 64, c)
    ref[pl.ds(14 - 2 * zz, 2)] = val[128:].reshape(2, 64, c)


def add(*vals):
    total = vals[0].astype(F32)
    for val in vals[1:]:
        total = total + val.astype(F32)
    return total


def z_room():
    return [
        pltpu.VMEM((4, 2, 64, 2048), BF),
        pltpu.VMEM((2, 64, 2048), BF),
        pltpu.VMEM((2, 2, 64, 2048), BF),
    ]


def reduce_z(w, p, part, room, out):
    mine, relay, last = room
    near = mine
    up, down, sib = p.at(z=p.up(1)), p.at(z=p.up(3)), p.at(core=1 - p.core)

    def block(n, core, k):
        t = 2 * p.up(n) + core
        return t if k == 0 else 15 - t

    first = {}

    def give(n):
        for k in (0, 1):
            first[n, k] = w.send(part.at[block(n, 1 - p.core, k)], near.at[n, k], sib)

    def fold(n, k):
        first[n, k].wait_recv()
        mine[n, k] = add(part[block(n, p.core, k)], near[n, k]).astype(BF)

    give(2)
    yield
    give(1)
    fold(2, 0)
    e0 = w.send(mine.at[2, 0], relay.at[0], up)
    fold(2, 1)
    e1 = w.send(mine.at[2, 1], relay.at[1], down)
    yield
    give(3)
    fold(1, 1)
    a1 = w.send(mine.at[1, 1], last.at[0, 1], up)
    fold(1, 0)
    yield
    give(0)
    fold(3, 0)
    b0 = w.send(mine.at[3, 0], last.at[1, 0], down)
    fold(3, 1)
    yield
    e0.wait_recv()
    mine[1, 0] = add(mine[1, 0], relay[0]).astype(BF)
    a0 = w.send(mine.at[1, 0], last.at[0, 0], up)
    e1.wait_recv()
    mine[3, 1] = add(mine[3, 1], relay[1]).astype(BF)
    b1 = w.send(mine.at[3, 1], last.at[1, 1], down)
    fold(0, 0)
    fold(0, 1)
    w.settle(list(first.values()))
    yield
    for k, (a, b) in enumerate(((a0, b0), (a1, b1))):
        a.wait_recv()
        b.wait_recv()
        out[k] = add(mine[0, k], last[0, k], last[1, k])


def xy_room(rows, cols, left=None):
    left = left or cols // 2
    return [
        pltpu.VMEM(lead + (rows, n), BF)
        for n in (left, cols - left)
        for lead in ((4,), (2, 4), (4,), (3,))
    ]


def put_half(out, cols, val):
    if len(out.shape) == 3:
        out[:, :, cols] = val.reshape(out.shape[0], out.shape[1], val.shape[1])
    else:
        out[:, cols] = val


def reduce_xy(w, p, part, room, out):
    ra, ta, sa, fa, rb, tb, sb, fb = room
    n_left = sa.shape[2]
    left, right = pl.ds(0, n_left), pl.ds(n_left, part.shape[3] - n_left)
    low, high = pl.ds(0, 2), pl.ds(2, 2)
    spans = (1, 2, 3)
    easts = [p.at(x=p.east(d)) for d in spans]
    norths = [p.north(d) for d in spans]
    xs = [p.east(d) for d in spans]
    ys = [lax.rem(p.y + d, 4) for d in spans]

    def start(bundle, r, t, peers):
        return [
            w.send(bundle(1, low), r.at[low], peers[0]),
            w.send(bundle(1, high), r.at[high], peers[2]),
            w.send(bundle(0, high), t.at[0, high], peers[0]),
            w.send(bundle(2, low), t.at[1, low], peers[2]),
        ]

    def of_x(d, some):
        return part.at[xs[d], some, :, left]

    def of_y(d, some):
        return part.at[some, ys[d], :, right]

    ca = start(of_x, ra, ta, easts)
    yield
    cb = start(of_y, rb, tb, norths)
    yield
    ca[0].wait_recv()
    for k in (0, 1):
        ra[k] = add(ra[k], part[xs[0], k, :, left]).astype(BF)
    ca.append(w.send(ra.at[low], ta.at[0, low], easts[0]))
    ca[1].wait_recv()
    for k in (2, 3):
        ra[k] = add(ra[k], part[xs[2], k, :, left]).astype(BF)
    ca.append(w.send(ra.at[high], ta.at[1, high], easts[2]))
    yield
    cb[0].wait_recv()
    for k in (0, 1):
        rb[k] = add(rb[k], part[k, ys[0], :, right]).astype(BF)
    cb.append(w.send(rb.at[low], tb.at[0, low], norths[0]))
    cb[1].wait_recv()
    for k in (2, 3):
        rb[k] = add(rb[k], part[k, ys[2], :, right]).astype(BF)
    cb.append(w.send(rb.at[high], tb.at[1, high], norths[2]))
    yield
    for copy in ca[2:]:
        copy.wait_recv()

    @pl.loop(0, 4)
    def _(y):
        sa[y] = add(part[p.x, y, :, left], ta[0, y], ta[1, y]).astype(BF)

    da = [w.send(sa.at[lax.rem(p.y + d, 4)], fa.at[d - 1], norths[d - 1]) for d in spans]
    yield
    for copy in cb[2:]:
        copy.wait_recv()

    @pl.loop(0, 4)
    def _(x):
        sb[x] = add(part[x, p.y, :, right], tb[0, x], tb[1, x]).astype(BF)

    db = [w.send(sb.at[p.east(d)], fb.at[d - 1], easts[d - 1]) for d in spans]
    yield
    for copy in da:
        copy.wait_recv()
    put_half(out, left, add(sa[p.y], fa[0], fa[1], fa[2]).astype(BF))
    yield
    for copy in db:
        copy.wait_recv()
    put_half(out, right, add(sb[p.x], fb[0], fb[1], fb[2]).astype(BF))


def mlp_kernel(
    h2_own, down_own, gate_hbm, up_hbm, g_hbm, out_hbm, y1, cot, gain,
    h2_out, dgate_out, dup_out, mixed_out, grad_mid, dz, d_tok, term, down_mine,
    h2, w_gate, w_up, w_down, g, gate, upper, part, down_part, act, dgate, dup, mixed, *rest
):
    zr, xr, (send_sem, recv_sem, here_sem) = rest[:3], rest[3:11], rest[11:]
    p = Place()
    w = Wire(send_sem, recv_sem, here_sem)
    loads = [w.here(gate_hbm, w_gate), w.here(up_hbm, w_up), w.here(g_hbm, g)]
    h2[p.t] = h2_own[0]
    h2[15 - p.t] = h2_own[1]
    w_down[pl.ds(pl.multiple_of(p.shard * 96, 96), 96)] = down_own[...]
    meet(p.peers(("z", "sib", "x", "plane", "cross")))

    def block(t, k):
        return h2.at[t if k == 0 else 15 - t]

    task_h = [gather_z(w, p, lambda k: block(p.t, k), block)]
    task_down = [gather_xy(w, p, shard_rows(w_down, 96), 96)]
    def forward(zz):
        left = rows_of(h2, zz)
        gate_n = jnp.dot(left, w_gate[...], preferred_element_type=F32)
        up_n = jnp.dot(left, w_up[...], preferred_element_type=F32)
        gate[zz] = gate_n
        upper[zz] = up_n
        put(act, zz, (gate_n * jax.nn.sigmoid(gate_n) * up_n).astype(BF))

    advance(task_h)
    advance(task_down)
    advance(task_h)
    for copy in loads:
        copy.wait()
    forward(p.z)
    advance(task_down)
    advance(task_h)
    advance(task_down)
    advance(task_h)
    advance(task_h)
    advance(task_down)
    forward(p.up(3))
    advance(task_h)
    forward(p.up(1))
    advance(task_down)
    run(*task_h)
    kept = [w.here(h2, h2_out)]
    forward(p.up(2))
    kept[0].wait()
    load = w.here(out_hbm.at[pl.ds(0, 16)], h2)

    @pl.loop(0, 6)
    def _(i):
        cols = pl.ds(pl.multiple_of(i * 128, 128), 128)
        left = act[:, :, cols].reshape(1024, 128)
        out = t_dot(left, g[...].reshape(1024, 2048)).astype(BF)
        for k in range(8):
            row = i * 8 + k
            piece = row // 3
            f = lax.rem(piece, 8)
            down_part[f // 2, 2 * lax.rem(f, 2) + piece // 8, pl.ds(pl.multiple_of(lax.rem(row, 3) * 16, 16), 16)] = out[
                k * 16 : k * 16 + 16
            ]

    run(*task_down)
    task_sum = [reduce_z(w, p, part, zr, grad_mid)]
    task_late = [reduce_xy(w, p, down_part, xr, down_mine)]
    advance(task_late)
    advance(task_late)
    for n in (2, 1, 3, 0):
        zz = p.up(n)
        gate_n, up_n = gate[zz], upper[zz]
        sig = jax.nn.sigmoid(gate_n)
        da = dot_t(rows_of(g, zz), w_down[...])
        silu = gate_n * sig
        d_gate = (da * up_n * sig * (1.0 + gate_n * (1.0 - sig))).astype(BF)
        d_up = (da * silu).astype(BF)
        put(dgate, zz, d_gate)
        put(dup, zz, d_up)
        total = dot_t(d_gate, w_gate[...]) + dot_t(d_up, w_up[...])
        put(part, zz, total.astype(BF))
        advance(task_sum)
        if n == 3:
            advance(task_late)
            advance(task_late)
    load2 = w.here(out_hbm.at[pl.ds(16, 16)], g)
    kept += [w.here(dgate, dgate_out), w.here(dup, dup_out)]
    advance(task_sum)

    @pl.loop(0, 4)
    def _(n):
        out = jnp.dot(rows_of(act, n), w_down[...], preferred_element_type=F32)
        put(mixed, n, out.astype(BF))

    kept.append(w.here(mixed, mixed_out))
    advance(task_late)
    run(*task_sum)
    advance(task_late)
    load.wait()
    load2.wait()
    term[...] = jnp.zeros_like(term)
    for k in (0, 1):
        y = y1[k]
        scale = lax.rsqrt(jnp.mean(y * y, -1, keepdims=True) + EPS)
        unit = y * scale
        dh = grad_mid[k]
        term[...] += jnp.sum(dh * unit, 0, keepdims=True)
        wv = dh * gain[...]
        dy = cot[k].astype(F32) + scale * (wv - unit * jnp.mean(wv * unit, -1, keepdims=True))
        grad_mid[k] = dy
        dz[k] = dy.astype(BF)
    dz_rows = dz[...].reshape(128, 2048)
    for t in range(8):
        half = h2 if t < 4 else g
        out = dot_t(dz_rows, half[4 * (t % 4) : 4 * (t % 4) + 4].reshape(256, 2048)).astype(BF)
        d_tok[t] = out.reshape(2, 64, 256)
    run(*task_late)
    w.finish()
    for copy in kept[1:]:
        copy.wait()


def mlp(*args):
    sds = jax.ShapeDtypeStruct
    return pl.pallas_call(
        mlp_kernel,
        out_shape=(
            sds((16, 64, 2048), BF),
            sds((16, 64, 768), BF),
            sds((16, 64, 768), BF),
            sds((16, 64, 2048), BF),
            sds((2, 64, 2048), F32),
            sds((2, 64, 2048), BF),
            sds((8, 2, 64, 256), BF),
            sds((1, 2048), F32),
            sds((48, 2048), BF),
        ),
        in_specs=[VMEM] * 2 + [HBM] * 4 + [VMEM] * 3,
        out_specs=[HBM] * 4 + [VMEM] * 5,
        scratch_shapes=[
            pltpu.VMEM((16, 64, 2048), BF),
            pltpu.VMEM((2048, 768), BF),
            pltpu.VMEM((2048, 768), BF),
            pltpu.VMEM((768, 2048), BF),
            pltpu.VMEM((16, 64, 2048), BF),
            pltpu.VMEM((4, 256, 768), F32),
            pltpu.VMEM((4, 256, 768), F32),
            pltpu.VMEM((16, 64, 2048), BF),
            pltpu.VMEM((4, 4, 48, 2048), BF),
            pltpu.VMEM((16, 64, 768), BF),
            pltpu.VMEM((16, 64, 768), BF),
            pltpu.VMEM((16, 64, 768), BF),
            pltpu.VMEM((16, 64, 2048), BF),
        ]
        + z_room()
        + xy_room(48, 2048)
        + sems(96, 12),
        compiler_params=pltpu.CompilerParams(
            collective_id=2, has_side_effects=True, vmem_limit_bytes=63 * MB
        ),
        name="mlp",
    )(*args)


def sum_all(w, p, vec, slots, out):
    ra, rb, rc = slots
    ra[p.t] = vec[...]
    first = [w.send(ra.at[p.t], ra.at[p.t], peer) for peer in p.peers(("tp",))]
    yield
    for copy in first:
        copy.wait_recv()
    rb[p.x] = sum((ra[i] for i in range(1, 8)), ra[0])
    xs = [w.send(rb.at[p.x], rb.at[p.x], p.at(x=p.east(d))) for d in (1, 2, 3)]
    yield
    for copy in xs:
        copy.wait_recv()
    rc[p.y] = sum((rb[i] for i in range(1, 4)), rb[0])
    ys = [w.send(rc.at[p.y], rc.at[p.y], p.north(d)) for d in (1, 2, 3)]
    yield
    for copy in ys:
        copy.wait_recv()
    out[...] = sum((rc[i] for i in range(1, 4)), rc[0])


def deal(w, p, src, dst):
    dst[p.t] = src[p.t]
    copies = []
    for dz in (2, 1, 3, 0):
        for dc in range(2):
            if dz or dc:
                z, core = p.up(dz), lax.rem(p.core + dc, 2)
                copies.append(w.send(src.at[2 * z + core], dst.at[p.t], p.at(z=z, core=core)))
    return copies


def to_pieces(part, i, out, cols):
    z, yl = i // 2, lax.rem(i, 2)
    for r in range(16):
        core, f = r // 8, r % 8
        at = pl.ds(pl.multiple_of((2 * z + core) * 16, 16), 16)
        part[f // 2, 2 * (f % 2) + yl, at, cols] = out[r * 16 : r * 16 + 16]


def turn_norm_back(grad, raw, gain, cosine, sine):
    scale = lax.rsqrt(jnp.mean(raw * raw, -1, keepdims=True) + EPS)
    unit = raw * scale
    back = grad * cosine + pltpu.roll(grad * sine, 64, 1)
    term = jnp.sum(back * unit, 0, keepdims=True)
    back = back * gain
    return scale * (back - unit * jnp.mean(back * unit, -1, keepdims=True)), term


def behind_kernel(
    q, kv, kv_far, gq, gk, d_tok, dz_own, o, tok, gain, term_mid, down_mine, table,
    raw_hbm, qkv_hbm, mid_hbm, y1_hbm, h2_hbm, dgate_hbm, dup_hbm, mixed_hbm, h_hbm,
    mixed, tokens_grad, g_gate, g_up, g_q, g_k, g_v, g_down, g_out, s_in, s_mid, s_q, s_k,
    mix_buf, dx_buf, cols_gu, cols_qkv, rows_out, vec_out, do, acc, acc_far, out_far, in_far, dz, big_x, big_y, dqkv, gu_part, qkv_part, out_part,
    gu_mine, qkv_mine, rows, vec, ra, rb, rc, dh, raw, w_qkv, grad_mid, y1, cosine, sine, *rest
):
    mix_room, dh_room = rest[:3], rest[3:6]
    gu_room, qkv_room, out_room = rest[6:14], rest[14:22], rest[22:30]
    send_sem, recv_sem, here_sem = rest[30:]
    p = Place()
    w = Wire(send_sem, recv_sem, here_sem)
    loads = [
        w.here(h2_hbm, big_y),
        w.here(dgate_hbm, big_x.at[:, :, pl.ds(0, 768)]),
        w.here(dup_hbm, big_x.at[:, :, pl.ds(768, 768)]),
        w.here(raw_hbm, raw),
        w.here(qkv_hbm, w_qkv),
        w.here(mid_hbm, grad_mid),
        w.here(y1_hbm, y1),
        w.here(table.at[p.yl, 0], cosine),
        w.here(table.at[p.yl, 1], sine),
    ]
    dz[p.t] = dz_own[0]
    dz[15 - p.t] = dz_own[1]
    vec[...] = jnp.zeros_like(vec)
    vec[2:3] = term_mid[...]
    rows[0:48] = down_mine[...]
    meet(p.peers(("tp", "plane", "swap")))
    pair = p.at(yl=1 - p.yl)
    spread = []
    for far in (2, 1, 3, 0):
        for dc in (0, 1):
            z, core = p.up(far), lax.rem(p.core + dc, 2)
            for k in (0, 1):
                if far or dc:
                    dst = do.at[p.t if k == 0 else 15 - p.t]
                    spread.append(w.send(d_tok.at[2 * z + core, k], dst, p.at(z=z, core=core)))
                else:
                    do[p.t if k == 0 else 15 - p.t] = d_tok[p.t, k]

    def block(t, k):
        return dz.at[t if k == 0 else 15 - t]

    task_dz = [gather_z(w, p, lambda k: block(p.t, k), block)]
    advance(task_dz)
    for copy in loads[:3]:
        copy.wait()

    def grad_gu(i):
        cols = pl.ds(pl.multiple_of(i * 256, 256), 256)
        left = big_y[:, :, cols].reshape(1024, 256)
        for n in (0, 1):
            at = slice(n * 768, n * 768 + 768)
            to_pieces(gu_part, i, t_dot(left, big_x[:, :, at].reshape(1024, 768)).astype(BF), at)

    pl.loop(0, 8)(grad_gu)
    task_gu = [reduce_xy(w, p, gu_part, gu_room, gu_mine)]
    advance(task_gu)
    load = w.here(mixed_hbm, big_y)
    acc[...] = jnp.zeros_like(acc)
    acc_far[...] = jnp.zeros_like(acc_far)
    for copy in loads[3:]:
        copy.wait()
    for copy in spread:
        copy.wait_recv()
    back = []
    for j in range(7, -1, -1):
        at = pl.ds(j * 128, 128)
        keys = pl.ds(0, j * 128 + 128)
        tri, seen = edges(p, j)
        qj = both(q, at)
        dj = jnp.concatenate(
            [do[2 * j : 2 * j + 2, :, n * 128 : n * 128 + 128].reshape(128, 128) for n in (0, 1)], 0
        )
        near = weights_of(qj, kv[keys, 0:128], j, tri)
        far = weights_of(qj, kv_far[keys, 0:128], j, seen)
        scale = 1.0 / (jnp.sum(near, -1, keepdims=True) + jnp.sum(far, -1, keepdims=True))
        near = near * scale
        far = far * scale
        d_near = dot_t(dj, kv[keys, 128:256])
        d_far = dot_t(dj, kv_far[keys, 128:256])
        delta = jnp.sum(near * d_near, -1, keepdims=True) + jnp.sum(
            far * d_far, -1, keepdims=True
        )
        s_near = (near * (d_near - delta)).astype(BF)
        s_far = (far * (d_far - delta)).astype(BF)
        acc_far[keys, 0:128] += t_dot(s_far, qj)
        acc_far[keys, 128:256] += t_dot(far.astype(BF), dj)
        out_far[at, 0:128] = (acc_far[at, 0:128] * 128**-0.5).astype(BF)
        out_far[at, 128:256] = acc_far[at, 128:256].astype(BF)
        back.append((j, w.send(out_far.at[at], in_far.at[at], pair)))
        acc[keys, 0:128] += t_dot(s_near, qj)
        acc[keys, 128:256] += t_dot(near.astype(BF), dj)
        grad = jnp.dot(s_near, kv[keys, 0:128], preferred_element_type=F32)
        grad += jnp.dot(s_far, kv_far[keys, 0:128], preferred_element_type=F32)
        grad = (grad * 128**-0.5).astype(BF).astype(F32)
        for n in (0, 1):
            cols = slice(n * 128, n * 128 + 128)
            val, term = turn_norm_back(grad[cols], raw[at, cols], gq[...], cosine[at], sine[at])
            dqkv[2 * j : 2 * j + 2, :, cols] = val.astype(BF).reshape(2, 64, 128)
            vec[4:5, 0:128] += term
        if j in (7, 5, 3, 1, 0):
            advance(task_dz)
    advance(task_gu)
    advance(task_gu)
    run(*task_dz)
    for i in range(2):
        out = t_dot(
            o[:, :, i * 128 : i * 128 + 128].reshape(1024, 128), dz[...].reshape(1024, 2048)
        ).astype(BF)
        for f in range(8):
            out_part[f // 2, 2 * (f % 2) + i] = out[f * 16 : f * 16 + 16]
    load.wait()
    load = w.here(h_hbm, dz)
    task_out = [reduce_xy(w, p, out_part, out_room, rows.at[pl.ds(48, 16)])]
    advance(task_out)
    advance(task_out)
    for j, copy in back:
        at = pl.ds(j * 128, 128)
        copy.wait_recv()
        grad = add(acc[at, 0:128] * 128**-0.5, in_far[at, 0:128]).astype(BF).astype(F32)
        val, term = turn_norm_back(grad, raw[at, 256:384], gk[...], cosine[at], sine[at])
        dqkv[2 * j : 2 * j + 2, :, 256:384] = val.astype(BF).reshape(2, 64, 128)
        vec[5:6, 0:128] += term
        dv = add(acc[at, 128:256], in_far[at, 128:256]).astype(BF)
        dqkv[2 * j : 2 * j + 2, :, 384:512] = dv.reshape(2, 64, 128)
    task_dh = [reduce_z(w, p, big_x, dh_room, dh)]
    for n in (2, 1, 3, 0):
        zz = p.up(n)
        put(big_x, zz, dot_t(rows_of(dqkv, zz), w_qkv[...]).astype(BF))
        advance(task_dh)
    load.wait()

    def grad_qkv(i):
        cols = pl.ds(pl.multiple_of(i * 256, 256), 256)
        out = t_dot(dz[:, :, cols].reshape(1024, 256), dqkv[...].reshape(1024, 512))
        to_pieces(qkv_part, i, out.astype(BF), slice(0, 512))

    pl.loop(0, 8)(grad_qkv)
    task_qkv = [reduce_xy(w, p, qkv_part, qkv_room, qkv_mine)]
    advance(task_qkv)
    advance(task_qkv)
    advance(task_gu)
    advance(task_dh)
    advance(task_out)
    advance(task_out)
    advance(task_gu)
    run(*task_dh)
    total = jnp.zeros((1, 2048), F32)
    for k in (0, 1):
        x = tok[k].astype(F32)
        scale = lax.rsqrt(jnp.mean(x * x, -1, keepdims=True) + EPS)
        unit = x * scale
        total += jnp.sum(dh[k] * unit, 0, keepdims=True)
        wv = dh[k] * gain[...]
        dx = grad_mid[k] + scale * (wv - unit * jnp.mean(wv * unit, -1, keepdims=True))
        dx_buf[k] = dx.astype(BF)
    vec[0:1] = total
    task_vec = [sum_all(w, p, vec, (ra, rb, rc), vec_out)]
    task_mix = [reduce_z(w, p, big_y, mix_room, dh)]
    advance(task_vec)
    advance(task_qkv)
    advance(task_qkv)
    advance(task_gu)
    for _ in range(4):
        advance(task_mix)
    advance(task_out)
    advance(task_out)
    advance(task_vec)
    run(*task_gu)
    dealt = deal(w, p, gu_mine, cols_gu)
    advance(task_qkv)
    advance(task_qkv)
    advance(task_vec)
    advance(task_mix)
    run(*task_out)
    stay = p.yl == p.core
    n = w.n
    w.n += 1
    swap = pltpu.make_async_remote_copy(
        src_ref=rows,
        dst_ref=rows_out,
        send_sem=send_sem.at[n],
        recv_sem=recv_sem.at[n],
        device_id=p.at(yl=1 - p.yl, core=1 - p.core),
        device_id_type=MESH,
    )

    @pl.when(jnp.logical_not(stay))
    def _():
        swap.start()

    @pl.when(stay)
    def _():
        rows_out[...] = rows[...]

    run(*task_qkv)
    dealt += deal(w, p, qkv_mine, cols_qkv)
    run(*task_mix)
    for k in (0, 1):
        mix_buf[k] = (y1[k] + dh[k]).astype(BF)
    run(*task_vec)
    kept = [
        w.here(mix_buf, mixed),
        w.here(dx_buf, tokens_grad),
        w.here(vec_out.at[pl.ds(0, 1)], s_in),
        w.here(vec_out.at[pl.ds(2, 1)], s_mid),
        w.here(vec_out.at[pl.ds(4, 1), pl.ds(0, 128)], s_q),
        w.here(vec_out.at[pl.ds(5, 1), pl.ds(0, 128)], s_k),
    ]

    def place(first, at, val):
        end = at + val.shape[1]
        while at < end:
            stop = min(end, (at // 2048 + 1) * 2048)
            slot, begin = first + at // 2048, end - val.shape[1]
            grad_mid[slot // 4, slot % 4 * 16 : slot % 4 * 16 + 16, at % 2048 : (stop - 1) % 2048 + 1] = val[
                :, at - begin : stop - begin
            ].astype(F32)
            at = stop

    def piece(slot):
        return grad_mid.at[slot // 4, pl.ds(slot % 4 * 16, 16)]

    for copy in dealt[:7]:
        copy.wait_recv()
    for t in range(8):
        place(0, t * 768, cols_gu[t, :, 0:768])
        place(3, t * 768, cols_gu[t, :, 768:1536])
    for i in range(3):
        kept.append(w.here(piece(i), g_gate.at[:, pl.ds(i * 2048, 2048)]))
        kept.append(w.here(piece(3 + i), g_up.at[:, pl.ds(i * 2048, 2048)]))

    @pl.when(jnp.logical_not(stay))
    def _():
        swap.wait()

    y1[0] = rows_out[...].astype(F32)
    kept.append(w.here(y1.at[0, pl.ds(0, 48)], g_down))
    kept.append(w.here(y1.at[0, pl.ds(48, 16)], g_out))
    for copy in dealt[7:]:
        copy.wait_recv()
    for t in range(8):
        place(6, t * 256, cols_qkv[t, :, 0:256])
        place(7, t * 128, cols_qkv[t, :, 256:384])
        place(7, 1024 + t * 128, cols_qkv[t, :, 384:512])
    kept += [
        w.here(piece(6), g_q),
        w.here(grad_mid.at[1, pl.ds(48, 16), pl.ds(0, 1024)], g_k),
        w.here(grad_mid.at[1, pl.ds(48, 16), pl.ds(1024, 1024)], g_v),
    ]
    for copy in kept:
        copy.wait()
    w.finish()


def behind(*args):
    sds = jax.ShapeDtypeStruct
    return pl.pallas_call(
        behind_kernel,
        out_shape=(
            sds((2, 64, 2048), BF),
            sds((2, 64, 2048), BF),
            sds((16, 6144), F32),
            sds((16, 6144), F32),
            sds((16, 2048), F32),
            sds((16, 1024), F32),
            sds((16, 1024), F32),
            sds((48, 2048), F32),
            sds((16, 2048), F32),
            sds((1, 2048), F32),
            sds((1, 2048), F32),
            sds((1, 128), F32),
            sds((1, 128), F32),
        ),
        in_specs=[VMEM] * 12 + [HBM] * 10,
        out_specs=[HBM] * 13,
        scratch_shapes=[
            pltpu.VMEM((2, 64, 2048), BF),
            pltpu.VMEM((2, 64, 2048), BF),
            pltpu.VMEM((8, 16, 1536), BF),
            pltpu.VMEM((8, 16, 512), BF),
            pltpu.VMEM((64, 2048), BF),
            pltpu.VMEM((8, 2048), F32),
            pltpu.VMEM((16, 64, 256), BF),
            pltpu.VMEM((1024, 256), F32),
            pltpu.VMEM((1024, 256), F32),
            pltpu.VMEM((1024, 256), BF),
            pltpu.VMEM((1024, 256), BF),
            pltpu.VMEM((16, 64, 2048), BF),
            pltpu.VMEM((16, 64, 2048), BF),
            pltpu.VMEM((16, 64, 2048), BF),
            pltpu.VMEM((16, 64, 512), BF),
            pltpu.VMEM((4, 4, 128, 1536), BF),
            pltpu.VMEM((4, 4, 128, 512), BF),
            pltpu.VMEM((4, 4, 16, 2048), BF),
            pltpu.VMEM((8, 16, 1536), BF),
            pltpu.VMEM((8, 16, 512), BF),
            pltpu.VMEM((64, 2048), BF),
            pltpu.VMEM((8, 2048), F32),
            pltpu.VMEM((8, 8, 2048), F32),
            pltpu.VMEM((4, 8, 2048), F32),
            pltpu.VMEM((4, 8, 2048), F32),
            pltpu.VMEM((2, 64, 2048), F32),
            pltpu.VMEM((1024, 384), F32),
            pltpu.VMEM((2048, 512), BF),
            pltpu.VMEM((2, 64, 2048), F32),
            pltpu.VMEM((2, 64, 2048), F32),
            pltpu.VMEM((1024, 128), F32),
            pltpu.VMEM((1024, 128), F32),
        ]
        + z_room()
        + z_room()
        + xy_room(128, 1536, 1024)
        + xy_room(128, 512)
        + xy_room(16, 2048)
        + sems(160, 32),
        compiler_params=pltpu.CompilerParams(
            collective_id=1, has_side_effects=True, vmem_limit_bytes=63 * MB
        ),
        name="behind",
    )(*args)


def pour_kernel(*refs):
    n = (len(refs) - 1) // 2
    copies = [pltpu.make_async_copy(refs[i], refs[n + i], refs[-1].at[i]) for i in range(n)]
    for copy in copies:
        copy.start()
    for copy in copies:
        copy.wait()


def pour(*vals):
    return pl.pallas_call(
        pour_kernel,
        out_shape=tuple(jax.ShapeDtypeStruct(val.shape, val.dtype) for val in vals),
        in_specs=[HBM] * len(vals),
        out_specs=[HBM] * len(vals),
        scratch_shapes=[pltpu.SemaphoreType.DMA((len(vals),))],
        name="pour",
    )(*vals)


def rotary(width):
    half = width // 2
    freq = np.float32(THETA) ** (-2.0 * np.arange(half, dtype=np.float32) / np.float32(width))
    row = np.arange(1024)
    tile = row // 128
    tables = []
    for lane in (0, 1):
        place = np.where(tile < 4, 2 * tile + lane, 2 * tile + 1 - lane)
        angle = (place * 128 + row % 128).astype(np.float32)[:, None] * freq.astype(np.float32)
        angle = angle.astype(np.float64)
        cos, sin = np.cos(angle), np.sin(angle)
        tables.append(
            (np.concatenate([cos, cos], 1), np.concatenate([-sin, sin], 1))
        )
    return np.array(tables, dtype=np.float32)


def shards(
    tokens,
    gain_in,
    query_weight,
    key_weight,
    value_weight,
    gain_query,
    gain_key,
    out_weight,
    gain_mid,
    gate_weight,
    up_weight,
    down_weight,
    cotangent,
):
    width = tokens.shape[4]
    table = jnp.asarray(rotary(128))
    tok = tokens.reshape(2, 64, width)
    cot = cotangent.reshape(2, 64, width)
    gain_q, gain_k = gain_query.reshape(1, -1), gain_key.reshape(1, -1)
    h, w_qkv, query_b, kv, kv_far, raw, attended, g, w_out, w_gate, w_up, y_mid, rows_d, h2_own = ahead(
        tok,
        gain_in.reshape(1, -1),
        gain_q,
        gain_k,
        cot,
        gain_mid.reshape(1, -1),
        table,
        query_weight,
        key_weight,
        value_weight,
        out_weight,
        gate_weight,
        up_weight,
        down_weight,
    )
    h2, dgate_b, dup_b, mixed_part, grad_mid, dz_own, d_tok, term_mid, down_mine = mlp(
        h2_own,
        rows_d,
        w_gate,
        w_up,
        g,
        w_out.reshape(32, 64, width),
        y_mid,
        cot,
        gain_mid.reshape(1, -1),
    )
    results = behind(
        query_b,
        kv,
        kv_far,
        gain_q,
        gain_k,
        d_tok,
        dz_own,
        attended,
        tok,
        gain_in.reshape(1, -1),
        term_mid,
        down_mine,
        table,
        raw,
        w_qkv,
        grad_mid,
        y_mid,
        h2,
        dgate_b,
        dup_b,
        mixed_part,
        h,
    )

    mixed, tokens_grad, g_gate, g_up, g_q, g_k, g_v, g_down, g_out, s_in, s_mid, s_q, s_k = pour(*results)
    return (
        mixed.reshape(tokens.shape),
        tokens_grad.reshape(tokens.shape),
        s_in.reshape(-1),
        g_q,
        g_k,
        g_v,
        s_q.reshape(-1),
        s_k.reshape(-1),
        g_out,
        s_mid.reshape(-1),
        g_gate,
        g_up,
        g_down,
    )


def solution(mesh):
    fine = Mesh(mesh.devices.reshape(4, 2, 2, 4, 2), ALL)
    ctx, fsdp = ("z", "yl", "core"), FS
    act = P(fsdp, None, ctx, None, None)
    weight = P(fsdp, None)
    grad = P(ctx + fsdp, None)
    placed = (
        act, P(), weight, weight, weight, P(), P(), weight, P(), weight, weight, weight, act,
    )
    return jax.shard_map(
        shards,
        mesh=fine,
        in_specs=placed,
        out_specs=(act, act, P(), grad, grad, grad, P(), P(), grad, P(), grad, grad, grad),
        check_vma=False,
    )
```

```python
import functools

import jax
import jax.numpy as jnp
import numpy as np
from jax import lax
from jax.experimental import pallas as pl
from jax.experimental.pallas import tpu as pltpu
from jax.sharding import Mesh, PartitionSpec as P

EPS = 1e-06
THETA = 1000000.0
BF = jnp.bfloat16
F32 = jnp.float32
TP = ("z", "core")
FS = ("x", "yh")
DP = ("yl", "x", "yh")
ALL = ("z", "yl", "core", "x", "yh")
MESH = pl.DeviceIdType.MESH
VMEM = pl.BlockSpec(memory_space=pltpu.VMEM)
HBM = pl.BlockSpec(memory_space=pl.ANY)
MB = 2**20
LOG2E = 1.4426950408889634


class Place:
    def __init__(self):
        self.z, self.yl, self.core, self.x, self.yh = (lax.axis_index(a) for a in ALL)
        self.t = 2 * self.z + self.core
        self.shard = 2 * self.x + self.yh
        self.y = 2 * self.yh + self.yl

    def at(self, z=None, yl=None, core=None, x=None, yh=None):
        here = (self.z, self.yl, self.core, self.x, self.yh)
        return tuple(h if n is None else n for h, n in zip(here, (z, yl, core, x, yh)))

    def up(self, n):
        return lax.rem(self.z + n, 4)

    def east(self, n):
        return lax.rem(self.x + n, 4)

    def north(self, n):
        y = lax.rem(self.y + n, 4)
        return self.at(yh=y // 2, yl=lax.rem(y, 2))

    def turned(self):
        to_x = lax.rem(self.z + self.x, 4)
        goal = self.at(z=self.x, core=self.yh, x=to_x, yh=self.core)
        source = self.at(z=lax.rem(self.x + 4 - self.z, 4), core=self.yh, x=self.z, yh=self.core)
        stay = (self.x == 0) & (self.z == 0) & (self.core == self.yh)
        return goal, source, stay, 2 * to_x + self.core

    def peers(self, which):
        table = {
            "z": [self.at(z=self.up(1)), self.at(z=self.up(3))],
            "sib": [self.at(core=1 - self.core)],
            "x": [self.at(x=self.east(1)), self.at(x=self.east(3))],
            "cross": [self.at(yl=1 - self.yl, yh=1 - self.yh)],
            "pair": [self.at(yl=1 - self.yl)],
            "plane": [self.at(x=self.east(d)) for d in (1, 2, 3)]
            + [self.north(d) for d in (1, 2, 3)],
            "swap": [self.at(yl=1 - self.yl, core=1 - self.core)],

            "tp": [
                self.at(z=self.up(dz), core=lax.rem(self.core + dc, 2))
                for dz in range(4)
                for dc in range(2)
                if dz or dc
            ],
        }
        return [p for name in which for p in table[name]]


class Wire:
    def __init__(self, send_sem, recv_sem, here_sem):
        self.send_sem, self.recv_sem, self.here_sem = send_sem, recv_sem, here_sem
        self.n = self.m = 0
        self.sent = []

    def send(self, src, dst, peer):
        copy = pltpu.make_async_remote_copy(
            src_ref=src,
            dst_ref=dst,
            send_sem=self.send_sem.at[self.n],
            recv_sem=self.recv_sem.at[self.n],
            device_id=peer,
            device_id_type=MESH,
        )
        self.n += 1
        assert self.n <= self.send_sem.shape[0]
        copy.start()
        self.sent.append(copy)
        return copy

    def here(self, src, dst):
        copy = pltpu.make_async_copy(src, dst, self.here_sem.at[self.m])
        self.m += 1
        assert self.m <= self.here_sem.shape[0]
        copy.start()
        return copy

    def settle(self, copies):
        for copy in copies:
            copy.wait_send()
        self.sent = [one for one in self.sent if all(one is not copy for copy in copies)]

    def finish(self):
        for copy in self.sent:
            copy.wait_send()


def sems(n, m):
    return [
        pltpu.SemaphoreType.DMA((n,)),
        pltpu.SemaphoreType.DMA((n,)),
        pltpu.SemaphoreType.DMA((m,)),
    ]


def meet(peers, source=None, stay=None):
    barrier = pltpu.get_barrier_semaphore()
    for peer in peers:
        pl.semaphore_signal(barrier, inc=1, device_id=peer, device_id_type=MESH)
    if source is not None:

        @pl.when(jnp.logical_not(stay))
        def _():
            pl.semaphore_signal(barrier, inc=1, device_id=source, device_id_type=MESH)

        pl.semaphore_wait(barrier, jnp.where(stay, len(peers), len(peers) + 1))
    else:
        pl.semaphore_wait(barrier, len(peers))


def run(*tasks):
    tasks = list(tasks)
    while tasks:
        advance(tasks)


def advance(tasks):
    for task in list(tasks):
        try:
            next(task)
        except StopIteration:
            tasks.remove(task)


def gather_z(w, p, own, dst):
    up, down, sib = p.at(z=p.up(1)), p.at(z=p.up(3)), p.at(core=1 - p.core)
    before, after, far = (2 * p.up(n) + p.core for n in (3, 1, 2))
    u0 = w.send(own(0), dst(p.t, 0), up)
    d1 = w.send(own(1), dst(p.t, 1), down)
    u1 = w.send(own(1), dst(p.t, 1), up)
    d0 = w.send(own(0), dst(p.t, 0), down)
    s = [w.send(own(k), dst(p.t, k), sib) for k in (0, 1)]

    def on(t, k):
        s.append(w.send(dst(t, k), dst(t, k), sib))

    yield
    for copy in s[:2]:
        copy.wait_recv()
    yield
    u0.wait_recv()
    f0 = w.send(dst(before, 0), dst(before, 0), up)
    on(before, 0)
    d1.wait_recv()
    f1 = w.send(dst(after, 1), dst(after, 1), down)
    on(after, 1)
    yield
    u1.wait_recv()
    on(before, 1)
    d0.wait_recv()
    on(after, 0)
    yield
    for copy in s[2:6]:
        copy.wait_recv()
    yield
    f0.wait_recv()
    on(far, 0)
    f1.wait_recv()
    on(far, 1)
    yield
    for copy in s[6:]:
        copy.wait_recv()
    w.settle([u0, d1, u1, d0, f0, f1] + s)


def gather_yx(w, p, dst, n):
    east, west = p.at(x=p.east(1)), p.at(x=p.east(3))
    cross, pair = p.at(yl=1 - p.yl, yh=1 - p.yh), p.at(yl=1 - p.yl)
    half = n // 2
    me, flip = p.shard, 1 - 2 * p.yh
    west_s, east_s, far_s = (2 * p.east(k) + p.yh for k in (3, 1, 2))
    mine = p.yl * half
    other = half - mine

    def one(s, at, peer):
        return w.send(dst(s, at, half), dst(s, at, half), peer)

    c0 = one(me, mine, cross)
    yield
    c0.wait_recv()
    a0 = one(me + flip, other, pair)
    yield
    e0 = one(me, 0, east)
    w1 = one(me, half, west)
    e1 = one(me, half, east)
    w0 = one(me, 0, west)
    yield
    e0.wait_recv()
    f0 = one(west_s, 0, east)
    w1.wait_recv()
    f1 = one(east_s, half, west)
    a0.wait_recv()
    g0 = one(me + flip, 0, east)
    h1 = one(me + flip, half, west)
    g1 = one(me + flip, half, east)
    h0 = one(me + flip, 0, west)
    yield
    for copy in (e1, w0, f0, f1):
        copy.wait_recv()
    g0.wait_recv()
    i0 = one(west_s + flip, 0, east)
    h1.wait_recv()
    i1 = one(east_s + flip, half, west)
    yield
    for copy in (g1, h0, i0, i1):
        copy.wait_recv()


def gather_xy(w, p, dst, n, ready=None):
    east, west = p.at(x=p.east(1)), p.at(x=p.east(3))
    cross, pair = p.at(yl=1 - p.yl, yh=1 - p.yh), p.at(yl=1 - p.yl)
    half = n // 2
    me = p.shard
    west_s, east_s, far_s = (2 * p.east(k) + p.yh for k in (3, 1, 2))
    mine = p.yl * half
    other = half - mine
    flip = 1 - 2 * p.yh

    def one(s, at, peer):
        return w.send(dst(s, at, half), dst(s, at, half), peer)

    def along(s):
        return one(s + flip, other, pair)

    e0 = one(me, mine, east)
    w0 = one(me, mine, west)
    c0 = one(me, mine, cross)
    w1 = one(me, other, west)
    yield
    e0.wait_recv()
    fe = one(west_s, mine, east)
    c1 = one(west_s, mine, cross)
    e1 = one(me, other, east)
    w0.wait_recv()
    c2 = one(east_s, mine, cross)
    c0.wait_recv()
    a0 = along(me)
    yield
    fe.wait_recv()
    c3 = one(far_s, mine, cross)
    w1.wait_recv()
    fw = one(east_s, other, west)
    if ready:
        ready(east_s)
    yield
    c1.wait_recv()
    a1 = along(west_s)
    e1.wait_recv()
    if ready:
        ready(west_s)
    c2.wait_recv()
    a2 = along(east_s)
    yield
    fw.wait_recv()
    if ready:
        ready(far_s)
    c3.wait_recv()
    a3 = along(far_s)
    yield
    for s, a in ((me, a0), (west_s, a1), (east_s, a2), (far_s, a3)):
        a.wait_recv()
        if ready:
            ready(s + flip)


def norm_rope(raw, gain, cosine, sine):
    unit = raw * lax.rsqrt(jnp.mean(raw * raw, -1, keepdims=True) + EPS)
    vals = unit * gain
    return vals * cosine + pltpu.roll(vals, 64, 1) * sine


SCALE = 128**-0.5 * LOG2E


def dot_t(a, b):
    return lax.dot_general(a, b, (((1,), (1,)), ((), ())), preferred_element_type=F32)


def t_dot(a, b):
    return lax.dot_general(a, b, (((0,), (0,)), ((), ())), preferred_element_type=F32)


def both(ref, at):
    return jnp.concatenate([ref[at, 0:128], ref[at, 128:256]], 0)


def weights_of(q, k, j, edge):
    s = jnp.exp2(dot_t(q, k) * SCALE)
    last = jnp.where(edge, s[:, j * 128 :], 0.0)
    return last if j == 0 else jnp.concatenate([s[:, : j * 128], last], 1)


def edges(p, j):
    row = lax.broadcasted_iota(jnp.int32, (256, 128), 0) % 128
    col = lax.broadcasted_iota(jnp.int32, (256, 128), 1)
    seen = (p.yl if j < 4 else 1 - p.yl) * 128
    return col <= row, col < seen


def shard_rows(ref, n):
    return lambda s, at, m: ref.at[pl.ds(pl.multiple_of(s * n + at, 16), m)]


def ahead_kernel(
    tok, gain, gq, gk, cot, gain_mid, table, wq, wk, wv, wo, wg, wu, wd,
    h_out, qkv_out, q_out, kv_out, kv_far_out, raw_out, o_out, g_out, out_out, gate_out, up_out,
    y1_out, down_out, h2, q, kv, kv_far, raw, o, y1, h, w_qkv, g, w_out, w_gate, w_up, o_tok,
    cosine, sine, down, down_in, send_sem, recv_sem, here_sem
):
    p = Place()
    w = Wire(send_sem, recv_sem, here_sem)
    own = pl.ds(pl.multiple_of(p.shard * 256, 256), 256)

    def cut(n):
        return pl.ds(pl.multiple_of(p.t * n, n), n)

    load_qkv = [
        w.here(wq.at[:, cut(256)], w_qkv.at[own, pl.ds(0, 256)]),
        w.here(wk.at[:, cut(128)], w_qkv.at[own, pl.ds(256, 128)]),
        w.here(wv.at[:, cut(128)], w_qkv.at[own, pl.ds(384, 128)]),
    ]
    load_out = w.here(wo.at[pl.ds(pl.multiple_of(p.core * 128, 128), 128)], w_out.at[p.shard, p.core])
    load_gate = w.here(wg.at[:, cut(768)], w_gate.at[own])
    load_up = w.here(wu.at[:, cut(768)], w_up.at[own])
    goal, source, stay, at_down = p.turned()
    load_down = w.here(wd.at[pl.ds(pl.multiple_of(at_down * 96, 96), 96)], down)
    load_table = [w.here(table.at[p.yl, 0], cosine), w.here(table.at[p.yl, 1], sine)]
    for k in (0, 1):
        x = tok[k].astype(F32)
        unit = x * lax.rsqrt(jnp.mean(x * x, -1, keepdims=True) + EPS)
        h[p.t if k == 0 else 15 - p.t] = (unit * gain[...]).astype(BF)
    meet(p.peers(("tp", "x", "cross", "pair")), source, stay)
    pair, sib = p.at(yl=1 - p.yl), p.at(core=1 - p.core)

    def block_of(ref):
        return lambda t, k: ref.at[t if k == 0 else 15 - t]

    def part_out(s, at, n):
        return w_out.at[s, p.core, pl.ds(pl.multiple_of(at, 64), n)]

    twin = []

    def ready(s):
        twin.append(w.send(w_out.at[s, p.core], w_out.at[s, p.core], sib))

    at_h, at_g = block_of(h), block_of(g)
    task_h = [gather_z(w, p, lambda k: at_h(p.t, k), at_h)]
    task_qkv = [gather_xy(w, p, shard_rows(w_qkv, 256), 256)]
    for copy in load_qkv:
        copy.wait()
    advance(task_qkv)
    advance(task_h)
    g[p.t] = cot[0]
    g[15 - p.t] = cot[1]
    task_up = [gather_xy(w, p, shard_rows(w_up, 256), 256)]
    task_out = [gather_xy(w, p, part_out, 128, ready)]
    task_gate = [gather_yx(w, p, shard_rows(w_gate, 256), 256)]
    task_g = [gather_z(w, p, lambda k: at_g(p.t, k), at_g)]
    load_gate.wait()
    advance(task_gate)
    load_out.wait()
    ready(p.shard)
    load_down.wait()
    n = w.n
    w.n += 1
    turn = pltpu.make_async_remote_copy(
        src_ref=down,
        dst_ref=down_in,
        send_sem=send_sem.at[n],
        recv_sem=recv_sem.at[n],
        device_id=goal,
        device_id_type=MESH,
    )
    advance(task_h)
    advance(task_qkv)
    advance(task_gate)
    advance(task_h)
    advance(task_qkv)
    advance(task_out)
    advance(task_qkv)
    advance(task_h)
    advance(task_qkv)
    advance(task_h)
    advance(task_h)
    advance(task_qkv)
    advance(task_out)
    load_up.wait()
    advance(task_gate)
    advance(task_g)
    run(*task_h)
    kept = [w.here(h, h_out), w.here(w_qkv, qkv_out)]
    for copy in load_table:
        copy.wait()
    swaps = []
    for j in range(4):
        at = pl.ds(j * 256, 256)
        out = jnp.dot(
            h[4 * j : 4 * j + 4].reshape(256, 2048), w_qkv[...], preferred_element_type=F32
        )
        cos, sin = cosine[at], sine[at]
        kv[at, 0:128] = norm_rope(out[:, 256:384], gk[...], cos, sin).astype(BF)
        kv[at, 128:256] = out[:, 384:].astype(BF)
        swaps.append(w.send(kv.at[at], kv_far.at[at], pair))
        for n in (0, 1):
            cols = slice(n * 128, n * 128 + 128)
            q[at, cols] = norm_rope(out[:, cols], gq[...], cos, sin).astype(BF)
        raw[at] = out[:, :384]
        if j == 1:
            advance(task_out)
            advance(task_g)
        if j == 2:
            advance(task_up)
        if j == 3:
            advance(task_out)
    for j in range(8):
        at = pl.ds(j * 128, 128)
        keys = pl.ds(0, j * 128 + 128)
        if j % 2 == 0:
            swaps[j // 2].wait_recv()
        tri, seen = edges(p, j)
        qj = both(q, at)
        near = weights_of(qj, kv[keys, 0:128], j, tri)
        far = weights_of(qj, kv_far[keys, 0:128], j, seen)
        total = jnp.sum(near, -1, keepdims=True) + jnp.sum(far, -1, keepdims=True)
        out = jnp.dot(near.astype(BF), kv[keys, 128:256], preferred_element_type=F32)
        out += jnp.dot(far.astype(BF), kv_far[keys, 128:256], preferred_element_type=F32)
        out = (out / total).astype(BF)
        for n in (0, 1):
            o[2 * j : 2 * j + 2, :, n * 128 : n * 128 + 128] = out[
                n * 128 : n * 128 + 128
            ].reshape(2, 64, 128)
        if j in (1, 2):
            advance(task_g)
        if j == 3:
            advance(task_out)
        if j == 4:
            advance(task_gate)
            advance(task_g)
        if j == 6:
            advance(task_g)
        if j == 7:
            advance(task_up)
    spread = []
    for dz in (2, 1, 3, 0):
        for dc in range(2):
            z, core = p.up(dz), lax.rem(p.core + dc, 2)
            t = 2 * z + core
            for k in (0, 1):
                src = o.at[t if k == 0 else 15 - t]
                if dz or dc:
                    spread.append(w.send(src, o_tok.at[p.t, k], p.at(z=z, core=core)))
                else:
                    o_tok[p.t, k] = o[t if k == 0 else 15 - t]
    @pl.when(jnp.logical_not(stay))
    def _():
        turn.start()

    @pl.when(stay)
    def _():
        down_in[...] = down[...]

    kept += [
        w.here(q, q_out),
        w.here(kv, kv_out),
        w.here(kv_far, kv_far_out),
        w.here(raw, raw_out),
        w.here(o, o_out),
    ]
    advance(task_gate)
    run(*task_g)
    kept.append(w.here(g, g_out))
    advance(task_up)
    run(*task_out)
    advance(task_up)
    for copy in twin:
        copy.wait_recv()
    kept.append(w.here(w_out, out_out))
    for copy in spread:
        copy.wait_recv()
    for n in range(4):
        cols = slice(n * 512, n * 512 + 512)
        for k in (0, 1):
            y1[k, :, cols] = tok[k, :, cols].astype(F32)
        for t in range(8):
            part = jnp.dot(
                o_tok[t].reshape(128, 256),
                w_out[t, :, :, cols].reshape(256, 512),
                preferred_element_type=F32,
            )
            for k in (0, 1):
                y1[k, :, cols] += part[k * 64 : k * 64 + 64]
    for k in (0, 1):
        y = y1[k]
        unit = y * lax.rsqrt(jnp.mean(y * y, -1, keepdims=True) + EPS)
        h2[k] = (unit * gain_mid[...]).astype(BF)
    kept.append(w.here(y1, y1_out))
    run(*task_gate)
    kept.append(w.here(w_gate, gate_out))
    run(*task_up)
    kept.append(w.here(w_up, up_out))

    @pl.when(jnp.logical_not(stay))
    def _():
        turn.wait()

    kept.append(w.here(down_in, down_out))
    w.finish()
    for copy in kept:
        copy.wait()


def ahead(*args):
    sds = jax.ShapeDtypeStruct
    return pl.pallas_call(
        ahead_kernel,
        out_shape=(
            sds((16, 64, 2048), BF),
            sds((2048, 512), BF),
            sds((1024, 256), BF),
            sds((1024, 256), BF),
            sds((1024, 256), BF),
            sds((1024, 384), F32),
            sds((16, 64, 256), BF),
            sds((16, 64, 2048), BF),
            sds((8, 2, 128, 2048), BF),
            sds((2048, 768), BF),
            sds((2048, 768), BF),
            sds((2, 64, 2048), F32),
            sds((96, 2048), BF),
            sds((2, 64, 2048), BF),
        ),
        in_specs=[VMEM] * 6 + [HBM] * 8,
        out_specs=[HBM] * 13 + [VMEM],
        scratch_shapes=[
            pltpu.VMEM((1024, 256), BF),
            pltpu.VMEM((1024, 256), BF),
            pltpu.VMEM((1024, 256), BF),
            pltpu.VMEM((1024, 384), F32),
            pltpu.VMEM((16, 64, 256), BF),
            pltpu.VMEM((2, 64, 2048), F32),
            pltpu.VMEM((16, 64, 2048), BF),
            pltpu.VMEM((2048, 512), BF),
            pltpu.VMEM((16, 64, 2048), BF),
            pltpu.VMEM((8, 2, 128, 2048), BF),
            pltpu.VMEM((2048, 768), BF),
            pltpu.VMEM((2048, 768), BF),
            pltpu.VMEM((8, 2, 64, 256), BF),
            pltpu.VMEM((1024, 128), F32),
            pltpu.VMEM((1024, 128), F32),
            pltpu.VMEM((96, 2048), BF),
            pltpu.VMEM((96, 2048), BF),
        ]
        + sems(160, 32),
        compiler_params=pltpu.CompilerParams(
            collective_id=0, has_side_effects=True, vmem_limit_bytes=56 * MB
        ),
        name="ahead",
    )(*args)


def rows_of(ref, zz):
    c = ref.shape[-1]
    return jnp.concatenate(
        [ref[pl.ds(2 * zz, 2)].reshape(128, c), ref[pl.ds(14 - 2 * zz, 2)].reshape(128, c)], 0
    )


def put(ref, zz, val):
    c = ref.shape[-1]
    ref[pl.ds(2 * zz, 2)] = val[:128].reshape(2, 64, c)
    ref[pl.ds(14 - 2 * zz, 2)] = val[128:].reshape(2, 64, c)


def add(*vals):
    total = vals[0].astype(F32)
    for val in vals[1:]:
        total = total + val.astype(F32)
    return total


def z_room():
    return [
        pltpu.VMEM((4, 2, 64, 2048), BF),
        pltpu.VMEM((2, 64, 2048), BF),
        pltpu.VMEM((2, 2, 64, 2048), BF),
    ]


def reduce_z(w, p, part, room, out):
    mine, relay, last = room
    near = mine
    up, down, sib = p.at(z=p.up(1)), p.at(z=p.up(3)), p.at(core=1 - p.core)

    def block(n, core, k):
        t = 2 * p.up(n) + core
        return t if k == 0 else 15 - t

    first = {}

    def give(n):
        for k in (0, 1):
            first[n, k] = w.send(part.at[block(n, 1 - p.core, k)], near.at[n, k], sib)

    def fold(n, k):
        first[n, k].wait_recv()
        mine[n, k] = add(part[block(n, p.core, k)], near[n, k]).astype(BF)

    give(2)
    yield
    give(1)
    fold(2, 0)
    e0 = w.send(mine.at[2, 0], relay.at[0], up)
    fold(2, 1)
    e1 = w.send(mine.at[2, 1], relay.at[1], down)
    yield
    give(3)
    fold(1, 1)
    a1 = w.send(mine.at[1, 1], last.at[0, 1], up)
    fold(1, 0)
    yield
    give(0)
    fold(3, 0)
    b0 = w.send(mine.at[3, 0], last.at[1, 0], down)
    fold(3, 1)
    yield
    e0.wait_recv()
    mine[1, 0] = add(mine[1, 0], relay[0]).astype(BF)
    a0 = w.send(mine.at[1, 0], last.at[0, 0], up)
    e1.wait_recv()
    mine[3, 1] = add(mine[3, 1], relay[1]).astype(BF)
    b1 = w.send(mine.at[3, 1], last.at[1, 1], down)
    fold(0, 0)
    fold(0, 1)
    w.settle(list(first.values()))
    yield
    for k, (a, b) in enumerate(((a0, b0), (a1, b1))):
        a.wait_recv()
        b.wait_recv()
        out[k] = add(mine[0, k], last[0, k], last[1, k])


def xy_room(rows, cols, left=None):
    left = left or cols // 2
    return [
        pltpu.VMEM(lead + (rows, n), BF)
        for n in (left, cols - left)
        for lead in ((4,), (2, 4), (4,), (3,))
    ]


def put_half(out, cols, val):
    if len(out.shape) == 3:
        out[:, :, cols] = val.reshape(out.shape[0], out.shape[1], val.shape[1])
    else:
        out[:, cols] = val


def reduce_xy(w, p, part, room, out):
    ra, ta, sa, fa, rb, tb, sb, fb = room
    n_left = sa.shape[2]
    left, right = pl.ds(0, n_left), pl.ds(n_left, part.shape[3] - n_left)
    low, high = pl.ds(0, 2), pl.ds(2, 2)
    spans = (1, 2, 3)
    easts = [p.at(x=p.east(d)) for d in spans]
    norths = [p.north(d) for d in spans]
    xs = [p.east(d) for d in spans]
    ys = [lax.rem(p.y + d, 4) for d in spans]

    def start(bundle, r, t, peers):
        return [
            w.send(bundle(1, low), r.at[low], peers[0]),
            w.send(bundle(1, high), r.at[high], peers[2]),
            w.send(bundle(0, high), t.at[0, high], peers[0]),
            w.send(bundle(2, low), t.at[1, low], peers[2]),
        ]

    def of_x(d, some):
        return part.at[xs[d], some, :, left]

    def of_y(d, some):
        return part.at[some, ys[d], :, right]

    ca = start(of_x, ra, ta, easts)
    yield
    cb = start(of_y, rb, tb, norths)
    yield
    ca[0].wait_recv()
    for k in (0, 1):
        ra[k] = add(ra[k], part[xs[0], k, :, left]).astype(BF)
    ca.append(w.send(ra.at[low], ta.at[0, low], easts[0]))
    ca[1].wait_recv()
    for k in (2, 3):
        ra[k] = add(ra[k], part[xs[2], k, :, left]).astype(BF)
    ca.append(w.send(ra.at[high], ta.at[1, high], easts[2]))
    yield
    cb[0].wait_recv()
    for k in (0, 1):
        rb[k] = add(rb[k], part[k, ys[0], :, right]).astype(BF)
    cb.append(w.send(rb.at[low], tb.at[0, low], norths[0]))
    cb[1].wait_recv()
    for k in (2, 3):
        rb[k] = add(rb[k], part[k, ys[2], :, right]).astype(BF)
    cb.append(w.send(rb.at[high], tb.at[1, high], norths[2]))
    yield
    for copy in ca[2:]:
        copy.wait_recv()

    @pl.loop(0, 4)
    def _(y):
        sa[y] = add(part[p.x, y, :, left], ta[0, y], ta[1, y]).astype(BF)

    da = [w.send(sa.at[lax.rem(p.y + d, 4)], fa.at[d - 1], norths[d - 1]) for d in spans]
    yield
    for copy in cb[2:]:
        copy.wait_recv()

    @pl.loop(0, 4)
    def _(x):
        sb[x] = add(part[x, p.y, :, right], tb[0, x], tb[1, x]).astype(BF)

    db = [w.send(sb.at[p.east(d)], fb.at[d - 1], easts[d - 1]) for d in spans]
    yield
    for copy in da:
        copy.wait_recv()
    put_half(out, left, add(sa[p.y], fa[0], fa[1], fa[2]).astype(BF))
    yield
    for copy in db:
        copy.wait_recv()
    put_half(out, right, add(sb[p.x], fb[0], fb[1], fb[2]).astype(BF))


def mlp_kernel(
    h2_own, down_own, gate_hbm, up_hbm, g_hbm, out_hbm, y1, cot, gain,
    h2_out, dgate_out, dup_out, mixed_out, grad_mid, dz, d_tok, term, down_mine,
    h2, w_gate, w_up, w_down, g, gate, upper, part, down_part, act, dgate, dup, mixed, *rest
):
    zr, xr, (send_sem, recv_sem, here_sem) = rest[:3], rest[3:11], rest[11:]
    p = Place()
    w = Wire(send_sem, recv_sem, here_sem)
    loads = [w.here(gate_hbm, w_gate), w.here(up_hbm, w_up), w.here(g_hbm, g)]
    h2[p.t] = h2_own[0]
    h2[15 - p.t] = h2_own[1]
    w_down[pl.ds(pl.multiple_of(p.shard * 96, 96), 96)] = down_own[...]
    meet(p.peers(("z", "sib", "x", "plane", "cross")))

    def block(t, k):
        return h2.at[t if k == 0 else 15 - t]

    task_h = [gather_z(w, p, lambda k: block(p.t, k), block)]
    task_down = [gather_xy(w, p, shard_rows(w_down, 96), 96)]
    def forward(zz):
        left = rows_of(h2, zz)
        gate_n = jnp.dot(left, w_gate[...], preferred_element_type=F32)
        up_n = jnp.dot(left, w_up[...], preferred_element_type=F32)
        gate[zz] = gate_n
        upper[zz] = up_n
        put(act, zz, (gate_n * jax.nn.sigmoid(gate_n) * up_n).astype(BF))

    advance(task_h)
    advance(task_down)
    advance(task_h)
    for copy in loads:
        copy.wait()
    forward(p.z)
    advance(task_down)
    advance(task_h)
    advance(task_down)
    advance(task_h)
    advance(task_h)
    advance(task_down)
    forward(p.up(3))
    advance(task_h)
    forward(p.up(1))
    advance(task_down)
    run(*task_h)
    kept = [w.here(h2, h2_out)]
    forward(p.up(2))
    kept[0].wait()
    load = w.here(out_hbm.at[pl.ds(0, 16)], h2)

    @pl.loop(0, 6)
    def _(i):
        cols = pl.ds(pl.multiple_of(i * 128, 128), 128)
        left = act[:, :, cols].reshape(1024, 128)
        out = t_dot(left, g[...].reshape(1024, 2048)).astype(BF)
        for k in range(8):
            row = i * 8 + k
            piece = row // 3
            f = lax.rem(piece, 8)
            down_part[f // 2, 2 * lax.rem(f, 2) + piece // 8, pl.ds(pl.multiple_of(lax.rem(row, 3) * 16, 16), 16)] = out[
                k * 16 : k * 16 + 16
            ]

    run(*task_down)
    task_sum = [reduce_z(w, p, part, zr, grad_mid)]
    task_late = [reduce_xy(w, p, down_part, xr, down_mine)]
    advance(task_late)
    advance(task_late)
    for n in (2, 1, 3, 0):
        zz = p.up(n)
        gate_n, up_n = gate[zz], upper[zz]
        sig = jax.nn.sigmoid(gate_n)
        da = dot_t(rows_of(g, zz), w_down[...])
        silu = gate_n * sig
        d_gate = (da * up_n * sig * (1.0 + gate_n * (1.0 - sig))).astype(BF)
        d_up = (da * silu).astype(BF)
        put(dgate, zz, d_gate)
        put(dup, zz, d_up)
        total = dot_t(d_gate, w_gate[...]) + dot_t(d_up, w_up[...])
        put(part, zz, total.astype(BF))
        advance(task_sum)
        if n == 3:
            advance(task_late)
            advance(task_late)
    load2 = w.here(out_hbm.at[pl.ds(16, 16)], g)
    kept += [w.here(dgate, dgate_out), w.here(dup, dup_out)]
    advance(task_sum)

    @pl.loop(0, 4)
    def _(n):
        out = jnp.dot(rows_of(act, n), w_down[...], preferred_element_type=F32)
        put(mixed, n, out.astype(BF))

    kept.append(w.here(mixed, mixed_out))
    advance(task_late)
    run(*task_sum)
    advance(task_late)
    load.wait()
    load2.wait()
    term[...] = jnp.zeros_like(term)
    for k in (0, 1):
        y = y1[k]
        scale = lax.rsqrt(jnp.mean(y * y, -1, keepdims=True) + EPS)
        unit = y * scale
        dh = grad_mid[k]
        term[...] += jnp.sum(dh * unit, 0, keepdims=True)
        wv = dh * gain[...]
        dy = cot[k].astype(F32) + scale * (wv - unit * jnp.mean(wv * unit, -1, keepdims=True))
        grad_mid[k] = dy
        dz[k] = dy.astype(BF)
    dz_rows = dz[...].reshape(128, 2048)
    for t in range(8):
        half = h2 if t < 4 else g
        out = dot_t(dz_rows, half[4 * (t % 4) : 4 * (t % 4) + 4].reshape(256, 2048)).astype(BF)
        d_tok[t] = out.reshape(2, 64, 256)
    run(*task_late)
    w.finish()
    for copy in kept[1:]:
        copy.wait()


def mlp(*args):
    sds = jax.ShapeDtypeStruct
    return pl.pallas_call(
        mlp_kernel,
        out_shape=(
            sds((16, 64, 2048), BF),
            sds((16, 64, 768), BF),
            sds((16, 64, 768), BF),
            sds((16, 64, 2048), BF),
            sds((2, 64, 2048), F32),
            sds((2, 64, 2048), BF),
            sds((8, 2, 64, 256), BF),
            sds((1, 2048), F32),
            sds((48, 2048), BF),
        ),
        in_specs=[VMEM] * 2 + [HBM] * 4 + [VMEM] * 3,
        out_specs=[HBM] * 4 + [VMEM] * 5,
        scratch_shapes=[
            pltpu.VMEM((16, 64, 2048), BF),
            pltpu.VMEM((2048, 768), BF),
            pltpu.VMEM((2048, 768), BF),
            pltpu.VMEM((768, 2048), BF),
            pltpu.VMEM((16, 64, 2048), BF),
            pltpu.VMEM((4, 256, 768), F32),
            pltpu.VMEM((4, 256, 768), F32),
            pltpu.VMEM((16, 64, 2048), BF),
            pltpu.VMEM((4, 4, 48, 2048), BF),
            pltpu.VMEM((16, 64, 768), BF),
            pltpu.VMEM((16, 64, 768), BF),
            pltpu.VMEM((16, 64, 768), BF),
            pltpu.VMEM((16, 64, 2048), BF),
        ]
        + z_room()
        + xy_room(48, 2048)
        + sems(96, 12),
        compiler_params=pltpu.CompilerParams(
            collective_id=2, has_side_effects=True, vmem_limit_bytes=63 * MB
        ),
        name="mlp",
    )(*args)


def sum_all(w, p, vec, slots, out):
    ra, rb, rc = slots
    ra[p.t] = vec[...]
    first = [w.send(ra.at[p.t], ra.at[p.t], peer) for peer in p.peers(("tp",))]
    yield
    for copy in first:
        copy.wait_recv()
    rb[p.x] = sum((ra[i] for i in range(1, 8)), ra[0])
    xs = [w.send(rb.at[p.x], rb.at[p.x], p.at(x=p.east(d))) for d in (1, 2, 3)]
    yield
    for copy in xs:
        copy.wait_recv()
    rc[p.y] = sum((rb[i] for i in range(1, 4)), rb[0])
    ys = [w.send(rc.at[p.y], rc.at[p.y], p.north(d)) for d in (1, 2, 3)]
    yield
    for copy in ys:
        copy.wait_recv()
    out[...] = sum((rc[i] for i in range(1, 4)), rc[0])


def deal(w, p, src, dst):
    dst[p.t] = src[p.t]
    copies = []
    for dz in (2, 1, 3, 0):
        for dc in range(2):
            if dz or dc:
                z, core = p.up(dz), lax.rem(p.core + dc, 2)
                copies.append(w.send(src.at[2 * z + core], dst.at[p.t], p.at(z=z, core=core)))
    return copies


def to_pieces(part, i, out, cols):
    z, yl = i // 2, lax.rem(i, 2)
    for r in range(16):
        core, f = r // 8, r % 8
        at = pl.ds(pl.multiple_of((2 * z + core) * 16, 16), 16)
        part[f // 2, 2 * (f % 2) + yl, at, cols] = out[r * 16 : r * 16 + 16]


def turn_norm_back(grad, raw, gain, cosine, sine):
    scale = lax.rsqrt(jnp.mean(raw * raw, -1, keepdims=True) + EPS)
    unit = raw * scale
    back = grad * cosine + pltpu.roll(grad * sine, 64, 1)
    term = jnp.sum(back * unit, 0, keepdims=True)
    back = back * gain
    return scale * (back - unit * jnp.mean(back * unit, -1, keepdims=True)), term


def behind_kernel(
    q, kv, kv_far, gq, gk, d_tok, dz_own, o, tok, gain, term_mid, down_mine, table,
    raw_hbm, qkv_hbm, mid_hbm, y1_hbm, h2_hbm, dgate_hbm, dup_hbm, mixed_hbm, h_hbm,
    mixed, tokens_grad, g_gate, g_up, g_q, g_k, g_v, g_down, g_out, s_in, s_mid, s_q, s_k,
    mix_buf, dx_buf, cols_gu, cols_qkv, rows_out, vec_out, do, acc, acc_far, out_far, in_far, dz, big_x, big_y, dqkv, gu_part, qkv_part, out_part,
    gu_mine, qkv_mine, rows, vec, ra, rb, rc, dh, raw, w_qkv, grad_mid, y1, cosine, sine, *rest
):
    mix_room, dh_room = rest[:3], rest[3:6]
    gu_room, qkv_room, out_room = rest[6:14], rest[14:22], rest[22:30]
    send_sem, recv_sem, here_sem = rest[30:]
    p = Place()
    w = Wire(send_sem, recv_sem, here_sem)
    loads = [
        w.here(h2_hbm, big_y),
        w.here(dgate_hbm, big_x.at[:, :, pl.ds(0, 768)]),
        w.here(dup_hbm, big_x.at[:, :, pl.ds(768, 768)]),
        w.here(raw_hbm, raw),
        w.here(qkv_hbm, w_qkv),
        w.here(mid_hbm, grad_mid),
        w.here(y1_hbm, y1),
        w.here(table.at[p.yl, 0], cosine),
        w.here(table.at[p.yl, 1], sine),
    ]
    dz[p.t] = dz_own[0]
    dz[15 - p.t] = dz_own[1]
    vec[...] = jnp.zeros_like(vec)
    vec[2:3] = term_mid[...]
    rows[0:48] = down_mine[...]
    meet(p.peers(("tp", "plane", "swap")))
    pair = p.at(yl=1 - p.yl)
    spread = []
    for far in (2, 1, 3, 0):
        for dc in (0, 1):
            z, core = p.up(far), lax.rem(p.core + dc, 2)
            for k in (0, 1):
                if far or dc:
                    dst = do.at[p.t if k == 0 else 15 - p.t]
                    spread.append(w.send(d_tok.at[2 * z + core, k], dst, p.at(z=z, core=core)))
                else:
                    do[p.t if k == 0 else 15 - p.t] = d_tok[p.t, k]

    def block(t, k):
        return dz.at[t if k == 0 else 15 - t]

    task_dz = [gather_z(w, p, lambda k: block(p.t, k), block)]
    advance(task_dz)
    for copy in loads[:3]:
        copy.wait()

    def grad_gu(i):
        cols = pl.ds(pl.multiple_of(i * 256, 256), 256)
        left = big_y[:, :, cols].reshape(1024, 256)
        for n in (0, 1):
            at = slice(n * 768, n * 768 + 768)
            to_pieces(gu_part, i, t_dot(left, big_x[:, :, at].reshape(1024, 768)).astype(BF), at)

    pl.loop(0, 8)(grad_gu)
    task_gu = [reduce_xy(w, p, gu_part, gu_room, gu_mine)]
    advance(task_gu)
    load = w.here(mixed_hbm, big_y)
    acc[...] = jnp.zeros_like(acc)
    acc_far[...] = jnp.zeros_like(acc_far)
    for copy in loads[3:]:
        copy.wait()
    for copy in spread:
        copy.wait_recv()
    back = []
    for j in range(7, -1, -1):
        at = pl.ds(j * 128, 128)
        keys = pl.ds(0, j * 128 + 128)
        tri, seen = edges(p, j)
        qj = both(q, at)
        dj = jnp.concatenate(
            [do[2 * j : 2 * j + 2, :, n * 128 : n * 128 + 128].reshape(128, 128) for n in (0, 1)], 0
        )
        near = weights_of(qj, kv[keys, 0:128], j, tri)
        far = weights_of(qj, kv_far[keys, 0:128], j, seen)
        scale = 1.0 / (jnp.sum(near, -1, keepdims=True) + jnp.sum(far, -1, keepdims=True))
        near = near * scale
        far = far * scale
        d_near = dot_t(dj, kv[keys, 128:256])
        d_far = dot_t(dj, kv_far[keys, 128:256])
        delta = jnp.sum(near * d_near, -1, keepdims=True) + jnp.sum(
            far * d_far, -1, keepdims=True
        )
        s_near = (near * (d_near - delta)).astype(BF)
        s_far = (far * (d_far - delta)).astype(BF)
        acc_far[keys, 0:128] += t_dot(s_far, qj)
        acc_far[keys, 128:256] += t_dot(far.astype(BF), dj)
        out_far[at, 0:128] = (acc_far[at, 0:128] * 128**-0.5).astype(BF)
        out_far[at, 128:256] = acc_far[at, 128:256].astype(BF)
        back.append((j, w.send(out_far.at[at], in_far.at[at], pair)))
        acc[keys, 0:128] += t_dot(s_near, qj)
        acc[keys, 128:256] += t_dot(near.astype(BF), dj)
        grad = jnp.dot(s_near, kv[keys, 0:128], preferred_element_type=F32)
        grad += jnp.dot(s_far, kv_far[keys, 0:128], preferred_element_type=F32)
        grad = (grad * 128**-0.5).astype(BF).astype(F32)
        for n in (0, 1):
            cols = slice(n * 128, n * 128 + 128)
            val, term = turn_norm_back(grad[cols], raw[at, cols], gq[...], cosine[at], sine[at])
            dqkv[2 * j : 2 * j + 2, :, cols] = val.astype(BF).reshape(2, 64, 128)
            vec[4:5, 0:128] += term
        if j in (7, 5, 3, 1, 0):
            advance(task_dz)
    advance(task_gu)
    advance(task_gu)
    run(*task_dz)
    for i in range(2):
        out = t_dot(
            o[:, :, i * 128 : i * 128 + 128].reshape(1024, 128), dz[...].reshape(1024, 2048)
        ).astype(BF)
        for f in range(8):
            out_part[f // 2, 2 * (f % 2) + i] = out[f * 16 : f * 16 + 16]
    load.wait()
    load = w.here(h_hbm, dz)
    task_out = [reduce_xy(w, p, out_part, out_room, rows.at[pl.ds(48, 16)])]
    advance(task_out)
    advance(task_out)
    for j, copy in back:
        at = pl.ds(j * 128, 128)
        copy.wait_recv()
        grad = add(acc[at, 0:128] * 128**-0.5, in_far[at, 0:128]).astype(BF).astype(F32)
        val, term = turn_norm_back(grad, raw[at, 256:384], gk[...], cosine[at], sine[at])
        dqkv[2 * j : 2 * j + 2, :, 256:384] = val.astype(BF).reshape(2, 64, 128)
        vec[5:6, 0:128] += term
        dv = add(acc[at, 128:256], in_far[at, 128:256]).astype(BF)
        dqkv[2 * j : 2 * j + 2, :, 384:512] = dv.reshape(2, 64, 128)
    task_dh = [reduce_z(w, p, big_x, dh_room, dh)]
    for n in (2, 1, 3, 0):
        zz = p.up(n)
        put(big_x, zz, dot_t(rows_of(dqkv, zz), w_qkv[...]).astype(BF))
        advance(task_dh)
    load.wait()

    def grad_qkv(i):
        cols = pl.ds(pl.multiple_of(i * 256, 256), 256)
        out = t_dot(dz[:, :, cols].reshape(1024, 256), dqkv[...].reshape(1024, 512))
        to_pieces(qkv_part, i, out.astype(BF), slice(0, 512))

    pl.loop(0, 8)(grad_qkv)
    task_qkv = [reduce_xy(w, p, qkv_part, qkv_room, qkv_mine)]
    advance(task_qkv)
    advance(task_qkv)
    advance(task_gu)
    advance(task_dh)
    advance(task_out)
    advance(task_out)
    advance(task_gu)
    run(*task_dh)
    total = jnp.zeros((1, 2048), F32)
    for k in (0, 1):
        x = tok[k].astype(F32)
        scale = lax.rsqrt(jnp.mean(x * x, -1, keepdims=True) + EPS)
        unit = x * scale
        total += jnp.sum(dh[k] * unit, 0, keepdims=True)
        wv = dh[k] * gain[...]
        dx = grad_mid[k] + scale * (wv - unit * jnp.mean(wv * unit, -1, keepdims=True))
        dx_buf[k] = dx.astype(BF)
    vec[0:1] = total
    task_vec = [sum_all(w, p, vec, (ra, rb, rc), vec_out)]
    task_mix = [reduce_z(w, p, big_y, mix_room, dh)]
    advance(task_vec)
    advance(task_qkv)
    advance(task_qkv)
    advance(task_gu)
    for _ in range(4):
        advance(task_mix)
    advance(task_out)
    advance(task_out)
    advance(task_vec)
    run(*task_gu)
    dealt = deal(w, p, gu_mine, cols_gu)
    advance(task_qkv)
    advance(task_qkv)
    advance(task_vec)
    advance(task_mix)
    run(*task_out)
    stay = p.yl == p.core
    n = w.n
    w.n += 1
    swap = pltpu.make_async_remote_copy(
        src_ref=rows,
        dst_ref=rows_out,
        send_sem=send_sem.at[n],
        recv_sem=recv_sem.at[n],
        device_id=p.at(yl=1 - p.yl, core=1 - p.core),
        device_id_type=MESH,
    )

    @pl.when(jnp.logical_not(stay))
    def _():
        swap.start()

    @pl.when(stay)
    def _():
        rows_out[...] = rows[...]

    run(*task_qkv)
    dealt += deal(w, p, qkv_mine, cols_qkv)
    run(*task_mix)
    for k in (0, 1):
        mix_buf[k] = (y1[k] + dh[k]).astype(BF)
    run(*task_vec)
    kept = [
        w.here(mix_buf, mixed),
        w.here(dx_buf, tokens_grad),
        w.here(vec_out.at[pl.ds(0, 1)], s_in),
        w.here(vec_out.at[pl.ds(2, 1)], s_mid),
        w.here(vec_out.at[pl.ds(4, 1), pl.ds(0, 128)], s_q),
        w.here(vec_out.at[pl.ds(5, 1), pl.ds(0, 128)], s_k),
    ]

    def place(first, at, val):
        end = at + val.shape[1]
        while at < end:
            stop = min(end, (at // 2048 + 1) * 2048)
            slot, begin = first + at // 2048, end - val.shape[1]
            grad_mid[slot // 4, slot % 4 * 16 : slot % 4 * 16 + 16, at % 2048 : (stop - 1) % 2048 + 1] = val[
                :, at - begin : stop - begin
            ].astype(F32)
            at = stop

    def piece(slot):
        return grad_mid.at[slot // 4, pl.ds(slot % 4 * 16, 16)]

    for copy in dealt[:7]:
        copy.wait_recv()
    for t in range(8):
        place(0, t * 768, cols_gu[t, :, 0:768])
        place(3, t * 768, cols_gu[t, :, 768:1536])
    for i in range(3):
        kept.append(w.here(piece(i), g_gate.at[:, pl.ds(i * 2048, 2048)]))
        kept.append(w.here(piece(3 + i), g_up.at[:, pl.ds(i * 2048, 2048)]))

    @pl.when(jnp.logical_not(stay))
    def _():
        swap.wait()

    y1[0] = rows_out[...].astype(F32)
    kept.append(w.here(y1.at[0, pl.ds(0, 48)], g_down))
    kept.append(w.here(y1.at[0, pl.ds(48, 16)], g_out))
    for copy in dealt[7:]:
        copy.wait_recv()
    for t in range(8):
        place(6, t * 256, cols_qkv[t, :, 0:256])
        place(7, t * 128, cols_qkv[t, :, 256:384])
        place(7, 1024 + t * 128, cols_qkv[t, :, 384:512])
    kept += [
        w.here(piece(6), g_q),
        w.here(grad_mid.at[1, pl.ds(48, 16), pl.ds(0, 1024)], g_k),
        w.here(grad_mid.at[1, pl.ds(48, 16), pl.ds(1024, 1024)], g_v),
    ]
    for copy in kept:
        copy.wait()
    w.finish()


def behind(*args):
    sds = jax.ShapeDtypeStruct
    return pl.pallas_call(
        behind_kernel,
        out_shape=(
            sds((2, 64, 2048), BF),
            sds((2, 64, 2048), BF),
            sds((16, 6144), F32),
            sds((16, 6144), F32),
            sds((16, 2048), F32),
            sds((16, 1024), F32),
            sds((16, 1024), F32),
            sds((48, 2048), F32),
            sds((16, 2048), F32),
            sds((1, 2048), F32),
            sds((1, 2048), F32),
            sds((1, 128), F32),
            sds((1, 128), F32),
        ),
        in_specs=[VMEM] * 12 + [HBM] * 10,
        out_specs=[HBM] * 13,
        scratch_shapes=[
            pltpu.VMEM((2, 64, 2048), BF),
            pltpu.VMEM((2, 64, 2048), BF),
            pltpu.VMEM((8, 16, 1536), BF),
            pltpu.VMEM((8, 16, 512), BF),
            pltpu.VMEM((64, 2048), BF),
            pltpu.VMEM((8, 2048), F32),
            pltpu.VMEM((16, 64, 256), BF),
            pltpu.VMEM((1024, 256), F32),
            pltpu.VMEM((1024, 256), F32),
            pltpu.VMEM((1024, 256), BF),
            pltpu.VMEM((1024, 256), BF),
            pltpu.VMEM((16, 64, 2048), BF),
            pltpu.VMEM((16, 64, 2048), BF),
            pltpu.VMEM((16, 64, 2048), BF),
            pltpu.VMEM((16, 64, 512), BF),
            pltpu.VMEM((4, 4, 128, 1536), BF),
            pltpu.VMEM((4, 4, 128, 512), BF),
            pltpu.VMEM((4, 4, 16, 2048), BF),
            pltpu.VMEM((8, 16, 1536), BF),
            pltpu.VMEM((8, 16, 512), BF),
            pltpu.VMEM((64, 2048), BF),
            pltpu.VMEM((8, 2048), F32),
            pltpu.VMEM((8, 8, 2048), F32),
            pltpu.VMEM((4, 8, 2048), F32),
            pltpu.VMEM((4, 8, 2048), F32),
            pltpu.VMEM((2, 64, 2048), F32),
            pltpu.VMEM((1024, 384), F32),
            pltpu.VMEM((2048, 512), BF),
            pltpu.VMEM((2, 64, 2048), F32),
            pltpu.VMEM((2, 64, 2048), F32),
            pltpu.VMEM((1024, 128), F32),
            pltpu.VMEM((1024, 128), F32),
        ]
        + z_room()
        + z_room()
        + xy_room(128, 1536, 1024)
        + xy_room(128, 512)
        + xy_room(16, 2048)
        + sems(160, 32),
        compiler_params=pltpu.CompilerParams(
            collective_id=1, has_side_effects=True, vmem_limit_bytes=63 * MB
        ),
        name="behind",
    )(*args)


def pour_kernel(*refs):
    n = (len(refs) - 2) // 3
    taken, given, held, (in_sem, out_sem) = refs[:n], refs[n : 2 * n], refs[2 * n : 3 * n], refs[3 * n :]
    first = [pltpu.make_async_copy(taken[i], held[i], in_sem.at[i]) for i in range(n)]
    second = [pltpu.make_async_copy(held[i], given[i], out_sem.at[i]) for i in range(n)]
    for copy in first:
        copy.start()
    for i in range(n):
        first[i].wait()
        second[i].start()
    for copy in second:
        copy.wait()


def pour(*vals):
    n = len(vals)
    return pl.pallas_call(
        pour_kernel,
        out_shape=tuple(jax.ShapeDtypeStruct(val.shape, val.dtype) for val in vals),
        in_specs=[HBM] * n,
        out_specs=[HBM] * n,
        scratch_shapes=[pltpu.VMEM(val.shape, val.dtype) for val in vals]
        + [pltpu.SemaphoreType.DMA((n,)), pltpu.SemaphoreType.DMA((n,))],
        compiler_params=pltpu.CompilerParams(vmem_limit_bytes=16 * MB),
        name="pour",
    )(*vals)


def rotary(width):
    half = width // 2
    freq = np.float32(THETA) ** (-2.0 * np.arange(half, dtype=np.float32) / np.float32(width))
    row = np.arange(1024)
    tile = row // 128
    tables = []
    for lane in (0, 1):
        place = np.where(tile < 4, 2 * tile + lane, 2 * tile + 1 - lane)
        angle = (place * 128 + row % 128).astype(np.float32)[:, None] * freq.astype(np.float32)
        angle = angle.astype(np.float64)
        cos, sin = np.cos(angle), np.sin(angle)
        tables.append(
            (np.concatenate([cos, cos], 1), np.concatenate([-sin, sin], 1))
        )
    return np.array(tables, dtype=np.float32)


def shards(
    tokens,
    gain_in,
    query_weight,
    key_weight,
    value_weight,
    gain_query,
    gain_key,
    out_weight,
    gain_mid,
    gate_weight,
    up_weight,
    down_weight,
    cotangent,
):
    width = tokens.shape[4]
    table = jnp.asarray(rotary(128))
    tok = tokens.reshape(2, 64, width)
    cot = cotangent.reshape(2, 64, width)
    gain_q, gain_k = gain_query.reshape(1, -1), gain_key.reshape(1, -1)
    h, w_qkv, query_b, kv, kv_far, raw, attended, g, w_out, w_gate, w_up, y_mid, rows_d, h2_own = ahead(
        tok,
        gain_in.reshape(1, -1),
        gain_q,
        gain_k,
        cot,
        gain_mid.reshape(1, -1),
        table,
        query_weight,
        key_weight,
        value_weight,
        out_weight,
        gate_weight,
        up_weight,
        down_weight,
    )
    h2, dgate_b, dup_b, mixed_part, grad_mid, dz_own, d_tok, term_mid, down_mine = mlp(
        h2_own,
        rows_d,
        w_gate,
        w_up,
        g,
        w_out.reshape(32, 64, width),
        y_mid,
        cot,
        gain_mid.reshape(1, -1),
    )
    results = behind(
        query_b,
        kv,
        kv_far,
        gain_q,
        gain_k,
        d_tok,
        dz_own,
        attended,
        tok,
        gain_in.reshape(1, -1),
        term_mid,
        down_mine,
        table,
        raw,
        w_qkv,
        grad_mid,
        y_mid,
        h2,
        dgate_b,
        dup_b,
        mixed_part,
        h,
    )

    mixed, tokens_grad, g_gate, g_up, g_q, g_k, g_v, g_down, g_out, s_in, s_mid, s_q, s_k = pour(*results)
    return (
        mixed.reshape(tokens.shape),
        tokens_grad.reshape(tokens.shape),
        s_in.reshape(-1),
        g_q,
        g_k,
        g_v,
        s_q.reshape(-1),
        s_k.reshape(-1),
        g_out,
        s_mid.reshape(-1),
        g_gate,
        g_up,
        g_down,
    )


def solution(mesh):
    fine = Mesh(mesh.devices.reshape(4, 2, 2, 4, 2), ALL)
    ctx, fsdp = ("z", "yl", "core"), FS
    act = P(fsdp, None, ctx, None, None)
    weight = P(fsdp, None)
    grad = P(ctx + fsdp, None)
    placed = (
        act, P(), weight, weight, weight, P(), P(), weight, P(), weight, weight, weight, act,
    )
    return jax.shard_map(
        shards,
        mesh=fine,
        in_specs=placed,
        out_specs=(act, act, P(), grad, grad, grad, P(), P(), grad, P(), grad, grad, grad),
        check_vma=False,
    )
```

```python
import functools

import jax
import jax.numpy as jnp
import numpy as np
from jax import lax
from jax.experimental import pallas as pl
from jax.experimental.pallas import tpu as pltpu
from jax.sharding import Mesh, PartitionSpec as P

EPS = 1e-06
THETA = 1000000.0
BF = jnp.bfloat16
F32 = jnp.float32
TP = ("z", "core")
FS = ("x", "yh")
DP = ("yl", "x", "yh")
ALL = ("z", "yl", "core", "x", "yh")
MESH = pl.DeviceIdType.MESH
VMEM = pl.BlockSpec(memory_space=pltpu.VMEM)
HBM = pl.BlockSpec(memory_space=pl.ANY)
MB = 2**20
LOG2E = 1.4426950408889634


class Place:
    def __init__(self):
        self.z, self.yl, self.core, self.x, self.yh = (lax.axis_index(a) for a in ALL)
        self.t = 2 * self.z + self.core
        self.shard = 2 * self.x + self.yh
        self.y = 2 * self.yh + self.yl

    def at(self, z=None, yl=None, core=None, x=None, yh=None):
        here = (self.z, self.yl, self.core, self.x, self.yh)
        return tuple(h if n is None else n for h, n in zip(here, (z, yl, core, x, yh)))

    def up(self, n):
        return lax.rem(self.z + n, 4)

    def east(self, n):
        return lax.rem(self.x + n, 4)

    def north(self, n):
        y = lax.rem(self.y + n, 4)
        return self.at(yh=y // 2, yl=lax.rem(y, 2))

    def turned(self):
        to_x = lax.rem(self.z + self.x, 4)
        goal = self.at(z=self.x, core=self.yh, x=to_x, yh=self.core)
        source = self.at(z=lax.rem(self.x + 4 - self.z, 4), core=self.yh, x=self.z, yh=self.core)
        stay = (self.x == 0) & (self.z == 0) & (self.core == self.yh)
        return goal, source, stay, 2 * to_x + self.core

    def peers(self, which):
        table = {
            "z": [self.at(z=self.up(1)), self.at(z=self.up(3))],
            "sib": [self.at(core=1 - self.core)],
            "x": [self.at(x=self.east(1)), self.at(x=self.east(3))],
            "cross": [self.at(yl=1 - self.yl, yh=1 - self.yh)],
            "pair": [self.at(yl=1 - self.yl)],
            "plane": [self.at(x=self.east(d)) for d in (1, 2, 3)]
            + [self.north(d) for d in (1, 2, 3)],
            "swap": [self.at(yl=1 - self.yl, core=1 - self.core)],

            "tp": [
                self.at(z=self.up(dz), core=lax.rem(self.core + dc, 2))
                for dz in range(4)
                for dc in range(2)
                if dz or dc
            ],
        }
        return [p for name in which for p in table[name]]


class Wire:
    def __init__(self, send_sem, recv_sem, here_sem):
        self.send_sem, self.recv_sem, self.here_sem = send_sem, recv_sem, here_sem
        self.n = self.m = 0
        self.sent = []

    def send(self, src, dst, peer):
        copy = pltpu.make_async_remote_copy(
            src_ref=src,
            dst_ref=dst,
            send_sem=self.send_sem.at[self.n],
            recv_sem=self.recv_sem.at[self.n],
            device_id=peer,
            device_id_type=MESH,
        )
        self.n += 1
        assert self.n <= self.send_sem.shape[0]
        copy.start()
        self.sent.append(copy)
        return copy

    def here(self, src, dst):
        copy = pltpu.make_async_copy(src, dst, self.here_sem.at[self.m])
        self.m += 1
        assert self.m <= self.here_sem.shape[0]
        copy.start()
        return copy

    def settle(self, copies):
        for copy in copies:
            copy.wait_send()
        self.sent = [one for one in self.sent if all(one is not copy for copy in copies)]

    def finish(self):
        for copy in self.sent:
            copy.wait_send()


def sems(n, m):
    return [
        pltpu.SemaphoreType.DMA((n,)),
        pltpu.SemaphoreType.DMA((n,)),
        pltpu.SemaphoreType.DMA((m,)),
    ]


def meet(peers, source=None, stay=None):
    barrier = pltpu.get_barrier_semaphore()
    for peer in peers:
        pl.semaphore_signal(barrier, inc=1, device_id=peer, device_id_type=MESH)
    if source is not None:

        @pl.when(jnp.logical_not(stay))
        def _():
            pl.semaphore_signal(barrier, inc=1, device_id=source, device_id_type=MESH)

        pl.semaphore_wait(barrier, jnp.where(stay, len(peers), len(peers) + 1))
    else:
        pl.semaphore_wait(barrier, len(peers))


def run(*tasks):
    tasks = list(tasks)
    while tasks:
        advance(tasks)


def advance(tasks):
    for task in list(tasks):
        try:
            next(task)
        except StopIteration:
            tasks.remove(task)


def gather_z(w, p, own, dst):
    up, down, sib = p.at(z=p.up(1)), p.at(z=p.up(3)), p.at(core=1 - p.core)
    before, after, far = (2 * p.up(n) + p.core for n in (3, 1, 2))
    u0 = w.send(own(0), dst(p.t, 0), up)
    d1 = w.send(own(1), dst(p.t, 1), down)
    u1 = w.send(own(1), dst(p.t, 1), up)
    d0 = w.send(own(0), dst(p.t, 0), down)
    s = [w.send(own(k), dst(p.t, k), sib) for k in (0, 1)]

    def on(t, k):
        s.append(w.send(dst(t, k), dst(t, k), sib))

    yield
    for copy in s[:2]:
        copy.wait_recv()
    yield
    u0.wait_recv()
    f0 = w.send(dst(before, 0), dst(before, 0), up)
    on(before, 0)
    d1.wait_recv()
    f1 = w.send(dst(after, 1), dst(after, 1), down)
    on(after, 1)
    yield
    u1.wait_recv()
    on(before, 1)
    d0.wait_recv()
    on(after, 0)
    yield
    for copy in s[2:6]:
        copy.wait_recv()
    yield
    f0.wait_recv()
    on(far, 0)
    f1.wait_recv()
    on(far, 1)
    yield
    for copy in s[6:]:
        copy.wait_recv()
    w.settle([u0, d1, u1, d0, f0, f1] + s)


def gather_yx(w, p, dst, n):
    east, west = p.at(x=p.east(1)), p.at(x=p.east(3))
    cross, pair = p.at(yl=1 - p.yl, yh=1 - p.yh), p.at(yl=1 - p.yl)
    half = n // 2
    me, flip = p.shard, 1 - 2 * p.yh
    west_s, east_s, far_s = (2 * p.east(k) + p.yh for k in (3, 1, 2))
    mine = p.yl * half
    other = half - mine

    def one(s, at, peer):
        return w.send(dst(s, at, half), dst(s, at, half), peer)

    c0 = one(me, mine, cross)
    yield
    c0.wait_recv()
    a0 = one(me + flip, other, pair)
    yield
    e0 = one(me, 0, east)
    w1 = one(me, half, west)
    e1 = one(me, half, east)
    w0 = one(me, 0, west)
    yield
    e0.wait_recv()
    f0 = one(west_s, 0, east)
    w1.wait_recv()
    f1 = one(east_s, half, west)
    a0.wait_recv()
    g0 = one(me + flip, 0, east)
    h1 = one(me + flip, half, west)
    g1 = one(me + flip, half, east)
    h0 = one(me + flip, 0, west)
    yield
    for copy in (e1, w0, f0, f1):
        copy.wait_recv()
    g0.wait_recv()
    i0 = one(west_s + flip, 0, east)
    h1.wait_recv()
    i1 = one(east_s + flip, half, west)
    yield
    for copy in (g1, h0, i0, i1):
        copy.wait_recv()


def gather_xy(w, p, dst, n, ready=None):
    east, west = p.at(x=p.east(1)), p.at(x=p.east(3))
    cross, pair = p.at(yl=1 - p.yl, yh=1 - p.yh), p.at(yl=1 - p.yl)
    half = n // 2
    me = p.shard
    west_s, east_s, far_s = (2 * p.east(k) + p.yh for k in (3, 1, 2))
    mine = p.yl * half
    other = half - mine
    flip = 1 - 2 * p.yh

    def one(s, at, peer):
        return w.send(dst(s, at, half), dst(s, at, half), peer)

    def along(s):
        return one(s + flip, other, pair)

    e0 = one(me, mine, east)
    w0 = one(me, mine, west)
    c0 = one(me, mine, cross)
    w1 = one(me, other, west)
    yield
    e0.wait_recv()
    fe = one(west_s, mine, east)
    c1 = one(west_s, mine, cross)
    e1 = one(me, other, east)
    w0.wait_recv()
    c2 = one(east_s, mine, cross)
    c0.wait_recv()
    a0 = along(me)
    yield
    fe.wait_recv()
    c3 = one(far_s, mine, cross)
    w1.wait_recv()
    fw = one(east_s, other, west)
    if ready:
        ready(east_s)
    yield
    c1.wait_recv()
    a1 = along(west_s)
    e1.wait_recv()
    if ready:
        ready(west_s)
    c2.wait_recv()
    a2 = along(east_s)
    yield
    fw.wait_recv()
    if ready:
        ready(far_s)
    c3.wait_recv()
    a3 = along(far_s)
    yield
    for s, a in ((me, a0), (west_s, a1), (east_s, a2), (far_s, a3)):
        a.wait_recv()
        if ready:
            ready(s + flip)


def norm_rope(raw, gain, cosine, sine):
    unit = raw * lax.rsqrt(jnp.mean(raw * raw, -1, keepdims=True) + EPS)
    vals = unit * gain
    return vals * cosine + pltpu.roll(vals, 64, 1) * sine


SCALE = 128**-0.5 * LOG2E


def dot_t(a, b):
    return lax.dot_general(a, b, (((1,), (1,)), ((), ())), preferred_element_type=F32)


def t_dot(a, b):
    return lax.dot_general(a, b, (((0,), (0,)), ((), ())), preferred_element_type=F32)


def both(ref, at):
    return jnp.concatenate([ref[at, 0:128], ref[at, 128:256]], 0)


def weights_of(q, k, j, edge):
    s = jnp.exp2(dot_t(q, k) * SCALE)
    last = jnp.where(edge, s[:, j * 128 :], 0.0)
    return last if j == 0 else jnp.concatenate([s[:, : j * 128], last], 1)


def edges(p, j):
    row = lax.broadcasted_iota(jnp.int32, (256, 128), 0) % 128
    col = lax.broadcasted_iota(jnp.int32, (256, 128), 1)
    seen = (p.yl if j < 4 else 1 - p.yl) * 128
    return col <= row, col < seen


def shard_rows(ref, n):
    return lambda s, at, m: ref.at[pl.ds(pl.multiple_of(s * n + at, 16), m)]


def ahead_kernel(
    tok, gain, gq, gk, cot, gain_mid, table, wq, wk, wv, wo, wg, wu, wd,
    h_out, qkv_out, q_out, kv_out, kv_far_out, raw_out, o_out, g_out, out_out, gate_out, up_out,
    y1_out, down_out, h2, q, kv, kv_far, raw, o, y1, h, w_qkv, g, w_out, w_gate, w_up, o_tok,
    cosine, sine, down, down_in, send_sem, recv_sem, here_sem
):
    p = Place()
    w = Wire(send_sem, recv_sem, here_sem)
    own = pl.ds(pl.multiple_of(p.shard * 256, 256), 256)

    def cut(n):
        return pl.ds(pl.multiple_of(p.t * n, n), n)

    load_qkv = [
        w.here(wq.at[:, cut(256)], w_qkv.at[own, pl.ds(0, 256)]),
        w.here(wk.at[:, cut(128)], w_qkv.at[own, pl.ds(256, 128)]),
        w.here(wv.at[:, cut(128)], w_qkv.at[own, pl.ds(384, 128)]),
    ]
    load_out = w.here(wo.at[pl.ds(pl.multiple_of(p.core * 128, 128), 128)], w_out.at[p.shard, p.core])
    load_gate = w.here(wg.at[:, cut(768)], w_gate.at[own])
    load_up = w.here(wu.at[:, cut(768)], w_up.at[own])
    goal, source, stay, at_down = p.turned()
    load_down = w.here(wd.at[pl.ds(pl.multiple_of(at_down * 96, 96), 96)], down)
    load_table = [w.here(table.at[p.yl, 0], cosine), w.here(table.at[p.yl, 1], sine)]
    for k in (0, 1):
        x = tok[k].astype(F32)
        unit = x * lax.rsqrt(jnp.mean(x * x, -1, keepdims=True) + EPS)
        h[p.t if k == 0 else 15 - p.t] = (unit * gain[...]).astype(BF)
    meet(p.peers(("tp", "x", "cross", "pair")), source, stay)
    pair, sib = p.at(yl=1 - p.yl), p.at(core=1 - p.core)

    def block_of(ref):
        return lambda t, k: ref.at[t if k == 0 else 15 - t]

    def part_out(s, at, n):
        return w_out.at[s, p.core, pl.ds(pl.multiple_of(at, 64), n)]

    twin = []

    def ready(s):
        twin.append(w.send(w_out.at[s, p.core], w_out.at[s, p.core], sib))

    at_h, at_g = block_of(h), block_of(g)
    task_h = [gather_z(w, p, lambda k: at_h(p.t, k), at_h)]
    task_qkv = [gather_xy(w, p, shard_rows(w_qkv, 256), 256)]
    for copy in load_qkv:
        copy.wait()
    advance(task_qkv)
    advance(task_h)
    g[p.t] = cot[0]
    g[15 - p.t] = cot[1]
    task_up = [gather_xy(w, p, shard_rows(w_up, 256), 256)]
    task_out = [gather_xy(w, p, part_out, 128, ready)]
    task_gate = [gather_yx(w, p, shard_rows(w_gate, 256), 256)]
    task_g = [gather_z(w, p, lambda k: at_g(p.t, k), at_g)]
    load_gate.wait()
    advance(task_gate)
    load_out.wait()
    ready(p.shard)
    load_down.wait()
    n = w.n
    w.n += 1
    turn = pltpu.make_async_remote_copy(
        src_ref=down,
        dst_ref=down_in,
        send_sem=send_sem.at[n],
        recv_sem=recv_sem.at[n],
        device_id=goal,
        device_id_type=MESH,
    )
    advance(task_h)
    advance(task_qkv)
    advance(task_gate)
    advance(task_h)
    advance(task_qkv)
    advance(task_out)
    advance(task_qkv)
    advance(task_h)
    advance(task_qkv)
    advance(task_h)
    advance(task_h)
    advance(task_qkv)
    advance(task_out)
    load_up.wait()
    advance(task_gate)
    advance(task_g)
    run(*task_h)
    kept = [w.here(h, h_out), w.here(w_qkv, qkv_out)]
    for copy in load_table:
        copy.wait()
    swaps = []
    for j in range(4):
        at = pl.ds(j * 256, 256)
        out = jnp.dot(
            h[4 * j : 4 * j + 4].reshape(256, 2048), w_qkv[...], preferred_element_type=F32
        )
        cos, sin = cosine[at], sine[at]
        kv[at, 0:128] = norm_rope(out[:, 256:384], gk[...], cos, sin).astype(BF)
        kv[at, 128:256] = out[:, 384:].astype(BF)
        swaps.append(w.send(kv.at[at], kv_far.at[at], pair))
        for n in (0, 1):
            cols = slice(n * 128, n * 128 + 128)
            q[at, cols] = norm_rope(out[:, cols], gq[...], cos, sin).astype(BF)
        raw[at] = out[:, :384]
        if j == 1:
            advance(task_out)
            advance(task_g)
        if j == 2:
            advance(task_up)
        if j == 3:
            advance(task_out)
    for j in range(8):
        at = pl.ds(j * 128, 128)
        keys = pl.ds(0, j * 128 + 128)
        if j % 2 == 0:
            swaps[j // 2].wait_recv()
        tri, seen = edges(p, j)
        qj = both(q, at)
        near = weights_of(qj, kv[keys, 0:128], j, tri)
        far = weights_of(qj, kv_far[keys, 0:128], j, seen)
        total = jnp.sum(near, -1, keepdims=True) + jnp.sum(far, -1, keepdims=True)
        out = jnp.dot(near.astype(BF), kv[keys, 128:256], preferred_element_type=F32)
        out += jnp.dot(far.astype(BF), kv_far[keys, 128:256], preferred_element_type=F32)
        out = (out / total).astype(BF)
        for n in (0, 1):
            o[2 * j : 2 * j + 2, :, n * 128 : n * 128 + 128] = out[
                n * 128 : n * 128 + 128
            ].reshape(2, 64, 128)
        if j in (1, 2):
            advance(task_g)
        if j == 3:
            advance(task_out)
        if j == 4:
            advance(task_gate)
            advance(task_g)
        if j == 6:
            advance(task_g)
        if j == 7:
            advance(task_up)
    spread = []
    for dz in (2, 1, 3, 0):
        for dc in range(2):
            z, core = p.up(dz), lax.rem(p.core + dc, 2)
            t = 2 * z + core
            for k in (0, 1):
                src = o.at[t if k == 0 else 15 - t]
                if dz or dc:
                    spread.append(w.send(src, o_tok.at[p.t, k], p.at(z=z, core=core)))
                else:
                    o_tok[p.t, k] = o[t if k == 0 else 15 - t]
    @pl.when(jnp.logical_not(stay))
    def _():
        turn.start()

    @pl.when(stay)
    def _():
        down_in[...] = down[...]

    kept += [
        w.here(q, q_out),
        w.here(kv, kv_out),
        w.here(kv_far, kv_far_out),
        w.here(raw, raw_out),
        w.here(o, o_out),
    ]
    advance(task_gate)
    run(*task_g)
    kept.append(w.here(g, g_out))
    advance(task_up)
    run(*task_out)
    advance(task_up)
    for copy in twin:
        copy.wait_recv()
    kept.append(w.here(w_out, out_out))
    for copy in spread:
        copy.wait_recv()
    for n in range(4):
        cols = slice(n * 512, n * 512 + 512)
        for k in (0, 1):
            y1[k, :, cols] = tok[k, :, cols].astype(F32)
        for t in range(8):
            part = jnp.dot(
                o_tok[t].reshape(128, 256),
                w_out[t, :, :, cols].reshape(256, 512),
                preferred_element_type=F32,
            )
            for k in (0, 1):
                y1[k, :, cols] += part[k * 64 : k * 64 + 64]
    for k in (0, 1):
        y = y1[k]
        unit = y * lax.rsqrt(jnp.mean(y * y, -1, keepdims=True) + EPS)
        h2[k] = (unit * gain_mid[...]).astype(BF)
    kept.append(w.here(y1, y1_out))
    run(*task_gate)
    kept.append(w.here(w_gate, gate_out))
    run(*task_up)
    kept.append(w.here(w_up, up_out))

    @pl.when(jnp.logical_not(stay))
    def _():
        turn.wait()

    kept.append(w.here(down_in, down_out))
    w.finish()
    for copy in kept:
        copy.wait()


def ahead(*args):
    sds = jax.ShapeDtypeStruct
    return pl.pallas_call(
        ahead_kernel,
        out_shape=(
            sds((16, 64, 2048), BF),
            sds((2048, 512), BF),
            sds((1024, 256), BF),
            sds((1024, 256), BF),
            sds((1024, 256), BF),
            sds((1024, 384), F32),
            sds((16, 64, 256), BF),
            sds((16, 64, 2048), BF),
            sds((8, 2, 128, 2048), BF),
            sds((2048, 768), BF),
            sds((2048, 768), BF),
            sds((2, 64, 2048), F32),
            sds((96, 2048), BF),
            sds((2, 64, 2048), BF),
        ),
        in_specs=[VMEM] * 6 + [HBM] * 8,
        out_specs=[HBM] * 13 + [VMEM],
        scratch_shapes=[
            pltpu.VMEM((1024, 256), BF),
            pltpu.VMEM((1024, 256), BF),
            pltpu.VMEM((1024, 256), BF),
            pltpu.VMEM((1024, 384), F32),
            pltpu.VMEM((16, 64, 256), BF),
            pltpu.VMEM((2, 64, 2048), F32),
            pltpu.VMEM((16, 64, 2048), BF),
            pltpu.VMEM((2048, 512), BF),
            pltpu.VMEM((16, 64, 2048), BF),
            pltpu.VMEM((8, 2, 128, 2048), BF),
            pltpu.VMEM((2048, 768), BF),
            pltpu.VMEM((2048, 768), BF),
            pltpu.VMEM((8, 2, 64, 256), BF),
            pltpu.VMEM((1024, 128), F32),
            pltpu.VMEM((1024, 128), F32),
            pltpu.VMEM((96, 2048), BF),
            pltpu.VMEM((96, 2048), BF),
        ]
        + sems(160, 32),
        compiler_params=pltpu.CompilerParams(
            collective_id=0, has_side_effects=True, vmem_limit_bytes=56 * MB
        ),
        name="ahead",
    )(*args)


def rows_of(ref, zz):
    c = ref.shape[-1]
    return jnp.concatenate(
        [ref[pl.ds(2 * zz, 2)].reshape(128, c), ref[pl.ds(14 - 2 * zz, 2)].reshape(128, c)], 0
    )


def put(ref, zz, val):
    c = ref.shape[-1]
    ref[pl.ds(2 * zz, 2)] = val[:128].reshape(2, 64, c)
    ref[pl.ds(14 - 2 * zz, 2)] = val[128:].reshape(2, 64, c)


def add(*vals):
    total = vals[0].astype(F32)
    for val in vals[1:]:
        total = total + val.astype(F32)
    return total


def z_room():
    return [
        pltpu.VMEM((4, 2, 64, 2048), BF),
        pltpu.VMEM((2, 64, 2048), BF),
        pltpu.VMEM((2, 2, 64, 2048), BF),
    ]


def reduce_z(w, p, part, room, out):
    mine, relay, last = room
    near = mine
    up, down, sib = p.at(z=p.up(1)), p.at(z=p.up(3)), p.at(core=1 - p.core)

    def block(n, core, k):
        t = 2 * p.up(n) + core
        return t if k == 0 else 15 - t

    first = {}

    def give(n):
        for k in (0, 1):
            first[n, k] = w.send(part.at[block(n, 1 - p.core, k)], near.at[n, k], sib)

    def fold(n, k):
        first[n, k].wait_recv()
        mine[n, k] = add(part[block(n, p.core, k)], near[n, k]).astype(BF)

    give(2)
    yield
    give(1)
    fold(2, 0)
    e0 = w.send(mine.at[2, 0], relay.at[0], up)
    fold(2, 1)
    e1 = w.send(mine.at[2, 1], relay.at[1], down)
    yield
    give(3)
    fold(1, 1)
    a1 = w.send(mine.at[1, 1], last.at[0, 1], up)
    fold(1, 0)
    yield
    give(0)
    fold(3, 0)
    b0 = w.send(mine.at[3, 0], last.at[1, 0], down)
    fold(3, 1)
    yield
    e0.wait_recv()
    mine[1, 0] = add(mine[1, 0], relay[0]).astype(BF)
    a0 = w.send(mine.at[1, 0], last.at[0, 0], up)
    e1.wait_recv()
    mine[3, 1] = add(mine[3, 1], relay[1]).astype(BF)
    b1 = w.send(mine.at[3, 1], last.at[1, 1], down)
    fold(0, 0)
    fold(0, 1)
    w.settle(list(first.values()))
    yield
    for k, (a, b) in enumerate(((a0, b0), (a1, b1))):
        a.wait_recv()
        b.wait_recv()
        out[k] = add(mine[0, k], last[0, k], last[1, k])


def xy_room(rows, cols, left=None):
    left = left or cols // 2
    return [
        pltpu.VMEM(lead + (rows, n), BF)
        for n in (left, cols - left)
        for lead in ((4,), (2, 4), (4,), (3,))
    ]


def put_half(out, cols, val):
    if len(out.shape) == 3:
        out[:, :, cols] = val.reshape(out.shape[0], out.shape[1], val.shape[1])
    else:
        out[:, cols] = val


def reduce_xy(w, p, part, room, out):
    ra, ta, sa, fa, rb, tb, sb, fb = room
    n_left = sa.shape[2]
    left, right = pl.ds(0, n_left), pl.ds(n_left, part.shape[3] - n_left)
    low, high = pl.ds(0, 2), pl.ds(2, 2)
    spans = (1, 2, 3)
    easts = [p.at(x=p.east(d)) for d in spans]
    norths = [p.north(d) for d in spans]
    xs = [p.east(d) for d in spans]
    ys = [lax.rem(p.y + d, 4) for d in spans]

    def start(bundle, r, t, peers):
        return [
            w.send(bundle(1, low), r.at[low], peers[0]),
            w.send(bundle(1, high), r.at[high], peers[2]),
            w.send(bundle(0, high), t.at[0, high], peers[0]),
            w.send(bundle(2, low), t.at[1, low], peers[2]),
        ]

    def of_x(d, some):
        return part.at[xs[d], some, :, left]

    def of_y(d, some):
        return part.at[some, ys[d], :, right]

    ca = start(of_x, ra, ta, easts)
    yield
    cb = start(of_y, rb, tb, norths)
    yield
    ca[0].wait_recv()
    for k in (0, 1):
        ra[k] = add(ra[k], part[xs[0], k, :, left]).astype(BF)
    ca.append(w.send(ra.at[low], ta.at[0, low], easts[0]))
    ca[1].wait_recv()
    for k in (2, 3):
        ra[k] = add(ra[k], part[xs[2], k, :, left]).astype(BF)
    ca.append(w.send(ra.at[high], ta.at[1, high], easts[2]))
    yield
    cb[0].wait_recv()
    for k in (0, 1):
        rb[k] = add(rb[k], part[k, ys[0], :, right]).astype(BF)
    cb.append(w.send(rb.at[low], tb.at[0, low], norths[0]))
    cb[1].wait_recv()
    for k in (2, 3):
        rb[k] = add(rb[k], part[k, ys[2], :, right]).astype(BF)
    cb.append(w.send(rb.at[high], tb.at[1, high], norths[2]))
    yield
    for copy in ca[2:]:
        copy.wait_recv()

    @pl.loop(0, 4)
    def _(y):
        sa[y] = add(part[p.x, y, :, left], ta[0, y], ta[1, y]).astype(BF)

    da = [w.send(sa.at[lax.rem(p.y + d, 4)], fa.at[d - 1], norths[d - 1]) for d in spans]
    yield
    for copy in cb[2:]:
        copy.wait_recv()

    @pl.loop(0, 4)
    def _(x):
        sb[x] = add(part[x, p.y, :, right], tb[0, x], tb[1, x]).astype(BF)

    db = [w.send(sb.at[p.east(d)], fb.at[d - 1], easts[d - 1]) for d in spans]
    yield
    for copy in da:
        copy.wait_recv()
    put_half(out, left, add(sa[p.y], fa[0], fa[1], fa[2]).astype(BF))
    yield
    for copy in db:
        copy.wait_recv()
    put_half(out, right, add(sb[p.x], fb[0], fb[1], fb[2]).astype(BF))


def mlp_kernel(
    h2_own, down_own, gate_hbm, up_hbm, g_hbm, out_hbm, y1, cot, gain,
    h2_out, dgate_out, dup_out, mixed_out, grad_mid, dz, d_tok, term, down_mine,
    h2, w_gate, w_up, w_down, g, gate, upper, part, down_part, act, dgate, dup, mixed, *rest
):
    zr, xr, (send_sem, recv_sem, here_sem) = rest[:3], rest[3:11], rest[11:]
    p = Place()
    w = Wire(send_sem, recv_sem, here_sem)
    loads = [w.here(gate_hbm, w_gate), w.here(up_hbm, w_up), w.here(g_hbm, g)]
    h2[p.t] = h2_own[0]
    h2[15 - p.t] = h2_own[1]
    w_down[pl.ds(pl.multiple_of(p.shard * 96, 96), 96)] = down_own[...]
    meet(p.peers(("z", "sib", "x", "plane", "cross")))

    def block(t, k):
        return h2.at[t if k == 0 else 15 - t]

    task_h = [gather_z(w, p, lambda k: block(p.t, k), block)]
    task_down = [gather_xy(w, p, shard_rows(w_down, 96), 96)]
    def forward(zz):
        left = rows_of(h2, zz)
        gate_n = jnp.dot(left, w_gate[...], preferred_element_type=F32)
        up_n = jnp.dot(left, w_up[...], preferred_element_type=F32)
        gate[zz] = gate_n
        upper[zz] = up_n
        put(act, zz, (gate_n * jax.nn.sigmoid(gate_n) * up_n).astype(BF))

    advance(task_h)
    advance(task_down)
    advance(task_h)
    for copy in loads:
        copy.wait()
    forward(p.z)
    advance(task_down)
    advance(task_h)
    advance(task_down)
    advance(task_h)
    advance(task_h)
    advance(task_down)
    forward(p.up(3))
    advance(task_h)
    forward(p.up(1))
    advance(task_down)
    run(*task_h)
    kept = [w.here(h2, h2_out)]
    forward(p.up(2))
    kept[0].wait()
    load = w.here(out_hbm.at[pl.ds(0, 16)], h2)

    @pl.loop(0, 6)
    def _(i):
        cols = pl.ds(pl.multiple_of(i * 128, 128), 128)
        left = act[:, :, cols].reshape(1024, 128)
        out = t_dot(left, g[...].reshape(1024, 2048)).astype(BF)
        for k in range(8):
            row = i * 8 + k
            piece = row // 3
            f = lax.rem(piece, 8)
            down_part[f // 2, 2 * lax.rem(f, 2) + piece // 8, pl.ds(pl.multiple_of(lax.rem(row, 3) * 16, 16), 16)] = out[
                k * 16 : k * 16 + 16
            ]

    run(*task_down)
    task_sum = [reduce_z(w, p, part, zr, grad_mid)]
    task_late = [reduce_xy(w, p, down_part, xr, down_mine)]
    advance(task_late)
    advance(task_late)
    for n in (2, 1, 3, 0):
        zz = p.up(n)
        gate_n, up_n = gate[zz], upper[zz]
        sig = jax.nn.sigmoid(gate_n)
        da = dot_t(rows_of(g, zz), w_down[...])
        silu = gate_n * sig
        d_gate = (da * up_n * sig * (1.0 + gate_n * (1.0 - sig))).astype(BF)
        d_up = (da * silu).astype(BF)
        put(dgate, zz, d_gate)
        put(dup, zz, d_up)
        total = dot_t(d_gate, w_gate[...]) + dot_t(d_up, w_up[...])
        put(part, zz, total.astype(BF))
        advance(task_sum)
        if n == 3:
            advance(task_late)
            advance(task_late)
    load2 = w.here(out_hbm.at[pl.ds(16, 16)], g)
    kept += [w.here(dgate, dgate_out), w.here(dup, dup_out)]
    advance(task_sum)

    @pl.loop(0, 4)
    def _(n):
        out = jnp.dot(rows_of(act, n), w_down[...], preferred_element_type=F32)
        put(mixed, n, out.astype(BF))

    kept.append(w.here(mixed, mixed_out))
    advance(task_late)
    advance(task_late)
    run(*task_sum)
    load.wait()
    load2.wait()
    term[...] = jnp.zeros_like(term)
    for k in (0, 1):
        y = y1[k]
        scale = lax.rsqrt(jnp.mean(y * y, -1, keepdims=True) + EPS)
        unit = y * scale
        dh = grad_mid[k]
        term[...] += jnp.sum(dh * unit, 0, keepdims=True)
        wv = dh * gain[...]
        dy = cot[k].astype(F32) + scale * (wv - unit * jnp.mean(wv * unit, -1, keepdims=True))
        grad_mid[k] = dy
        dz[k] = dy.astype(BF)
    dz_rows = dz[...].reshape(128, 2048)
    for t in range(8):
        half = h2 if t < 4 else g
        out = dot_t(dz_rows, half[4 * (t % 4) : 4 * (t % 4) + 4].reshape(256, 2048)).astype(BF)
        d_tok[t] = out.reshape(2, 64, 256)
    run(*task_late)
    w.finish()
    for copy in kept[1:]:
        copy.wait()


def mlp(*args):
    sds = jax.ShapeDtypeStruct
    return pl.pallas_call(
        mlp_kernel,
        out_shape=(
            sds((16, 64, 2048), BF),
            sds((16, 64, 768), BF),
            sds((16, 64, 768), BF),
            sds((16, 64, 2048), BF),
            sds((2, 64, 2048), F32),
            sds((2, 64, 2048), BF),
            sds((8, 2, 64, 256), BF),
            sds((1, 2048), F32),
            sds((48, 2048), BF),
        ),
        in_specs=[VMEM] * 2 + [HBM] * 4 + [VMEM] * 3,
        out_specs=[HBM] * 4 + [VMEM] * 5,
        scratch_shapes=[
            pltpu.VMEM((16, 64, 2048), BF),
            pltpu.VMEM((2048, 768), BF),
            pltpu.VMEM((2048, 768), BF),
            pltpu.VMEM((768, 2048), BF),
            pltpu.VMEM((16, 64, 2048), BF),
            pltpu.VMEM((4, 256, 768), F32),
            pltpu.VMEM((4, 256, 768), F32),
            pltpu.VMEM((16, 64, 2048), BF),
            pltpu.VMEM((4, 4, 48, 2048), BF),
            pltpu.VMEM((16, 64, 768), BF),
            pltpu.VMEM((16, 64, 768), BF),
            pltpu.VMEM((16, 64, 768), BF),
            pltpu.VMEM((16, 64, 2048), BF),
        ]
        + z_room()
        + xy_room(48, 2048)
        + sems(96, 12),
        compiler_params=pltpu.CompilerParams(
            collective_id=2, has_side_effects=True, vmem_limit_bytes=63 * MB
        ),
        name="mlp",
    )(*args)


def sum_all(w, p, vec, slots, out):
    ra, rb, rc = slots
    ra[p.t] = vec[...]
    first = [w.send(ra.at[p.t], ra.at[p.t], peer) for peer in p.peers(("tp",))]
    yield
    for copy in first:
        copy.wait_recv()
    rb[p.x] = sum((ra[i] for i in range(1, 8)), ra[0])
    xs = [w.send(rb.at[p.x], rb.at[p.x], p.at(x=p.east(d))) for d in (1, 2, 3)]
    yield
    for copy in xs:
        copy.wait_recv()
    rc[p.y] = sum((rb[i] for i in range(1, 4)), rb[0])
    ys = [w.send(rc.at[p.y], rc.at[p.y], p.north(d)) for d in (1, 2, 3)]
    yield
    for copy in ys:
        copy.wait_recv()
    out[...] = sum((rc[i] for i in range(1, 4)), rc[0])


def deal(w, p, src, dst):
    dst[p.t] = src[p.t]
    copies = []
    for dz in (2, 1, 3, 0):
        for dc in range(2):
            if dz or dc:
                z, core = p.up(dz), lax.rem(p.core + dc, 2)
                copies.append(w.send(src.at[2 * z + core], dst.at[p.t], p.at(z=z, core=core)))
    return copies


def to_pieces(part, i, out, cols):
    z, yl = i // 2, lax.rem(i, 2)
    for r in range(16):
        core, f = r // 8, r % 8
        at = pl.ds(pl.multiple_of((2 * z + core) * 16, 16), 16)
        part[f // 2, 2 * (f % 2) + yl, at, cols] = out[r * 16 : r * 16 + 16]


def turn_norm_back(grad, raw, gain, cosine, sine):
    scale = lax.rsqrt(jnp.mean(raw * raw, -1, keepdims=True) + EPS)
    unit = raw * scale
    back = grad * cosine + pltpu.roll(grad * sine, 64, 1)
    term = jnp.sum(back * unit, 0, keepdims=True)
    back = back * gain
    return scale * (back - unit * jnp.mean(back * unit, -1, keepdims=True)), term


def behind_kernel(
    q, kv, kv_far, gq, gk, d_tok, dz_own, o, tok, gain, term_mid, down_mine, table,
    raw_hbm, qkv_hbm, mid_hbm, y1_hbm, h2_hbm, dgate_hbm, dup_hbm, mixed_hbm, h_hbm,
    mixed, tokens_grad, g_gate, g_up, g_q, g_k, g_v, g_down, g_out, s_in, s_mid, s_q, s_k,
    mix_sum, mix_buf, dx_buf, cols_gu, cols_qkv, rows_out, vec_out, do, acc, acc_far, out_far, in_far, dz, big_x, big_y, dqkv, gu_part, qkv_part, out_part,
    gu_mine, qkv_mine, rows, vec, ra, rb, rc, dh, raw, w_qkv, grad_mid, y1, cosine, sine, *rest
):
    mix_room, dh_room = rest[:3], rest[3:6]
    gu_room, qkv_room, out_room = rest[6:14], rest[14:22], rest[22:30]
    send_sem, recv_sem, here_sem = rest[30:]
    p = Place()
    w = Wire(send_sem, recv_sem, here_sem)
    loads = [
        w.here(h2_hbm, big_y),
        w.here(dgate_hbm, big_x.at[:, :, pl.ds(0, 768)]),
        w.here(dup_hbm, big_x.at[:, :, pl.ds(768, 768)]),
        w.here(raw_hbm, raw),
        w.here(qkv_hbm, w_qkv),
        w.here(mid_hbm, grad_mid),
        w.here(y1_hbm, y1),
        w.here(table.at[p.yl, 0], cosine),
        w.here(table.at[p.yl, 1], sine),
    ]
    dz[p.t] = dz_own[0]
    dz[15 - p.t] = dz_own[1]
    vec[...] = jnp.zeros_like(vec)
    vec[2:3] = term_mid[...]
    rows[0:48] = down_mine[...]
    meet(p.peers(("tp", "plane", "swap")))
    pair = p.at(yl=1 - p.yl)
    spread = []
    for far in (2, 1, 3, 0):
        for dc in (0, 1):
            z, core = p.up(far), lax.rem(p.core + dc, 2)
            for k in (0, 1):
                if far or dc:
                    dst = do.at[p.t if k == 0 else 15 - p.t]
                    spread.append(w.send(d_tok.at[2 * z + core, k], dst, p.at(z=z, core=core)))
                else:
                    do[p.t if k == 0 else 15 - p.t] = d_tok[p.t, k]

    def block(t, k):
        return dz.at[t if k == 0 else 15 - t]

    task_dz = [gather_z(w, p, lambda k: block(p.t, k), block)]
    advance(task_dz)
    for copy in loads[:3]:
        copy.wait()

    def grad_gu(i):
        cols = pl.ds(pl.multiple_of(i * 256, 256), 256)
        left = big_y[:, :, cols].reshape(1024, 256)
        for n in (0, 1):
            at = slice(n * 768, n * 768 + 768)
            to_pieces(gu_part, i, t_dot(left, big_x[:, :, at].reshape(1024, 768)).astype(BF), at)

    pl.loop(0, 8)(grad_gu)
    task_gu = [reduce_xy(w, p, gu_part, gu_room, gu_mine)]
    advance(task_gu)
    load = w.here(mixed_hbm, big_y)
    acc[...] = jnp.zeros_like(acc)
    acc_far[...] = jnp.zeros_like(acc_far)
    for copy in loads[3:]:
        copy.wait()
    for copy in spread:
        copy.wait_recv()
    back = []
    for j in range(7, -1, -1):
        at = pl.ds(j * 128, 128)
        keys = pl.ds(0, j * 128 + 128)
        tri, seen = edges(p, j)
        qj = both(q, at)
        dj = jnp.concatenate(
            [do[2 * j : 2 * j + 2, :, n * 128 : n * 128 + 128].reshape(128, 128) for n in (0, 1)], 0
        )
        near = weights_of(qj, kv[keys, 0:128], j, tri)
        far = weights_of(qj, kv_far[keys, 0:128], j, seen)
        scale = 1.0 / (jnp.sum(near, -1, keepdims=True) + jnp.sum(far, -1, keepdims=True))
        near = near * scale
        far = far * scale
        d_near = dot_t(dj, kv[keys, 128:256])
        d_far = dot_t(dj, kv_far[keys, 128:256])
        delta = jnp.sum(near * d_near, -1, keepdims=True) + jnp.sum(
            far * d_far, -1, keepdims=True
        )
        s_near = (near * (d_near - delta)).astype(BF)
        s_far = (far * (d_far - delta)).astype(BF)
        acc_far[keys, 0:128] += t_dot(s_far, qj)
        acc_far[keys, 128:256] += t_dot(far.astype(BF), dj)
        out_far[at, 0:128] = (acc_far[at, 0:128] * 128**-0.5).astype(BF)
        out_far[at, 128:256] = acc_far[at, 128:256].astype(BF)
        back.append((j, w.send(out_far.at[at], in_far.at[at], pair)))
        acc[keys, 0:128] += t_dot(s_near, qj)
        acc[keys, 128:256] += t_dot(near.astype(BF), dj)
        grad = jnp.dot(s_near, kv[keys, 0:128], preferred_element_type=F32)
        grad += jnp.dot(s_far, kv_far[keys, 0:128], preferred_element_type=F32)
        grad = (grad * 128**-0.5).astype(BF).astype(F32)
        for n in (0, 1):
            cols = slice(n * 128, n * 128 + 128)
            val, term = turn_norm_back(grad[cols], raw[at, cols], gq[...], cosine[at], sine[at])
            dqkv[2 * j : 2 * j + 2, :, cols] = val.astype(BF).reshape(2, 64, 128)
            vec[4:5, 0:128] += term
        if j in (7, 5, 3, 1, 0):
            advance(task_dz)
    advance(task_gu)
    advance(task_gu)
    run(*task_dz)
    for i in range(2):
        out = t_dot(
            o[:, :, i * 128 : i * 128 + 128].reshape(1024, 128), dz[...].reshape(1024, 2048)
        ).astype(BF)
        for f in range(8):
            out_part[f // 2, 2 * (f % 2) + i] = out[f * 16 : f * 16 + 16]
    load.wait()
    load = w.here(h_hbm, dz)
    task_out = [reduce_xy(w, p, out_part, out_room, rows.at[pl.ds(48, 16)])]
    advance(task_out)
    advance(task_out)
    for j, copy in back:
        at = pl.ds(j * 128, 128)
        copy.wait_recv()
        grad = add(acc[at, 0:128] * 128**-0.5, in_far[at, 0:128]).astype(BF).astype(F32)
        val, term = turn_norm_back(grad, raw[at, 256:384], gk[...], cosine[at], sine[at])
        dqkv[2 * j : 2 * j + 2, :, 256:384] = val.astype(BF).reshape(2, 64, 128)
        vec[5:6, 0:128] += term
        dv = add(acc[at, 128:256], in_far[at, 128:256]).astype(BF)
        dqkv[2 * j : 2 * j + 2, :, 384:512] = dv.reshape(2, 64, 128)
    task_dh = [reduce_z(w, p, big_x, dh_room, dh)]
    for n in (2, 1, 3, 0):
        zz = p.up(n)
        put(big_x, zz, dot_t(rows_of(dqkv, zz), w_qkv[...]).astype(BF))
        advance(task_dh)
    load.wait()

    def grad_qkv(i):
        cols = pl.ds(pl.multiple_of(i * 256, 256), 256)
        out = t_dot(dz[:, :, cols].reshape(1024, 256), dqkv[...].reshape(1024, 512))
        to_pieces(qkv_part, i, out.astype(BF), slice(0, 512))

    pl.loop(0, 8)(grad_qkv)
    task_qkv = [reduce_xy(w, p, qkv_part, qkv_room, qkv_mine)]
    advance(task_qkv)
    advance(task_qkv)
    advance(task_gu)
    advance(task_dh)
    task_mix = [reduce_z(w, p, big_y, mix_room, mix_sum)]
    advance(task_mix)
    advance(task_mix)
    advance(task_out)
    advance(task_out)
    advance(task_gu)
    run(*task_dh)
    total = jnp.zeros((1, 2048), F32)
    for k in (0, 1):
        x = tok[k].astype(F32)
        scale = lax.rsqrt(jnp.mean(x * x, -1, keepdims=True) + EPS)
        unit = x * scale
        total += jnp.sum(dh[k] * unit, 0, keepdims=True)
        wv = dh[k] * gain[...]
        dx = grad_mid[k] + scale * (wv - unit * jnp.mean(wv * unit, -1, keepdims=True))
        dx_buf[k] = dx.astype(BF)
    vec[0:1] = total
    task_vec = [sum_all(w, p, vec, (ra, rb, rc), vec_out)]
    advance(task_vec)
    advance(task_mix)
    advance(task_mix)
    advance(task_qkv)
    advance(task_qkv)
    advance(task_gu)
    advance(task_mix)
    advance(task_out)
    advance(task_out)
    advance(task_vec)
    run(*task_gu)
    dealt = deal(w, p, gu_mine, cols_gu)
    advance(task_qkv)
    advance(task_qkv)
    advance(task_vec)
    run(*task_mix)
    for k in (0, 1):
        mix_buf[k] = (y1[k] + mix_sum[k]).astype(BF)
    run(*task_out)
    stay = p.yl == p.core
    n = w.n
    w.n += 1
    swap = pltpu.make_async_remote_copy(
        src_ref=rows,
        dst_ref=rows_out,
        send_sem=send_sem.at[n],
        recv_sem=recv_sem.at[n],
        device_id=p.at(yl=1 - p.yl, core=1 - p.core),
        device_id_type=MESH,
    )

    @pl.when(jnp.logical_not(stay))
    def _():
        swap.start()

    @pl.when(stay)
    def _():
        rows_out[...] = rows[...]

    run(*task_qkv)
    dealt += deal(w, p, qkv_mine, cols_qkv)
    run(*task_vec)
    kept = [
        w.here(mix_buf, mixed),
        w.here(dx_buf, tokens_grad),
        w.here(vec_out.at[pl.ds(0, 1)], s_in),
        w.here(vec_out.at[pl.ds(2, 1)], s_mid),
        w.here(vec_out.at[pl.ds(4, 1), pl.ds(0, 128)], s_q),
        w.here(vec_out.at[pl.ds(5, 1), pl.ds(0, 128)], s_k),
    ]

    def place(first, at, val):
        end = at + val.shape[1]
        while at < end:
            stop = min(end, (at // 2048 + 1) * 2048)
            slot, begin = first + at // 2048, end - val.shape[1]
            grad_mid[slot // 4, slot % 4 * 16 : slot % 4 * 16 + 16, at % 2048 : (stop - 1) % 2048 + 1] = val[
                :, at - begin : stop - begin
            ].astype(F32)
            at = stop

    def piece(slot):
        return grad_mid.at[slot // 4, pl.ds(slot % 4 * 16, 16)]

    for copy in dealt[:7]:
        copy.wait_recv()
    for t in range(8):
        place(0, t * 768, cols_gu[t, :, 0:768])
        place(3, t * 768, cols_gu[t, :, 768:1536])
    for i in range(3):
        kept.append(w.here(piece(i), g_gate.at[:, pl.ds(i * 2048, 2048)]))
        kept.append(w.here(piece(3 + i), g_up.at[:, pl.ds(i * 2048, 2048)]))

    @pl.when(jnp.logical_not(stay))
    def _():
        swap.wait()

    y1[0] = rows_out[...].astype(F32)
    kept.append(w.here(y1.at[0, pl.ds(0, 48)], g_down))
    kept.append(w.here(y1.at[0, pl.ds(48, 16)], g_out))
    for copy in dealt[7:]:
        copy.wait_recv()
    for t in range(8):
        place(6, t * 256, cols_qkv[t, :, 0:256])
        place(7, t * 128, cols_qkv[t, :, 256:384])
        place(7, 1024 + t * 128, cols_qkv[t, :, 384:512])
    kept += [
        w.here(piece(6), g_q),
        w.here(grad_mid.at[1, pl.ds(48, 16), pl.ds(0, 1024)], g_k),
        w.here(grad_mid.at[1, pl.ds(48, 16), pl.ds(1024, 1024)], g_v),
    ]
    for copy in kept:
        copy.wait()
    w.finish()


def behind(*args):
    sds = jax.ShapeDtypeStruct
    return pl.pallas_call(
        behind_kernel,
        out_shape=(
            sds((2, 64, 2048), BF),
            sds((2, 64, 2048), BF),
            sds((16, 6144), F32),
            sds((16, 6144), F32),
            sds((16, 2048), F32),
            sds((16, 1024), F32),
            sds((16, 1024), F32),
            sds((48, 2048), F32),
            sds((16, 2048), F32),
            sds((1, 2048), F32),
            sds((1, 2048), F32),
            sds((1, 128), F32),
            sds((1, 128), F32),
        ),
        in_specs=[VMEM] * 12 + [HBM] * 10,
        out_specs=[HBM] * 13,
        scratch_shapes=[
            pltpu.VMEM((2, 64, 2048), F32),
            pltpu.VMEM((2, 64, 2048), BF),
            pltpu.VMEM((2, 64, 2048), BF),
            pltpu.VMEM((8, 16, 1536), BF),
            pltpu.VMEM((8, 16, 512), BF),
            pltpu.VMEM((64, 2048), BF),
            pltpu.VMEM((8, 2048), F32),
            pltpu.VMEM((16, 64, 256), BF),
            pltpu.VMEM((1024, 256), F32),
            pltpu.VMEM((1024, 256), F32),
            pltpu.VMEM((1024, 256), BF),
            pltpu.VMEM((1024, 256), BF),
            pltpu.VMEM((16, 64, 2048), BF),
            pltpu.VMEM((16, 64, 2048), BF),
            pltpu.VMEM((16, 64, 2048), BF),
            pltpu.VMEM((16, 64, 512), BF),
            pltpu.VMEM((4, 4, 128, 1536), BF),
            pltpu.VMEM((4, 4, 128, 512), BF),
            pltpu.VMEM((4, 4, 16, 2048), BF),
            pltpu.VMEM((8, 16, 1536), BF),
            pltpu.VMEM((8, 16, 512), BF),
            pltpu.VMEM((64, 2048), BF),
            pltpu.VMEM((8, 2048), F32),
            pltpu.VMEM((8, 8, 2048), F32),
            pltpu.VMEM((4, 8, 2048), F32),
            pltpu.VMEM((4, 8, 2048), F32),
            pltpu.VMEM((2, 64, 2048), F32),
            pltpu.VMEM((1024, 384), F32),
            pltpu.VMEM((2048, 512), BF),
            pltpu.VMEM((2, 64, 2048), F32),
            pltpu.VMEM((2, 64, 2048), F32),
            pltpu.VMEM((1024, 128), F32),
            pltpu.VMEM((1024, 128), F32),
        ]
        + z_room()
        + z_room()
        + xy_room(128, 1536, 1024)
        + xy_room(128, 512)
        + xy_room(16, 2048)
        + sems(160, 32),
        compiler_params=pltpu.CompilerParams(
            collective_id=1, has_side_effects=True, vmem_limit_bytes=63 * MB
        ),
        name="behind",
    )(*args)


def pour_kernel(*refs):
    n = (len(refs) - 2) // 3
    taken, given, held, (in_sem, out_sem) = refs[:n], refs[n : 2 * n], refs[2 * n : 3 * n], refs[3 * n :]
    first = [pltpu.make_async_copy(taken[i], held[i], in_sem.at[i]) for i in range(n)]
    second = [pltpu.make_async_copy(held[i], given[i], out_sem.at[i]) for i in range(n)]
    for copy in first:
        copy.start()
    for i in range(n):
        first[i].wait()
        second[i].start()
    for copy in second:
        copy.wait()


def pour(*vals):
    n = len(vals)
    return pl.pallas_call(
        pour_kernel,
        out_shape=tuple(jax.ShapeDtypeStruct(val.shape, val.dtype) for val in vals),
        in_specs=[HBM] * n,
        out_specs=[HBM] * n,
        scratch_shapes=[pltpu.VMEM(val.shape, val.dtype) for val in vals]
        + [pltpu.SemaphoreType.DMA((n,)), pltpu.SemaphoreType.DMA((n,))],
        compiler_params=pltpu.CompilerParams(vmem_limit_bytes=63 * MB),
        name="pour",
    )(*vals)


def rotary(width):
    half = width // 2
    freq = np.float32(THETA) ** (-2.0 * np.arange(half, dtype=np.float32) / np.float32(width))
    row = np.arange(1024)
    tile = row // 128
    tables = []
    for lane in (0, 1):
        place = np.where(tile < 4, 2 * tile + lane, 2 * tile + 1 - lane)
        angle = (place * 128 + row % 128).astype(np.float32)[:, None] * freq.astype(np.float32)
        angle = angle.astype(np.float64)
        cos, sin = np.cos(angle), np.sin(angle)
        tables.append(
            (np.concatenate([cos, cos], 1), np.concatenate([-sin, sin], 1))
        )
    return np.array(tables, dtype=np.float32)


def shards(
    tokens,
    gain_in,
    query_weight,
    key_weight,
    value_weight,
    gain_query,
    gain_key,
    out_weight,
    gain_mid,
    gate_weight,
    up_weight,
    down_weight,
    cotangent,
):
    width = tokens.shape[4]
    table = jnp.asarray(rotary(128))
    tok = tokens.reshape(2, 64, width)
    cot = cotangent.reshape(2, 64, width)
    gain_q, gain_k = gain_query.reshape(1, -1), gain_key.reshape(1, -1)
    h, w_qkv, query_b, kv, kv_far, raw, attended, g, w_out, w_gate, w_up, y_mid, rows_d, h2_own = ahead(
        tok,
        gain_in.reshape(1, -1),
        gain_q,
        gain_k,
        cot,
        gain_mid.reshape(1, -1),
        table,
        query_weight,
        key_weight,
        value_weight,
        out_weight,
        gate_weight,
        up_weight,
        down_weight,
    )
    h2, dgate_b, dup_b, mixed_part, grad_mid, dz_own, d_tok, term_mid, down_mine = mlp(
        h2_own,
        rows_d,
        w_gate,
        w_up,
        g,
        w_out.reshape(32, 64, width),
        y_mid,
        cot,
        gain_mid.reshape(1, -1),
    )
    results = behind(
        query_b,
        kv,
        kv_far,
        gain_q,
        gain_k,
        d_tok,
        dz_own,
        attended,
        tok,
        gain_in.reshape(1, -1),
        term_mid,
        down_mine,
        table,
        raw,
        w_qkv,
        grad_mid,
        y_mid,
        h2,
        dgate_b,
        dup_b,
        mixed_part,
        h,
    )

    mixed, tokens_grad, g_gate, g_up, g_q, g_k, g_v, g_down, g_out, s_in, s_mid, s_q, s_k = pour(*results)
    return (
        mixed.reshape(tokens.shape),
        tokens_grad.reshape(tokens.shape),
        s_in.reshape(-1),
        g_q,
        g_k,
        g_v,
        s_q.reshape(-1),
        s_k.reshape(-1),
        g_out,
        s_mid.reshape(-1),
        g_gate,
        g_up,
        g_down,
    )


def solution(mesh):
    fine = Mesh(mesh.devices.reshape(4, 2, 2, 4, 2), ALL)
    ctx, fsdp = ("z", "yl", "core"), FS
    act = P(fsdp, None, ctx, None, None)
    weight = P(fsdp, None)
    grad = P(ctx + fsdp, None)
    placed = (
        act, P(), weight, weight, weight, P(), P(), weight, P(), weight, weight, weight, act,
    )
    return jax.shard_map(
        shards,
        mesh=fine,
        in_specs=placed,
        out_specs=(act, act, P(), grad, grad, grad, P(), P(), grad, P(), grad, grad, grad),
        check_vma=False,
    )
```
